32 devices in a mesh: ctx: 8 (over y, x, core), exp: 4 (over z).
Axes of the slice: x: 2, y: 2, z: 4, core: 2. Of those that a mesh axis runs over, the one named last changes fastest.
Arguments:
- queries: bfloat16 [1024, 8192], P('ctx', 'exp'), may hold values from -160 to 160, as said below
- keys: bfloat16 [1024, 512], P('ctx'), may hold values from -7 to 7
- values: bfloat16 [1024, 512], P('ctx'), may hold values from -6 to 6
- positions: int32 [1024], P('ctx'), may hold values from 0 to 1023, as said below
- bounds: int32 [1024], P('ctx'), may hold values from 0 to 1023, as said below
- w_out: bfloat16 [8192, 4096], P('exp'), may hold values from -0.0625 to 0.0625
- residual: bfloat16 [1024, 4096], P(('ctx', 'exp')), may hold values from -60 to 60
- norm_gain: float32 [4096], replicated, may hold values from 0.1 to 1.9
- routes: int32 [1024, 8], P(('ctx', 'exp')), may hold values from 0 to 127, as said below
- gates: float32 [1024, 8], P(('ctx', 'exp')), may hold values from 0.1 to 1
- w_in: bfloat16 [4, 384, 4096], P('exp'), may hold values from -0.09375 to 0.09375
- w_back: bfloat16 [4, 192, 4096], P('exp'), may hold values from -1.75 to 1.75
Outputs:
- middle: bfloat16 [1024, 4096], P(('ctx', 'exp'))
- expert_out: bfloat16 [1024, 4096], P(('ctx', 'exp'))
The draws below stay inside these ranges and needn't reach their ends.
Inputs may be any that keep to these rules, and one draw needn't show every extreme that they name: `queries`: rows scaled at most as far as the range. Each of 0 to 1023 appears once; a device's 128 tokens hold consecutive positions in order. bounds[i] is positions[i] or the last position of its frame of 256 positions (frames start at multiples of 256). `routes`: each row names 8 different experts, exactly one of them below 1; among the rows of one device, each expert below 1 is chosen by at most 32 rows and some one by exactly 32; for some index of ctx, one expert below 1 is chosen by 32 rows on every device of that index.
All inputs are finite; a program needn't handle non-finite values.
Results may differ from the reference program's by a relative error of at most 0.022.
Values may be sent and summed in bfloat16 or wider, within the bound.
No kernel may reach another device: no remote copies, remote signals or barrier semaphores. Data moves between devices by JAX's collectives and lax.ppermute only.
A program may use at most 64 MiB of HBM per device.

```python
import math
import jax
import jax.numpy as jnp
from jax import lax

D = 4096
HEADS = 64
KV_HEADS = 4
HEAD_DIM = 128
EXPERTS = 128
TOPK = 8
EXP_HID = 768
HID_SPLIT = 4
TOK = 128
IMG = 256
SEQ = 1024
HID_DEV = 192
N_EXP = 4


def window_layout(key):
    order_key, frame_key = jax.random.split(key)
    block_count = SEQ // TOK
    order = jax.random.permutation(order_key, block_count).astype(jnp.int32)
    index = jnp.arange(SEQ, dtype=jnp.int32)
    placed = order[index // TOK] * TOK + index % TOK
    frame_count = SEQ // IMG + 1
    is_image = jax.random.randint(frame_key, (frame_count,), 0, 2)
    frame = placed // IMG
    frame_end = jnp.minimum((frame + 1) * IMG, SEQ) - 1
    bound = jnp.where(is_image[frame] == 1, frame_end, placed)
    return (placed.astype(jnp.int32), bound.astype(jnp.int32))


def topic_layout(key):
    topic_key = jax.random.fold_in(key, 101)
    table_key, key_pick, query_pick = jax.random.split(topic_key, 3)
    topic_total = 64
    sign_bits = jax.random.randint(table_key, (KV_HEADS, topic_total, HEAD_DIM), 0, 2)
    topic_table = (2 * sign_bits - 1).astype(jnp.float32)
    key_topic = jax.random.randint(key_pick, (SEQ, KV_HEADS), 0, topic_total).astype(jnp.int32)
    query_topic = jax.random.randint(query_pick, (SEQ, HEADS), 0, topic_total).astype(jnp.int32)
    return (topic_table, key_topic, query_topic)


def draw_positions(key, part):
    shared = window_layout(key)
    return shared[0]


def draw_bounds(key, part):
    shared = window_layout(key)
    return shared[1]


def draw_routes(key, part):
    key = jax.random.fold_in(key, 5)
    subkeys = jax.random.split(key, 7)
    block_rows = TOK // N_EXP
    block_count = SEQ // block_rows
    window_experts = N_EXP // HID_SPLIT
    capacity = max(2, block_rows // 2, (block_rows + window_experts - 1) // window_experts)
    hot_expert = jax.random.randint(subkeys[0], (block_count,), 0, window_experts)
    chosen_group = jax.random.randint(subkeys[1], (), 0, SEQ // TOK)
    group_hot = jax.random.randint(subkeys[2], (), 0, window_experts)
    block_ids = jnp.arange(block_count, dtype=jnp.int32)
    hot_expert = jnp.where(block_ids // N_EXP == chosen_group, group_hot, hot_expert).astype(jnp.int32)
    spread = max(window_experts - 1, 1)
    offset = jax.random.randint(subkeys[3], (block_count, 1), 0, spread)
    row_index = jnp.arange(block_rows, dtype=jnp.int32)[None, :]
    others = (row_index - capacity + offset) % spread
    others = jnp.where(others >= hot_expert[:, None], others + 1, others)
    computed = jnp.where(row_index < capacity, hot_expert[:, None], others).astype(jnp.int32)
    block_keys = jax.random.split(subkeys[4], block_count)
    computed = jax.vmap(lambda one_key, one_row: jax.random.permutation(one_key, one_row))(block_keys, computed)
    computed = computed.reshape(SEQ).astype(jnp.int32)
    row_keys = jax.random.split(subkeys[5], SEQ)
    rest = jax.vmap(lambda one_key: jax.random.permutation(one_key, EXPERTS - window_experts)[:TOPK - 1])(row_keys)
    rest = (rest + window_experts).astype(jnp.int32)
    column = jax.random.randint(subkeys[6], (SEQ, 1), 0, TOPK)
    slot_index = jnp.arange(TOPK, dtype=jnp.int32)[None, :]
    taken = jnp.clip(slot_index - (slot_index > column).astype(jnp.int32), 0, TOPK - 2)
    picked = jnp.take_along_axis(rest, taken, axis=1)
    return jnp.where(slot_index == column, computed[:, None], picked).astype(jnp.int32)


def draw_keys(key, part):
    topic_table, key_topic, query_topic = topic_layout(key)
    key = jax.random.fold_in(key, 13)
    head_ids = jnp.arange(KV_HEADS, dtype=jnp.int32)[None, :]
    topic_shift = topic_table[head_ids, key_topic]
    shape = (SEQ, KV_HEADS, HEAD_DIM)
    noise_part = jnp.clip(jax.random.normal(key, shape, jnp.float32), -6.0, 6.0)
    return (noise_part + 0.8 * topic_shift).reshape(SEQ, KV_HEADS * HEAD_DIM).astype(jnp.bfloat16)


def draw_queries(key, part):
    topic_table, key_topic, query_topic = topic_layout(key)
    key = jax.random.fold_in(key, 11)
    noise_key = jax.random.fold_in(key, 0)
    head_kv = jnp.arange(HEADS, dtype=jnp.int32) // (HEADS // KV_HEADS)
    per_head = topic_table[head_kv]
    head_ids = jnp.arange(HEADS, dtype=jnp.int32)[None, :]
    topic_shift = per_head[head_ids, query_topic].reshape(SEQ, HEADS * HEAD_DIM)
    shape = (SEQ, HEADS * HEAD_DIM)
    noise_part = jnp.clip(jax.random.normal(noise_key, shape, jnp.float32), -6.0, 6.0)
    return (noise_part + 0.8 * topic_shift).astype(jnp.bfloat16)


def draw_residual(key, part):
    key = jax.random.fold_in(key, 7)
    row_key, col_key, noise_key = jax.random.split(key, 3)
    row_scale = 0.3 * jnp.exp(jax.random.uniform(row_key, (SEQ, 1), jnp.float32, 0.0, 2.302585))
    col_scale = 0.3 * jnp.exp(jax.random.uniform(col_key, (1, D), jnp.float32, 0.0, 2.302585))
    noise_part = jnp.clip(jax.random.normal(noise_key, (SEQ, D), jnp.float32), -4.0, 4.0)
    return (noise_part * row_scale * col_scale).astype(jnp.bfloat16)


def level_of(own_key, shape, shards, low, top_value):
    def one(position, shards_of):
        steps = jax.random.uniform(jax.random.fold_in(jax.random.fold_in(own_key, 6), position), (shards_of,), jnp.float32, low / len(shards), top_value / len(shards))
        return jnp.repeat(jnp.exp(steps), shape[position] // shards_of).reshape((-1,) + (1,) * (len(shape) - position - 1))

    gain = one(*shards[0])
    for cut in shards[1:]:
        gain = gain * one(*cut)
    return gain


def normal_values(key, dims, deviation, most, cuts=(), held_as=jnp.bfloat16):
    values = jax.random.normal(key, dims, jnp.float32) * deviation
    if len(cuts) > 0:
        values = level_of(key, dims, cuts, -0.22, 0.18) * values
    return jnp.clip(values, min=-most, max=most).astype(held_as)


def setup_inputs(seed: int = 0) -> dict:
    arg_keys = jax.random.split(jax.random.key(seed), 13)
    return {
        "queries": draw_queries(jax.random.fold_in(arg_keys[12], 71), 0),
        "keys": draw_keys(jax.random.fold_in(arg_keys[12], 71), 0),
        "values": normal_values(arg_keys[2], (SEQ, KV_HEADS * HEAD_DIM), 1.0, 6.0, ((0, 8),)),
        "positions": draw_positions(jax.random.fold_in(arg_keys[12], 71), 0),
        "bounds": draw_bounds(jax.random.fold_in(arg_keys[12], 71), 0),
        "w_out": normal_values(arg_keys[5], (HEADS * HEAD_DIM, D), (HEADS * HEAD_DIM) ** -0.5, 0.0625, ((0, 4),)),
        "residual": draw_residual(jax.random.fold_in(arg_keys[12], 71), 0),
        "norm_gain": jnp.clip(1.0 + 0.18 * jax.random.normal(arg_keys[7], (D,), jnp.float32), 0.1, 1.9),
        "routes": draw_routes(jax.random.fold_in(arg_keys[12], 71), 0),
        "gates": jnp.clip(jnp.exp(math.log(1.0) - 2.3025851 * jax.random.uniform(arg_keys[9], (SEQ, TOPK), jnp.float32) ** level_of(arg_keys[9], (SEQ, TOPK), ((0, 32),), -0.2, 0.2)), 0.1, 1.0),
        "w_in": normal_values(arg_keys[10], (N_EXP, 2 * HID_DEV, D), D ** -0.5, 0.09375, ((0, 4),)),
        "w_back": normal_values(arg_keys[11], (N_EXP, HID_DEV, D), (max(EXP_HID // 64, 1)) ** -0.5, 1.75, ((0, 4),)),
    }


def settle(value):
    return lax.optimization_barrier(value.astype(jnp.bfloat16)).astype(jnp.float32)

def attend_all(queries, keys, values, positions, bounds):
    query_block = math.gcd(SEQ, 1024)
    scale = HEAD_DIM ** (-0.5)
    grouped = HEADS // KV_HEADS
    query_heads = queries.reshape(SEQ, HEADS, HEAD_DIM).transpose(1, 0, 2)
    key_heads = keys.reshape(SEQ, KV_HEADS, HEAD_DIM).transpose(1, 0, 2)
    value_heads = values.reshape(SEQ, KV_HEADS, HEAD_DIM).transpose(1, 0, 2)
    bound_blocks = bounds.reshape(SEQ // query_block, query_block)

    def one_head(inputs):
        query_head, head_number = inputs
        key_head = key_heads[head_number // grouped]
        value_head = value_heads[head_number // grouped]

        def one_block(block_inputs):
            query_rows, bound_rows = block_inputs
            scores = jnp.dot(query_rows, key_head.T, preferred_element_type=jnp.float32) * scale
            visible = positions[None, :] <= bound_rows[:, None]
            row_max = lax.optimization_barrier(jnp.max(jnp.where(visible, scores, -1e+30), axis=1, keepdims=True))
            weights = jnp.where(visible, jnp.exp(scores - row_max), 0.0)
            row_sum = lax.optimization_barrier(jnp.sum(weights, axis=1, keepdims=True))
            summed = jnp.dot(weights.astype(jnp.bfloat16), value_head, preferred_element_type=jnp.float32)
            return (summed / row_sum).astype(jnp.bfloat16)
        query_rows = query_head.reshape(SEQ // query_block, query_block, HEAD_DIM)
        return lax.map(one_block, (query_rows, bound_blocks)).reshape(SEQ, HEAD_DIM)
    attended = lax.map(one_head, (query_heads, jnp.arange(HEADS, dtype=jnp.int32)))
    return attended.transpose(1, 0, 2).reshape(SEQ, HEADS * HEAD_DIM)

def reference(queries, keys, values, positions, bounds, w_out, residual, norm_gain, routes, gates, w_in, w_back):
    attended = attend_all(queries, keys, values, positions, bounds)
    group_cols = HEADS // N_EXP * HEAD_DIM
    attn_sum = jnp.zeros((SEQ, D), jnp.float32)
    for group_number in range(N_EXP):
        lower = group_number * group_cols
        upper = lower + group_cols
        part = jnp.dot(attended[:, lower:upper], w_out[lower:upper], preferred_element_type=jnp.float32)
        attn_sum = attn_sum + settle(part)
    middle = (residual.astype(jnp.float32) + attn_sum).astype(jnp.bfloat16)
    wide = middle.astype(jnp.float32)
    mean_square = lax.optimization_barrier(jnp.mean(wide * wide, axis=1, keepdims=True))
    normed = (wide * lax.rsqrt(mean_square + 1e-06) * norm_gain.astype(jnp.float32)[None, :]).astype(jnp.bfloat16)
    shares = gates / lax.optimization_barrier(jnp.sum(gates, axis=1, keepdims=True))
    expert_total = jnp.zeros((SEQ, D), jnp.float32)
    for slice_number in range(N_EXP):
        expert_id = slice_number // HID_SPLIT
        coefficient = lax.optimization_barrier(jnp.sum(jnp.where(routes == expert_id, shares, 0.0), axis=1, keepdims=True)).astype(jnp.bfloat16)
        projected = jnp.dot(normed, w_in[slice_number].T, preferred_element_type=jnp.float32)
        activated = jax.nn.silu(projected[:, :HID_DEV]) * projected[:, HID_DEV:]
        blended = (coefficient.astype(jnp.float32) * activated).astype(jnp.bfloat16)
        expert_total = expert_total + settle(jnp.dot(blended, w_back[slice_number], preferred_element_type=jnp.float32))
    return (middle, expert_total.astype(jnp.bfloat16))
```

```python
import functools

import jax
import jax.numpy as jnp
from jax import lax
from jax.experimental import pallas as pl
from jax.experimental.pallas import tpu as pltpu
from jax.sharding import PartitionSpec as P

D = 4096
HEADS = 64
KV_HEADS = 4
HEAD_DIM = 128
HID_SPLIT = 4
STACK = 4
COL_CHUNKS = 4
PAD_ROWS = 16
LOG2E = 1.4426950408889634
VMEM = pl.BlockSpec(memory_space=pltpu.VMEM)


def exchange(value, axis, offset, size):
    return lax.ppermute(value, axis, [(i, i ^ offset) for i in range(size)])


def attend_kernel(
    block_count,
    rank_ref,
    q_ref,
    bound_ref,
    resid_ref,
    *refs,
):
    payloads = refs[:block_count]
    w_hbm = refs[block_count]
    outs = refs[block_count + 1 : block_count + 1 + COL_CHUNKS]
    w_buf, k_buf, v_buf, bias, attended, acc, sems = refs[block_count + 1 + COL_CHUNKS :]
    tok = q_ref.shape[0]
    heads = q_ref.shape[1] // HEAD_DIM
    cols = D // COL_CHUNKS
    copies = []
    for chunk in range(COL_CHUNKS):
        copy = pltpu.make_async_copy(
            w_hbm.at[:, pl.ds(chunk * cols, cols)], w_buf.at[chunk], sems.at[chunk]
        )
        copy.start()
        copies.append(copy)
    bound = bound_ref[...]
    lane = lax.broadcasted_iota(jnp.int32, (1, tok), 1).astype(jnp.float32)
    ones = jnp.ones((tok, HEAD_DIM), jnp.bfloat16)
    for b in range(block_count):
        rows = slice(b * tok, (b + 1) * tok)
        k_buf[rows, :] = payloads[b][:tok, :HEAD_DIM]
        v_buf[rows, :HEAD_DIM] = payloads[b][:tok, HEAD_DIM:]
        v_buf[rows, HEAD_DIM:] = ones
        start = payloads[b][tok : tok + PAD_ROWS, :HEAD_DIM].astype(jnp.float32)[:1]
        place = start * tok + lane
        bias[:, rows] = jnp.where(place <= bound, 0.0, -1e30)
    factor = HEAD_DIM ** (-0.5) * LOG2E

    def some_heads(step, carry):
        base = step * STACK * HEAD_DIM
        parts = []
        for j in range(STACK):
            start = pl.multiple_of(base + j * HEAD_DIM, HEAD_DIM)
            parts.append(q_ref[:, pl.ds(start, HEAD_DIM)])
        stacked = jnp.concatenate(parts, axis=0)
        scores = lax.dot_general(
            stacked, k_buf[...], (((1,), (1,)), ((), ())), preferred_element_type=jnp.float32
        )
        scores = scores.reshape(STACK, tok, -1) * factor + bias[...][None]
        row_max = jnp.max(scores, axis=2, keepdims=True)
        weights = jnp.exp2(scores - row_max).astype(jnp.bfloat16)
        summed = jnp.dot(
            weights.reshape(STACK * tok, -1), v_buf[...], preferred_element_type=jnp.float32
        )
        result = (summed[:, :HEAD_DIM] / summed[:, HEAD_DIM:]).astype(jnp.bfloat16)
        for j in range(STACK):
            start = pl.multiple_of(base + j * HEAD_DIM, HEAD_DIM)
            attended[:, pl.ds(start, HEAD_DIM)] = result[j * tok : (j + 1) * tok]
        return carry

    lax.fori_loop(0, heads // STACK, some_heads, 0)
    home = resid_ref.shape[0]
    first = pl.multiple_of(rank_ref[0] * home, home)
    for chunk in range(COL_CHUNKS):
        copies[chunk].wait()
        acc[...] = jnp.dot(attended[...], w_buf[chunk], preferred_element_type=jnp.float32)
        own = resid_ref[:, chunk * cols : (chunk + 1) * cols].astype(jnp.float32)
        acc[pl.ds(first, home), :] += own
        outs[chunk][...] = acc[...].astype(jnp.bfloat16)


def attend_project(rank, queries, bounds, residual, payloads, w_out):
    tok, width = queries.shape
    count = len(payloads)
    cols = D // COL_CHUNKS
    keys_in_all = tok * count
    return pl.pallas_call(
        functools.partial(attend_kernel, count),
        out_shape=[jax.ShapeDtypeStruct((tok, cols), jnp.bfloat16)] * COL_CHUNKS,
        in_specs=[pl.BlockSpec(memory_space=pltpu.SMEM)]
        + [VMEM] * (3 + count)
        + [pl.BlockSpec(memory_space=pl.ANY)],
        out_specs=[VMEM] * COL_CHUNKS,
        scratch_shapes=[
            pltpu.VMEM((COL_CHUNKS, width, cols), jnp.bfloat16),
            pltpu.VMEM((keys_in_all, HEAD_DIM), jnp.bfloat16),
            pltpu.VMEM((keys_in_all, 2 * HEAD_DIM), jnp.bfloat16),
            pltpu.VMEM((tok, keys_in_all), jnp.float32),
            pltpu.VMEM((tok, width), jnp.bfloat16),
            pltpu.VMEM((tok, cols), jnp.float32),
            pltpu.SemaphoreType.DMA((COL_CHUNKS,)),
        ],
        compiler_params=pltpu.CompilerParams(vmem_limit_bytes=44 * 1024 * 1024),
        cost_estimate=pl.CostEstimate(
            flops=2 * tok * width * (2 * keys_in_all + D),
            bytes_accessed=2 * width * D,
            transcendentals=tok * width // HEAD_DIM * keys_in_all,
        ),
        name="attend_project",
    )(rank, queries, bounds, residual, *payloads, w_out)


def own_heads(queries, keys, values):
    heads_here = queries.shape[1] // HEAD_DIM
    kv_number = lax.axis_index("exp") * heads_here // (HEADS // KV_HEADS)
    key_head = lax.dynamic_slice_in_dim(keys, kv_number * HEAD_DIM, HEAD_DIM, 1)
    value_head = lax.dynamic_slice_in_dim(values, kv_number * HEAD_DIM, HEAD_DIM, 1)
    return key_head, value_head


def line_device(
    queries,
    keys,
    values,
    positions,
    bounds,
    w_out,
    residual,
    norm_gain,
    routes,
    gates,
    w_in,
    w_back,
):
    tok = queries.shape[0]
    home = residual.shape[0]
    hidden = w_back.shape[1]
    ctx_count = lax.axis_size("ctx")
    exp_count = lax.axis_size("exp")
    rank = lax.axis_index("exp")
    key_head, value_head = own_heads(queries, keys, values)
    block = (positions[0] // tok).astype(jnp.bfloat16)
    pair = jnp.concatenate([key_head, value_head], axis=1)
    payload = jnp.concatenate(
        [pair, jnp.full((PAD_ROWS, 2 * HEAD_DIM), block, jnp.bfloat16)], axis=0
    )
    payloads = [payload] + [exchange(payload, "ctx", r, ctx_count) for r in range(1, ctx_count)]
    parts = attend_project(
        rank.astype(jnp.int32).reshape(1),
        queries,
        bounds.astype(jnp.float32).reshape(tok, 1),
        residual,
        payloads,
        w_out,
    )
    at_end = (rank == 0) | (rank == exp_count - 1)
    cols = D // COL_CHUNKS
    flat_in = w_in.reshape(2 * hidden, D)
    total_square = jnp.zeros((tok, 1), jnp.float32)
    projected = jnp.zeros((tok, 2 * hidden), jnp.float32)
    middles = []
    for chunk in range(COL_CHUNKS):
        inward = lax.ppermute(parts[chunk], "exp", [(0, 1), (3, 2)])
        near = parts[chunk] + inward
        across = lax.ppermute(near, "exp", [(1, 2), (2, 1)])
        total = near + across
        outward = lax.ppermute(total, "exp", [(1, 0), (2, 3)])
        middle = jnp.where(at_end, outward, total)
        wide = middle.astype(jnp.float32)
        total_square = total_square + jnp.sum(wide * wide, axis=1, keepdims=True)
        span = slice(chunk * cols, (chunk + 1) * cols)
        gained = (wide * norm_gain[None, span]).astype(jnp.bfloat16)
        projected = projected + lax.dot_general(
            gained,
            flat_in[:, span],
            (((1,), (1,)), ((), ())),
            preferred_element_type=jnp.float32,
        )
        middles.append(lax.dynamic_slice_in_dim(middle, rank * home, home, 0))
    middle_out = jnp.concatenate(middles, axis=1)
    projected = projected * lax.rsqrt(total_square / D + 1e-06)
    activated = (jax.nn.silu(projected[:, :hidden]) * projected[:, hidden:]).astype(jnp.bfloat16)
    share = jnp.dot(
        activated, w_back.reshape(hidden, D), preferred_element_type=jnp.float32
    ).astype(jnp.bfloat16)
    gathered = lax.dynamic_slice_in_dim(share, rank * home, home, 0).astype(jnp.float32)
    for offset in range(1, exp_count):
        leaving = lax.dynamic_slice_in_dim(share, (rank ^ offset) * home, home, 0)
        gathered = gathered + exchange(leaving, "exp", offset, exp_count).astype(jnp.float32)
    shares = gates / jnp.sum(gates, axis=1, keepdims=True)
    coefficient = jnp.sum(jnp.where(routes == 0, shares, 0.0), axis=1, keepdims=True)
    coefficient = coefficient.astype(jnp.bfloat16).astype(jnp.float32)
    return (middle_out, (gathered * coefficient).astype(jnp.bfloat16))


def largest_divisor(row_count):
    candidate = min(row_count, 1024)
    while row_count % candidate != 0:
        candidate = candidate - 1
    return candidate


def apply_slice(row_block, coefficient, w_in, w_back):
    hidden_here = w_back.shape[1]
    flat_in = w_in.reshape(2 * hidden_here, D)
    projected = lax.dot_general(
        row_block, flat_in, (((1,), (1,)), ((), ())), preferred_element_type=jnp.float32
    )
    activated = jax.nn.silu(projected[:, :hidden_here]) * projected[:, hidden_here:]
    blended = (coefficient.astype(jnp.float32) * activated).astype(jnp.bfloat16)
    flat_back = w_back.reshape(hidden_here, D)
    return jnp.dot(blended, flat_back, preferred_element_type=jnp.float32).astype(jnp.bfloat16)


def wide_device(
    queries,
    keys,
    values,
    positions,
    bounds,
    w_out,
    residual,
    norm_gain,
    routes,
    gates,
    w_in,
    w_back,
):
    tok_rows = queries.shape[0]
    head_cols = queries.shape[1]
    heads_here = head_cols // HEAD_DIM
    exp_count = lax.axis_size("exp")
    key_head, value_head = own_heads(queries, keys, values)
    query_heads = queries.reshape(tok_rows, heads_here, HEAD_DIM).transpose(1, 0, 2)
    scale = HEAD_DIM ** (-0.5)
    reach_max = jnp.max(bounds)
    all_keys, all_values, all_places = (
        lax.all_gather(key_head, "ctx", axis=0, tiled=True),
        lax.all_gather(value_head, "ctx", axis=0, tiled=True),
        lax.all_gather(positions, "ctx", axis=0, tiled=True),
    )
    total_rows = all_keys.shape[0]
    tile_len = largest_divisor(total_rows)
    tile_count = total_rows // tile_len

    def process(state_in, key_rows, value_rows, place_rows):
        row_max, row_sum, running = state_in
        scores = (
            jnp.einsum("htd,nd->htn", query_heads, key_rows, preferred_element_type=jnp.float32)
            * scale
        )
        visible = (place_rows[None, :] <= bounds[:, None])[None, :, :]
        masked = jnp.where(visible, scores, -1e30)
        new_max = jnp.maximum(row_max, jnp.max(masked, axis=2))
        weights = jnp.exp(masked - new_max[..., None])
        rescale = jnp.exp(row_max - new_max)
        row_sum = row_sum * rescale + jnp.sum(weights, axis=2)
        running = running * rescale[..., None] + jnp.einsum(
            "htn,nd->htd",
            weights.astype(jnp.bfloat16),
            value_rows,
            preferred_element_type=jnp.float32,
        )
        return (new_max, row_sum, running)

    def one_tile(tile_number, state_now):
        first = tile_number * tile_len
        key_rows = lax.dynamic_slice_in_dim(all_keys, first, tile_len, 0)
        value_rows = lax.dynamic_slice_in_dim(all_values, first, tile_len, 0)
        place_rows = lax.dynamic_slice_in_dim(all_places, first, tile_len, 0)
        return lax.cond(
            jnp.min(place_rows) <= reach_max,
            lambda state_in: process(state_in, key_rows, value_rows, place_rows),
            lambda state_in: state_in,
            state_now,
        )

    start_state = (
        jnp.full((heads_here, tok_rows), -1e30, jnp.float32),
        jnp.zeros((heads_here, tok_rows), jnp.float32),
        jnp.zeros((heads_here, tok_rows, HEAD_DIM), jnp.float32),
    )
    row_max, row_sum, running = lax.fori_loop(0, tile_count, one_tile, start_state)
    attended = (running / row_sum[..., None]).astype(jnp.bfloat16)
    attended = attended.transpose(1, 0, 2).reshape(tok_rows, head_cols)
    attention_rows = lax.psum_scatter(
        jnp.dot(attended, w_out, preferred_element_type=jnp.float32).astype(jnp.bfloat16),
        "exp",
        scatter_dimension=0,
        tiled=True,
    ).astype(jnp.float32)
    middle = (residual.astype(jnp.float32) + attention_rows).astype(jnp.bfloat16)
    wide = middle.astype(jnp.float32)
    mean_square = jnp.mean(wide * wide, axis=1, keepdims=True)
    normed = (wide * lax.rsqrt(mean_square + 1e-06) * norm_gain[None, :]).astype(jnp.bfloat16)
    local_rows = residual.shape[0]
    shares = gates / jnp.sum(gates, axis=1, keepdims=True)
    slice_expert = jnp.arange(exp_count, dtype=jnp.int32) // HID_SPLIT
    hits = routes[:, :, None] == slice_expert[None, None, :]
    coefficient = jnp.sum(jnp.where(hits, shares[:, :, None], 0.0), axis=1).astype(jnp.bfloat16)
    owner_weights = coefficient.transpose(1, 0)[:, :, None]
    copies = jnp.broadcast_to(normed[None, :, :], (exp_count, local_rows, D))
    row_block = lax.all_to_all(copies, "exp", split_axis=0, concat_axis=0, tiled=True)
    weight_block = lax.all_to_all(owner_weights, "exp", split_axis=0, concat_axis=0, tiled=True)
    slot_count = row_block.shape[1]
    produced = apply_slice(
        row_block.reshape(exp_count * slot_count, D),
        weight_block.reshape(exp_count * slot_count, 1),
        w_in,
        w_back,
    )
    produced = produced.reshape(exp_count, slot_count, D)
    arrived = lax.all_to_all(produced, "exp", split_axis=0, concat_axis=0, tiled=True)
    expert_out = jnp.sum(arrived.astype(jnp.float32), axis=0).astype(jnp.bfloat16)
    return (middle, expert_out)


def solution(mesh):
    in_specs = (
        P("ctx", "exp"),
        P("ctx", None),
        P("ctx", None),
        P("ctx"),
        P("ctx"),
        P("exp", None),
        P(("ctx", "exp"), None),
        P(),
        P(("ctx", "exp"), None),
        P(("ctx", "exp"), None),
        P("exp", None, None),
        P("exp", None, None),
    )
    out_specs = (P(("ctx", "exp"), None), P(("ctx", "exp"), None))
    one_line = mesh.shape["exp"] == HID_SPLIT and mesh.shape["ctx"] == 8
    return jax.shard_map(
        line_device if one_line else wide_device,
        mesh=mesh,
        in_specs=in_specs,
        out_specs=out_specs,
        check_vma=False,
    )
```

```python
import functools

import jax
import jax.numpy as jnp
from jax import lax
from jax.experimental import pallas as pl
from jax.experimental.pallas import tpu as pltpu
from jax.sharding import PartitionSpec as P

D = 4096
HEADS = 64
KV_HEADS = 4
HEAD_DIM = 128
HID_SPLIT = 4
STACK = 4
WIDTHS = (1024, 1024, 1024, 512, 512)
SPANS = tuple((sum(WIDTHS[:i]), width) for i, width in enumerate(WIDTHS))
PAD_ROWS = 16
ORDER = (
    ("near", 0),
    ("near", 1),
    ("total", 0),
    ("near", 2),
    ("total", 1),
    ("near", 3),
    ("absorb", 0),
    ("near", 4),
    ("total", 2),
    ("absorb", 1),
    ("total", 3),
    ("total", 4),
    ("absorb", 2),
    ("absorb", 3),
    ("absorb", 4),
)
LOG2E = 1.4426950408889634
VMEM = pl.BlockSpec(memory_space=pltpu.VMEM)
ANY = pl.BlockSpec(memory_space=pl.ANY)
LIGHT = pl.CostEstimate(flops=1024, bytes_accessed=1024, transcendentals=0)


def exchange(value, axis, offset, size):
    return lax.ppermute(value, axis, [(i, i ^ offset) for i in range(size)])


def attend_kernel(rank_ref, bound_ref, same_ref, other_ref, q_hbm, resid_hbm, w_hbm, after_ref, *refs):
    outs = refs[: len(WIDTHS)]
    q_ref, resid_ref, w_buf, k_buf, v_buf, bias, attended, acc, sems, side = refs[len(WIDTHS) :]
    tok = q_ref.shape[0]
    heads = q_ref.shape[1] // HEAD_DIM
    q_copy = pltpu.make_async_copy(q_hbm, q_ref, side.at[0])
    q_copy.start()
    resid_copy = pltpu.make_async_copy(resid_hbm, resid_ref, side.at[1])
    resid_copy.start()
    copies = []
    for chunk, (first, width) in enumerate(SPANS):
        span = pl.ds(first, width)
        copy = pltpu.make_async_copy(w_hbm.at[:, span], w_buf.at[:, span], sems.at[chunk])
        copy.start()
        copies.append(copy)
    bound = bound_ref[...]
    lane = lax.broadcasted_iota(jnp.int32, (1, tok), 1).astype(jnp.float32)
    ones = jnp.ones((tok, HEAD_DIM), jnp.bfloat16)
    half_count = same_ref.shape[0]
    for b in range(2 * half_count):
        rows = slice(b * tok, (b + 1) * tok)
        group, row = (same_ref, b) if b < half_count else (other_ref, b - half_count)
        k_buf[rows, :] = group[row, :tok, :HEAD_DIM]
        v_buf[rows, :HEAD_DIM] = group[row, :tok, HEAD_DIM:]
        v_buf[rows, HEAD_DIM:] = ones
        start = group[row, tok : tok + PAD_ROWS, :HEAD_DIM].astype(jnp.float32)[:1]
        place = start * tok + lane
        bias[:, rows] = jnp.where(place <= bound, 0.0, -1e30)
    factor = HEAD_DIM ** (-0.5) * LOG2E
    q_copy.wait()

    def some_heads(step, carry):
        base = step * STACK * HEAD_DIM
        parts = []
        for j in range(STACK):
            start = pl.multiple_of(base + j * HEAD_DIM, HEAD_DIM)
            parts.append(q_ref[:, pl.ds(start, HEAD_DIM)])
        stacked = jnp.concatenate(parts, axis=0)
        scores = lax.dot_general(
            stacked, k_buf[...], (((1,), (1,)), ((), ())), preferred_element_type=jnp.float32
        )
        scores = scores.reshape(STACK, tok, -1) * factor + bias[...][None]
        row_max = jnp.max(scores, axis=2, keepdims=True)
        weights = jnp.exp2(scores - row_max).astype(jnp.bfloat16)
        summed = jnp.dot(
            weights.reshape(STACK * tok, -1), v_buf[...], preferred_element_type=jnp.float32
        )
        result = (summed[:, :HEAD_DIM] / summed[:, HEAD_DIM:]).astype(jnp.bfloat16)
        for j in range(STACK):
            start = pl.multiple_of(base + j * HEAD_DIM, HEAD_DIM)
            attended[:, pl.ds(start, HEAD_DIM)] = result[j * tok : (j + 1) * tok]
        return carry

    lax.fori_loop(0, heads // STACK, some_heads, 0)
    resid_copy.wait()
    home = resid_ref.shape[0]
    top = pl.multiple_of(rank_ref[0] * home, home)
    for chunk, (first, width) in enumerate(SPANS):
        copies[chunk].wait()
        span = slice(first, first + width)
        acc[:, span] = jnp.dot(
            attended[...], w_buf[:, span], preferred_element_type=jnp.float32
        )
        acc[pl.ds(top, home), span] += resid_ref[:, span].astype(jnp.float32)
        outs[chunk][...] = acc[:, span].astype(jnp.bfloat16)


def attend_project(rank, bounds, same, other, queries, residual, w_out, after):
    tok, width = queries.shape
    keys_in_all = 2 * same.shape[0] * tok
    return pl.pallas_call(
        attend_kernel,
        out_shape=[jax.ShapeDtypeStruct((tok, w), jnp.bfloat16) for w in WIDTHS],
        in_specs=[pl.BlockSpec(memory_space=pltpu.SMEM)] + [VMEM] * 3 + [ANY] * 4,
        out_specs=[VMEM] * len(WIDTHS),
        scratch_shapes=[
            pltpu.VMEM(queries.shape, jnp.bfloat16),
            pltpu.VMEM(residual.shape, jnp.bfloat16),
            pltpu.VMEM((width, D), jnp.bfloat16),
            pltpu.VMEM((keys_in_all, HEAD_DIM), jnp.bfloat16),
            pltpu.VMEM((keys_in_all, 2 * HEAD_DIM), jnp.bfloat16),
            pltpu.VMEM((tok, keys_in_all), jnp.float32),
            pltpu.VMEM((tok, width), jnp.bfloat16),
            pltpu.VMEM((tok, D), jnp.float32),
            pltpu.SemaphoreType.DMA((len(WIDTHS),)),
            pltpu.SemaphoreType.DMA((2,)),
        ],
        compiler_params=pltpu.CompilerParams(vmem_limit_bytes=36 * 1024 * 1024),
        cost_estimate=LIGHT,
        name="attend_project",
    )(rank, bounds, same, other, queries, residual, w_out, after)


def down_kernel(place_ref, coef_ref, a0, a1, a2, a3, own_ref, same_ref, other_ref, out_ref):
    coef = coef_ref[...]
    blended = [(a[...].astype(jnp.float32) * coef).astype(jnp.bfloat16) for a in (a0, a1, a2, a3)]
    hidden = own_ref.shape[0]
    count, _, width = same_ref.shape
    for group, buf in enumerate((same_ref, other_ref)):
        for j in range(count):
            block = place_ref[0] ^ (2 * j + group)
            span = pl.ds(pl.multiple_of(block * width, width), width)
            total = jnp.dot(blended[0], own_ref[:, span], preferred_element_type=jnp.float32)
            for s in range(1, len(blended)):
                rows = slice((s - 1) * hidden, s * hidden)
                total += jnp.dot(
                    blended[s], buf[j, rows, :], preferred_element_type=jnp.float32
                )
            out_ref[:, span] = total.astype(jnp.bfloat16)


def down(place, coefficient, acts, own, same, other):
    rows = acts[0].shape[0]
    return pl.pallas_call(
        down_kernel,
        out_shape=jax.ShapeDtypeStruct((rows, D), jnp.bfloat16),
        in_specs=[pl.BlockSpec(memory_space=pltpu.SMEM)] + [VMEM] * 8,
        out_specs=VMEM,
        compiler_params=pltpu.CompilerParams(vmem_limit_bytes=24 * 1024 * 1024),
        cost_estimate=LIGHT,
        name="down",
    )(place, coefficient, *acts, own, same, other)


def half_kernel(first, after_ref, piece_ref, out_ref):
    out_ref[...] = piece_ref[first : first + out_ref.shape[0], :]


def half_after(piece, first, after):
    shape = (piece.shape[0] // 2, piece.shape[1])
    return pl.pallas_call(
        functools.partial(half_kernel, first),
        out_shape=jax.ShapeDtypeStruct(shape, jnp.bfloat16),
        in_specs=[ANY, VMEM],
        out_specs=VMEM,
        compiler_params=pltpu.CompilerParams(vmem_limit_bytes=4 * 1024 * 1024),
        cost_estimate=LIGHT,
        name="half_after",
    )(after, piece)


def join_kernel(*refs):
    out_ref = refs[-1]
    first = 0
    for piece in refs[1:-1]:
        rows = piece.shape[0]
        out_ref[first : first + rows, :] = piece[...]
        first += rows


def join_after(pieces, after):
    rows = sum(piece.shape[0] for piece in pieces)
    width = pieces[0].shape[1]
    return pl.pallas_call(
        join_kernel,
        out_shape=jax.ShapeDtypeStruct((rows, width), jnp.bfloat16),
        in_specs=[ANY] + [VMEM] * len(pieces),
        out_specs=VMEM,
        compiler_params=pltpu.CompilerParams(vmem_limit_bytes=8 * 1024 * 1024),
        cost_estimate=LIGHT,
        name="join_after",
    )(after, *pieces)


def shard_kernel(place_ref, whole_hbm, after_ref, out_ref, sem):
    width = out_ref.shape[1]
    first = pl.multiple_of(place_ref[0] * width, width)
    copy = pltpu.make_async_copy(whole_hbm.at[:, pl.ds(first, width)], out_ref, sem)
    copy.start()
    copy.wait()


def shard_after(place, whole, width, after):
    return pl.pallas_call(
        shard_kernel,
        out_shape=jax.ShapeDtypeStruct((whole.shape[0], width), jnp.bfloat16),
        in_specs=[pl.BlockSpec(memory_space=pltpu.SMEM), ANY, ANY],
        out_specs=VMEM,
        scratch_shapes=[pltpu.SemaphoreType.DMA],
        compiler_params=pltpu.CompilerParams(vmem_limit_bytes=4 * 1024 * 1024),
        cost_estimate=LIGHT,
        name="shard_after",
    )(place, whole, after)


def add_kernel(a_ref, b_ref, after_ref, out_ref):
    out_ref[...] = (a_ref[...].astype(jnp.float32) + b_ref[...].astype(jnp.float32)).astype(
        jnp.bfloat16
    )


def add_after(left, right, after):
    return pl.pallas_call(
        add_kernel,
        out_shape=jax.ShapeDtypeStruct(left.shape, jnp.bfloat16),
        in_specs=[VMEM, VMEM, ANY],
        out_specs=VMEM,
        compiler_params=pltpu.CompilerParams(vmem_limit_bytes=4 * 1024 * 1024),
        cost_estimate=LIGHT,
        name="add_after",
    )(left, right, after)


def absorb_kernel(chunk, flag_ref, total_ref, outward_ref, gain_ref, w_ref, *refs):
    last = chunk == len(WIDTHS) - 1
    states = refs[1 : 1 if chunk == 0 else 3]
    outs = refs[1 + len(states) : -1]
    scratch = refs[-1]
    first, width = SPANS[chunk]
    span = slice(first, first + width)
    middle = jnp.where(flag_ref[1] == 1, outward_ref[...], total_ref[...])
    scratch[...] = middle
    home_ref = outs[0]
    home = home_ref.shape[0]
    top = pl.multiple_of(flag_ref[0] * home, home)
    home_ref[...] = scratch[pl.ds(top, home), :]
    wide = middle.astype(jnp.float32)
    gained = (wide * gain_ref[:, span]).astype(jnp.bfloat16)
    product = lax.dot_general(
        gained, w_ref[:, span], (((1,), (1,)), ((), ())), preferred_element_type=jnp.float32
    )
    square = sum(
        wide[:, i * 128 : (i + 1) * 128] * wide[:, i * 128 : (i + 1) * 128]
        for i in range(width // 128)
    )
    if chunk > 0:
        product += states[0][...]
        square += states[1][...]
    if last:
        hidden = product.shape[1] // 2
        mean_square = jnp.sum(square, axis=1, keepdims=True) / D
        product = product * lax.rsqrt(mean_square + 1e-06)
        gate = product[:, :hidden]
        act = gate / (1.0 + jnp.exp(-gate)) * product[:, hidden:]
        outs[1][...] = act.astype(jnp.bfloat16)
    else:
        outs[1][...] = product
        outs[2][...] = square


def absorb(chunk, flags, total, outward, gain, w_in, after, states):
    tok, width = total.shape
    rows = w_in.shape[0]
    home = jax.ShapeDtypeStruct((tok // lax.axis_size("exp"), width), jnp.bfloat16)
    if chunk == len(WIDTHS) - 1:
        out_shape = [home, jax.ShapeDtypeStruct((tok, rows // 2), jnp.bfloat16)]
    else:
        out_shape = [
            home,
            jax.ShapeDtypeStruct((tok, rows), jnp.float32),
            jax.ShapeDtypeStruct((tok, 128), jnp.float32),
        ]
    return pl.pallas_call(
        functools.partial(absorb_kernel, chunk),
        out_shape=out_shape,
        in_specs=[pl.BlockSpec(memory_space=pltpu.SMEM)]
        + [VMEM] * 4
        + [ANY]
        + [VMEM] * len(states),
        out_specs=[VMEM] * len(out_shape),
        scratch_shapes=[pltpu.VMEM((tok, width), jnp.bfloat16)],
        compiler_params=pltpu.CompilerParams(vmem_limit_bytes=12 * 1024 * 1024),
        cost_estimate=LIGHT,
        name="absorb",
    )(flags, total, outward, gain, w_in, after, *states)


def own_heads(queries, keys, values):
    heads_here = queries.shape[1] // HEAD_DIM
    kv_number = lax.axis_index("exp") * heads_here // (HEADS // KV_HEADS)
    key_head = lax.dynamic_slice_in_dim(keys, kv_number * HEAD_DIM, HEAD_DIM, 1)
    value_head = lax.dynamic_slice_in_dim(values, kv_number * HEAD_DIM, HEAD_DIM, 1)
    return key_head, value_head


def line_device(
    queries,
    keys,
    values,
    positions,
    bounds,
    w_out,
    residual,
    norm_gain,
    routes,
    gates,
    w_in,
    w_back,
):
    tok = queries.shape[0]
    home = residual.shape[0]
    hidden = w_back.shape[1]
    ctx_count = lax.axis_size("ctx")
    exp_count = lax.axis_size("exp")
    rank = lax.axis_index("exp")
    place = lax.axis_index("ctx")
    key_head, value_head = own_heads(queries, keys, values)
    block = (positions[0] // tok).astype(jnp.bfloat16)
    pair = jnp.concatenate([key_head, value_head], axis=1)
    payload = jnp.concatenate(
        [pair, jnp.full((PAD_ROWS, 2 * HEAD_DIM), block, jnp.bfloat16)], axis=0
    )
    same_rows = join_after(
        [payload] + [exchange(payload, "ctx", r, ctx_count) for r in range(2, ctx_count, 2)],
        payload,
    )
    same_keys = same_rows.reshape(ctx_count // 2, tok + PAD_ROWS, 2 * HEAD_DIM)
    other_keys = exchange(same_rows, "ctx", 1, ctx_count).reshape(same_keys.shape)
    places = place.astype(jnp.int32).reshape(1)
    flat_back = w_back.reshape(hidden, D)
    mine = shard_after(places, flat_back, D // ctx_count, same_rows)
    planes = [exchange(mine, "exp", s, exp_count) for s in range(1, exp_count)]

    parts = attend_project(
        rank.astype(jnp.int32).reshape(1),
        bounds.astype(jnp.float32).reshape(tok, 1),
        same_keys,
        other_keys,
        queries,
        residual,
        w_out,
        mine,
    )
    at_end = (rank == 0) | (rank == exp_count - 1)
    flags = jnp.stack([rank, at_end]).astype(jnp.int32)
    gain = norm_gain.reshape(1, D)
    flat_in = w_in.reshape(2 * hidden, D)
    count = len(parts)
    inward = [lax.ppermute(part, "exp", [(0, 1), (3, 2)]) for part in parts]
    near, across, total, outward = {}, {}, {}, {}
    homes, states, after = [], [], parts[0]
    for step, chunk in ORDER:
        if step == "near":
            after = near[chunk] = add_after(parts[chunk], inward[chunk], after)
            across[chunk] = lax.ppermute(near[chunk], "exp", [(1, 2), (2, 1)])
        elif step == "total":
            after = total[chunk] = add_after(near[chunk], across[chunk], after)
            outward[chunk] = lax.ppermute(total[chunk], "exp", [(1, 0), (2, 3)])
        else:
            own, *states = absorb(
                chunk, flags, total[chunk], outward[chunk], gain, flat_in, after, states
            )
            homes.append(own)
            after = states[0]
    planes = join_after(planes, near[0])
    from_x = exchange(planes, "ctx", 2, ctx_count)
    from_y = exchange(planes, "ctx", 4, ctx_count)
    upper = exchange(half_after(from_x, 0, homes[0]), "ctx", 4, ctx_count)
    lower = exchange(half_after(from_y, planes.shape[0] // 2, homes[0]), "ctx", 2, ctx_count)
    same_rows = join_after([planes, from_x, from_y, upper, lower], homes[2])
    same_back = same_rows.reshape(ctx_count // 2, planes.shape[0], planes.shape[1])
    other_back = exchange(same_rows, "ctx", 1, ctx_count).reshape(same_back.shape)
    middle_out = jnp.concatenate(homes, axis=1)
    activated = states[0]
    acts = [lax.dynamic_slice_in_dim(activated, rank * home, home, 0)]
    for offset in range(1, exp_count):
        leaving = lax.dynamic_slice_in_dim(activated, (rank ^ offset) * home, home, 0)
        acts.append(exchange(leaving, "exp", offset, exp_count))
    shares = gates / jnp.sum(gates, axis=1, keepdims=True)
    coefficient = jnp.sum(jnp.where(routes == 0, shares, 0.0), axis=1, keepdims=True)
    coefficient = coefficient.astype(jnp.bfloat16).astype(jnp.float32)
    expert_out = down(places, coefficient, acts, flat_back, same_back, other_back)
    return (middle_out, expert_out)


def largest_divisor(row_count):
    candidate = min(row_count, 1024)
    while row_count % candidate != 0:
        candidate = candidate - 1
    return candidate


def apply_slice(row_block, coefficient, w_in, w_back):
    hidden_here = w_back.shape[1]
    flat_in = w_in.reshape(2 * hidden_here, D)
    projected = lax.dot_general(
        row_block, flat_in, (((1,), (1,)), ((), ())), preferred_element_type=jnp.float32
    )
    activated = jax.nn.silu(projected[:, :hidden_here]) * projected[:, hidden_here:]
    blended = (coefficient.astype(jnp.float32) * activated).astype(jnp.bfloat16)
    flat_back = w_back.reshape(hidden_here, D)
    return jnp.dot(blended, flat_back, preferred_element_type=jnp.float32).astype(jnp.bfloat16)


def wide_device(
    queries,
    keys,
    values,
    positions,
    bounds,
    w_out,
    residual,
    norm_gain,
    routes,
    gates,
    w_in,
    w_back,
):
    tok_rows = queries.shape[0]
    head_cols = queries.shape[1]
    heads_here = head_cols // HEAD_DIM
    exp_count = lax.axis_size("exp")
    key_head, value_head = own_heads(queries, keys, values)
    query_heads = queries.reshape(tok_rows, heads_here, HEAD_DIM).transpose(1, 0, 2)
    scale = HEAD_DIM ** (-0.5)
    reach_max = jnp.max(bounds)
    all_keys, all_values, all_places = (
        lax.all_gather(key_head, "ctx", axis=0, tiled=True),
        lax.all_gather(value_head, "ctx", axis=0, tiled=True),
        lax.all_gather(positions, "ctx", axis=0, tiled=True),
    )
    total_rows = all_keys.shape[0]
    tile_len = largest_divisor(total_rows)
    tile_count = total_rows // tile_len

    def process(state_in, key_rows, value_rows, place_rows):
        row_max, row_sum, running = state_in
        scores = (
            jnp.einsum("htd,nd->htn", query_heads, key_rows, preferred_element_type=jnp.float32)
            * scale
        )
        visible = (place_rows[None, :] <= bounds[:, None])[None, :, :]
        masked = jnp.where(visible, scores, -1e30)
        new_max = jnp.maximum(row_max, jnp.max(masked, axis=2))
        weights = jnp.exp(masked - new_max[..., None])
        rescale = jnp.exp(row_max - new_max)
        row_sum = row_sum * rescale + jnp.sum(weights, axis=2)
        running = running * rescale[..., None] + jnp.einsum(
            "htn,nd->htd",
            weights.astype(jnp.bfloat16),
            value_rows,
            preferred_element_type=jnp.float32,
        )
        return (new_max, row_sum, running)

    def one_tile(tile_number, state_now):
        first = tile_number * tile_len
        key_rows = lax.dynamic_slice_in_dim(all_keys, first, tile_len, 0)
        value_rows = lax.dynamic_slice_in_dim(all_values, first, tile_len, 0)
        place_rows = lax.dynamic_slice_in_dim(all_places, first, tile_len, 0)
        return lax.cond(
            jnp.min(place_rows) <= reach_max,
            lambda state_in: process(state_in, key_rows, value_rows, place_rows),
            lambda state_in: state_in,
            state_now,
        )

    start_state = (
        jnp.full((heads_here, tok_rows), -1e30, jnp.float32),
        jnp.zeros((heads_here, tok_rows), jnp.float32),
        jnp.zeros((heads_here, tok_rows, HEAD_DIM), jnp.float32),
    )
    row_max, row_sum, running = lax.fori_loop(0, tile_count, one_tile, start_state)
    attended = (running / row_sum[..., None]).astype(jnp.bfloat16)
    attended = attended.transpose(1, 0, 2).reshape(tok_rows, head_cols)
    attention_rows = lax.psum_scatter(
        jnp.dot(attended, w_out, preferred_element_type=jnp.float32).astype(jnp.bfloat16),
        "exp",
        scatter_dimension=0,
        tiled=True,
    ).astype(jnp.float32)
    middle = (residual.astype(jnp.float32) + attention_rows).astype(jnp.bfloat16)
    wide = middle.astype(jnp.float32)
    mean_square = jnp.mean(wide * wide, axis=1, keepdims=True)
    normed = (wide * lax.rsqrt(mean_square + 1e-06) * norm_gain[None, :]).astype(jnp.bfloat16)
    local_rows = residual.shape[0]
    shares = gates / jnp.sum(gates, axis=1, keepdims=True)
    slice_expert = jnp.arange(exp_count, dtype=jnp.int32) // HID_SPLIT
    hits = routes[:, :, None] == slice_expert[None, None, :]
    coefficient = jnp.sum(jnp.where(hits, shares[:, :, None], 0.0), axis=1).astype(jnp.bfloat16)
    owner_weights = coefficient.transpose(1, 0)[:, :, None]
    copies = jnp.broadcast_to(normed[None, :, :], (exp_count, local_rows, D))
    row_block = lax.all_to_all(copies, "exp", split_axis=0, concat_axis=0, tiled=True)
    weight_block = lax.all_to_all(owner_weights, "exp", split_axis=0, concat_axis=0, tiled=True)
    slot_count = row_block.shape[1]
    produced = apply_slice(
        row_block.reshape(exp_count * slot_count, D),
        weight_block.reshape(exp_count * slot_count, 1),
        w_in,
        w_back,
    )
    produced = produced.reshape(exp_count, slot_count, D)
    arrived = lax.all_to_all(produced, "exp", split_axis=0, concat_axis=0, tiled=True)
    expert_out = jnp.sum(arrived.astype(jnp.float32), axis=0).astype(jnp.bfloat16)
    return (middle, expert_out)


def solution(mesh):
    in_specs = (
        P("ctx", "exp"),
        P("ctx", None),
        P("ctx", None),
        P("ctx"),
        P("ctx"),
        P("exp", None),
        P(("ctx", "exp"), None),
        P(),
        P(("ctx", "exp"), None),
        P(("ctx", "exp"), None),
        P("exp", None, None),
        P("exp", None, None),
    )
    out_specs = (P(("ctx", "exp"), None), P(("ctx", "exp"), None))
    one_line = mesh.shape["exp"] == HID_SPLIT and mesh.shape["ctx"] == 8
    return jax.shard_map(
        line_device if one_line else wide_device,
        mesh=mesh,
        in_specs=in_specs,
        out_specs=out_specs,
        check_vma=False,
    )
```

```python
import functools

import jax
import jax.numpy as jnp
from jax import lax
from jax.experimental import pallas as pl
from jax.experimental.pallas import tpu as pltpu
from jax.sharding import PartitionSpec as P

D = 4096
HEADS = 64
KV_HEADS = 4
HEAD_DIM = 128
HID_SPLIT = 4
STACK = 4
WIDTHS = (896, 896, 768, 768, 768)
SPANS = tuple((sum(WIDTHS[:i]), width) for i, width in enumerate(WIDTHS))
PAD_ROWS = 16
ORDER = (
    ("near", 0),
    ("near", 1),
    ("total", 0),
    ("near", 2),
    ("total", 1),
    ("near", 3),
    ("absorb", 0),
    ("near", 4),
    ("total", 2),
    ("absorb", 1),
    ("total", 3),
    ("total", 4),
    ("absorb", 2),
    ("absorb", 3),
    ("absorb", 4),
)
LOG2E = 1.4426950408889634
VMEM = pl.BlockSpec(memory_space=pltpu.VMEM)
ANY = pl.BlockSpec(memory_space=pl.ANY)
LIGHT = pl.CostEstimate(flops=1024, bytes_accessed=1024, transcendentals=0)


def exchange(value, axis, offset, size):
    return lax.ppermute(value, axis, [(i, i ^ offset) for i in range(size)])


def attend_kernel(rank_ref, bound_ref, same_ref, other_ref, q_hbm, resid_hbm, w_hbm, *refs):
    outs = refs[: len(WIDTHS)]
    q_ref, resid_ref, w_buf, k_buf, v_buf, bias, attended, acc, sems, side = refs[len(WIDTHS) :]
    tok = q_ref.shape[0]
    heads = q_ref.shape[1] // HEAD_DIM
    q_copy = pltpu.make_async_copy(q_hbm, q_ref, side.at[0])
    q_copy.start()
    resid_copy = pltpu.make_async_copy(resid_hbm, resid_ref, side.at[1])
    resid_copy.start()
    copies = []
    for chunk, (first, width) in enumerate(SPANS):
        span = pl.ds(first, width)
        copy = pltpu.make_async_copy(w_hbm.at[:, span], w_buf.at[:, span], sems.at[chunk])
        copy.start()
        copies.append(copy)
    bound = bound_ref[...]
    lane = lax.broadcasted_iota(jnp.int32, (1, tok), 1).astype(jnp.float32)
    ones = jnp.ones((tok, HEAD_DIM), jnp.bfloat16)
    half_count = same_ref.shape[0]
    for b in range(2 * half_count):
        rows = slice(b * tok, (b + 1) * tok)
        group, row = (same_ref, b) if b < half_count else (other_ref, b - half_count)
        k_buf[rows, :] = group[row, :tok, :HEAD_DIM]
        v_buf[rows, :HEAD_DIM] = group[row, :tok, HEAD_DIM:]
        v_buf[rows, HEAD_DIM:] = ones
        start = group[row, tok : tok + PAD_ROWS, :HEAD_DIM].astype(jnp.float32)[:1]
        place = start * tok + lane
        bias[:, rows] = jnp.where(place <= bound, 0.0, -1e30)
    factor = HEAD_DIM ** (-0.5) * LOG2E
    q_copy.wait()

    def some_heads(step, carry):
        base = step * STACK * HEAD_DIM
        parts = []
        for j in range(STACK):
            start = pl.multiple_of(base + j * HEAD_DIM, HEAD_DIM)
            parts.append(q_ref[:, pl.ds(start, HEAD_DIM)])
        stacked = jnp.concatenate(parts, axis=0)
        scores = lax.dot_general(
            stacked, k_buf[...], (((1,), (1,)), ((), ())), preferred_element_type=jnp.float32
        )
        scores = scores.reshape(STACK, tok, -1) * factor + bias[...][None]
        row_max = jnp.max(scores, axis=2, keepdims=True)
        weights = jnp.exp2(scores - row_max).astype(jnp.bfloat16)
        summed = jnp.dot(
            weights.reshape(STACK * tok, -1), v_buf[...], preferred_element_type=jnp.float32
        )
        result = (summed[:, :HEAD_DIM] / summed[:, HEAD_DIM:]).astype(jnp.bfloat16)
        for j in range(STACK):
            start = pl.multiple_of(base + j * HEAD_DIM, HEAD_DIM)
            attended[:, pl.ds(start, HEAD_DIM)] = result[j * tok : (j + 1) * tok]
        return carry

    lax.fori_loop(0, heads // STACK, some_heads, 0)
    resid_copy.wait()
    home = resid_ref.shape[0]
    top = pl.multiple_of(rank_ref[0] * home, home)
    for chunk, (first, width) in enumerate(SPANS):
        copies[chunk].wait()
        span = slice(first, first + width)
        acc[:, span] = jnp.dot(
            attended[...], w_buf[:, span], preferred_element_type=jnp.float32
        )
        acc[pl.ds(top, home), span] += resid_ref[:, span].astype(jnp.float32)
        outs[chunk][...] = acc[:, span].astype(jnp.bfloat16)


def attend_project(rank, bounds, same, other, queries, residual, w_out):
    tok, width = queries.shape
    keys_in_all = 2 * same.shape[0] * tok
    return pl.pallas_call(
        attend_kernel,
        out_shape=[jax.ShapeDtypeStruct((tok, w), jnp.bfloat16) for w in WIDTHS],
        in_specs=[pl.BlockSpec(memory_space=pltpu.SMEM)] + [VMEM] * 3 + [ANY] * 3,
        out_specs=[VMEM] * len(WIDTHS),
        scratch_shapes=[
            pltpu.VMEM(queries.shape, jnp.bfloat16),
            pltpu.VMEM(residual.shape, jnp.bfloat16),
            pltpu.VMEM((width, D), jnp.bfloat16),
            pltpu.VMEM((keys_in_all, HEAD_DIM), jnp.bfloat16),
            pltpu.VMEM((keys_in_all, 2 * HEAD_DIM), jnp.bfloat16),
            pltpu.VMEM((tok, keys_in_all), jnp.float32),
            pltpu.VMEM((tok, width), jnp.bfloat16),
            pltpu.VMEM((tok, D), jnp.float32),
            pltpu.SemaphoreType.DMA((len(WIDTHS),)),
            pltpu.SemaphoreType.DMA((2,)),
        ],
        compiler_params=pltpu.CompilerParams(vmem_limit_bytes=40 * 1024 * 1024),
        cost_estimate=LIGHT,
        name="attend_project",
    )(rank, bounds, same, other, queries, residual, w_out)


def down_kernel(rank_ref, coef_ref, a0, a1, a2, a3, back_ref, out_ref):
    count, _, width = back_ref.shape
    coef = coef_ref[...]
    blended = [(a[...].astype(jnp.float32) * coef).astype(jnp.bfloat16) for a in (a0, a1, a2, a3)]
    hidden = blended[0].shape[1]
    for block in range(count):
        total = None
        for s in range(len(blended)):
            rows = pl.ds(pl.multiple_of((rank_ref[0] ^ s) * hidden, hidden), hidden)
            term = jnp.dot(
                blended[s], back_ref[block, rows, :], preferred_element_type=jnp.float32
            )
            total = term if total is None else total + term
        out_ref[:, block * width : (block + 1) * width] = total.astype(jnp.bfloat16)


def down(rank, coefficient, acts, back):
    rows = acts[0].shape[0]
    return pl.pallas_call(
        down_kernel,
        out_shape=jax.ShapeDtypeStruct((rows, D), jnp.bfloat16),
        in_specs=[pl.BlockSpec(memory_space=pltpu.SMEM)] + [VMEM] * 6,
        out_specs=VMEM,
        compiler_params=pltpu.CompilerParams(vmem_limit_bytes=12 * 1024 * 1024),
        cost_estimate=LIGHT,
        name="down",
    )(rank, coefficient, *acts, back)


def join_kernel(*refs):
    out_ref = refs[-1]
    first = 0
    for piece in refs[1:-1]:
        rows = piece.shape[0]
        out_ref[first : first + rows, :] = piece[...]
        first += rows


def join_after(pieces, after):
    rows = sum(piece.shape[0] for piece in pieces)
    width = pieces[0].shape[1]
    return pl.pallas_call(
        join_kernel,
        out_shape=jax.ShapeDtypeStruct((rows, width), jnp.bfloat16),
        in_specs=[ANY] + [VMEM] * len(pieces),
        out_specs=VMEM,
        compiler_params=pltpu.CompilerParams(vmem_limit_bytes=8 * 1024 * 1024),
        cost_estimate=LIGHT,
        name="join_after",
    )(after, *pieces)


def add_kernel(a_ref, b_ref, after_ref, out_ref):
    out_ref[...] = (a_ref[...].astype(jnp.float32) + b_ref[...].astype(jnp.float32)).astype(
        jnp.bfloat16
    )


def add_after(left, right, after):
    return pl.pallas_call(
        add_kernel,
        out_shape=jax.ShapeDtypeStruct(left.shape, jnp.bfloat16),
        in_specs=[VMEM, VMEM, ANY],
        out_specs=VMEM,
        compiler_params=pltpu.CompilerParams(vmem_limit_bytes=4 * 1024 * 1024),
        cost_estimate=LIGHT,
        name="add_after",
    )(left, right, after)


def absorb_kernel(chunk, flag_ref, total_ref, outward_ref, gain_ref, w_ref, *refs):
    last = chunk == len(WIDTHS) - 1
    states = refs[1 : 1 if chunk == 0 else 3]
    outs = refs[1 + len(states) : -1]
    scratch = refs[-1]
    first, width = SPANS[chunk]
    span = slice(first, first + width)
    middle = jnp.where(flag_ref[1] == 1, outward_ref[...], total_ref[...])
    scratch[...] = middle
    home_ref = outs[0]
    home = home_ref.shape[0]
    top = pl.multiple_of(flag_ref[0] * home, home)
    home_ref[...] = scratch[pl.ds(top, home), :]
    wide = middle.astype(jnp.float32)
    gained = (wide * gain_ref[:, span]).astype(jnp.bfloat16)
    product = lax.dot_general(
        gained, w_ref[:, span], (((1,), (1,)), ((), ())), preferred_element_type=jnp.float32
    )
    square = sum(
        wide[:, i * 128 : (i + 1) * 128] * wide[:, i * 128 : (i + 1) * 128]
        for i in range(width // 128)
    )
    if chunk > 0:
        product += states[0][...]
        square += states[1][...]
    if last:
        hidden = product.shape[1] // 2
        mean_square = jnp.sum(square, axis=1, keepdims=True) / D
        product = product * lax.rsqrt(mean_square + 1e-06)
        gate = product[:, :hidden]
        act = gate / (1.0 + jnp.exp(-gate)) * product[:, hidden:]
        outs[1][...] = act.astype(jnp.bfloat16)
    else:
        outs[1][...] = product
        outs[2][...] = square


def absorb(chunk, flags, total, outward, gain, w_in, after, states):
    tok, width = total.shape
    rows = w_in.shape[0]
    home = jax.ShapeDtypeStruct((tok // lax.axis_size("exp"), width), jnp.bfloat16)
    if chunk == len(WIDTHS) - 1:
        out_shape = [home, jax.ShapeDtypeStruct((tok, rows // 2), jnp.bfloat16)]
    else:
        out_shape = [
            home,
            jax.ShapeDtypeStruct((tok, rows), jnp.float32),
            jax.ShapeDtypeStruct((tok, 128), jnp.float32),
        ]
    return pl.pallas_call(
        functools.partial(absorb_kernel, chunk),
        out_shape=out_shape,
        in_specs=[pl.BlockSpec(memory_space=pltpu.SMEM)]
        + [VMEM] * 4
        + [ANY]
        + [VMEM] * len(states),
        out_specs=[VMEM] * len(out_shape),
        scratch_shapes=[pltpu.VMEM((tok, width), jnp.bfloat16)],
        compiler_params=pltpu.CompilerParams(vmem_limit_bytes=12 * 1024 * 1024),
        cost_estimate=LIGHT,
        name="absorb",
    )(flags, total, outward, gain, w_in, after, *states)


def own_heads(queries, keys, values):
    heads_here = queries.shape[1] // HEAD_DIM
    kv_number = lax.axis_index("exp") * heads_here // (HEADS // KV_HEADS)
    key_head = lax.dynamic_slice_in_dim(keys, kv_number * HEAD_DIM, HEAD_DIM, 1)
    value_head = lax.dynamic_slice_in_dim(values, kv_number * HEAD_DIM, HEAD_DIM, 1)
    return key_head, value_head


def line_device(
    queries,
    keys,
    values,
    positions,
    bounds,
    w_out,
    residual,
    norm_gain,
    routes,
    gates,
    w_in,
    w_back,
):
    tok = queries.shape[0]
    home = residual.shape[0]
    hidden = w_back.shape[1]
    ctx_count = lax.axis_size("ctx")
    exp_count = lax.axis_size("exp")
    rank = lax.axis_index("exp")
    place = lax.axis_index("ctx")
    key_head, value_head = own_heads(queries, keys, values)
    block = (positions[0] // tok).astype(jnp.bfloat16)
    pair = jnp.concatenate([key_head, value_head], axis=1)
    payload = jnp.concatenate(
        [pair, jnp.full((PAD_ROWS, 2 * HEAD_DIM), block, jnp.bfloat16)], axis=0
    )
    same_rows = join_after(
        [payload] + [exchange(payload, "ctx", r, ctx_count) for r in range(2, ctx_count, 2)],
        payload,
    )
    same_keys = same_rows.reshape(ctx_count // 2, tok + PAD_ROWS, 2 * HEAD_DIM)
    other_keys = exchange(same_rows, "ctx", 1, ctx_count).reshape(same_keys.shape)
    flat_back = w_back.reshape(hidden, D)
    mine = lax.dynamic_slice_in_dim(flat_back, place * (D // ctx_count), D // ctx_count, 1)
    all_back = lax.all_gather(mine, ("ctx", "exp"), axis=0, tiled=True)
    all_back = all_back.reshape(ctx_count, exp_count * hidden, D // ctx_count)

    parts = attend_project(
        rank.astype(jnp.int32).reshape(1),
        bounds.astype(jnp.float32).reshape(tok, 1),
        same_keys,
        other_keys,
        queries,
        residual,
        w_out,
    )
    at_end = (rank == 0) | (rank == exp_count - 1)
    flags = jnp.stack([rank, at_end]).astype(jnp.int32)
    gain = norm_gain.reshape(1, D)
    flat_in = w_in.reshape(2 * hidden, D)
    count = len(parts)
    inward = [lax.ppermute(part, "exp", [(0, 1), (3, 2)]) for part in parts]
    near, across, total, outward = {}, {}, {}, {}
    homes, states, after = [], [], parts[0]
    for step, chunk in ORDER:
        if step == "near":
            after = near[chunk] = add_after(parts[chunk], inward[chunk], after)
            across[chunk] = lax.ppermute(near[chunk], "exp", [(1, 2), (2, 1)])
        elif step == "total":
            after = total[chunk] = add_after(near[chunk], across[chunk], after)
            outward[chunk] = lax.ppermute(total[chunk], "exp", [(1, 0), (2, 3)])
        else:
            own, *states = absorb(
                chunk, flags, total[chunk], outward[chunk], gain, flat_in, after, states
            )
            homes.append(own)
            after = states[0]
    middle_out = jnp.concatenate(homes, axis=1)
    activated = states[0]
    acts = [lax.dynamic_slice_in_dim(activated, rank * home, home, 0)]
    for offset in range(1, exp_count):
        leaving = lax.dynamic_slice_in_dim(activated, (rank ^ offset) * home, home, 0)
        acts.append(exchange(leaving, "exp", offset, exp_count))
    shares = gates / jnp.sum(gates, axis=1, keepdims=True)
    coefficient = jnp.sum(jnp.where(routes == 0, shares, 0.0), axis=1, keepdims=True)
    coefficient = coefficient.astype(jnp.bfloat16).astype(jnp.float32)
    expert_out = down(flags, coefficient, acts, all_back)
    return (middle_out, expert_out)


def largest_divisor(row_count):
    candidate = min(row_count, 1024)
    while row_count % candidate != 0:
        candidate = candidate - 1
    return candidate


def apply_slice(row_block, coefficient, w_in, w_back):
    hidden_here = w_back.shape[1]
    flat_in = w_in.reshape(2 * hidden_here, D)
    projected = lax.dot_general(
        row_block, flat_in, (((1,), (1,)), ((), ())), preferred_element_type=jnp.float32
    )
    activated = jax.nn.silu(projected[:, :hidden_here]) * projected[:, hidden_here:]
    blended = (coefficient.astype(jnp.float32) * activated).astype(jnp.bfloat16)
    flat_back = w_back.reshape(hidden_here, D)
    return jnp.dot(blended, flat_back, preferred_element_type=jnp.float32).astype(jnp.bfloat16)


def wide_device(
    queries,
    keys,
    values,
    positions,
    bounds,
    w_out,
    residual,
    norm_gain,
    routes,
    gates,
    w_in,
    w_back,
):
    tok_rows = queries.shape[0]
    head_cols = queries.shape[1]
    heads_here = head_cols // HEAD_DIM
    exp_count = lax.axis_size("exp")
    key_head, value_head = own_heads(queries, keys, values)
    query_heads = queries.reshape(tok_rows, heads_here, HEAD_DIM).transpose(1, 0, 2)
    scale = HEAD_DIM ** (-0.5)
    reach_max = jnp.max(bounds)
    all_keys, all_values, all_places = (
        lax.all_gather(key_head, "ctx", axis=0, tiled=True),
        lax.all_gather(value_head, "ctx", axis=0, tiled=True),
        lax.all_gather(positions, "ctx", axis=0, tiled=True),
    )
    total_rows = all_keys.shape[0]
    tile_len = largest_divisor(total_rows)
    tile_count = total_rows // tile_len

    def process(state_in, key_rows, value_rows, place_rows):
        row_max, row_sum, running = state_in
        scores = (
            jnp.einsum("htd,nd->htn", query_heads, key_rows, preferred_element_type=jnp.float32)
            * scale
        )
        visible = (place_rows[None, :] <= bounds[:, None])[None, :, :]
        masked = jnp.where(visible, scores, -1e30)
        new_max = jnp.maximum(row_max, jnp.max(masked, axis=2))
        weights = jnp.exp(masked - new_max[..., None])
        rescale = jnp.exp(row_max - new_max)
        row_sum = row_sum * rescale + jnp.sum(weights, axis=2)
        running = running * rescale[..., None] + jnp.einsum(
            "htn,nd->htd",
            weights.astype(jnp.bfloat16),
            value_rows,
            preferred_element_type=jnp.float32,
        )
        return (new_max, row_sum, running)

    def one_tile(tile_number, state_now):
        first = tile_number * tile_len
        key_rows = lax.dynamic_slice_in_dim(all_keys, first, tile_len, 0)
        value_rows = lax.dynamic_slice_in_dim(all_values, first, tile_len, 0)
        place_rows = lax.dynamic_slice_in_dim(all_places, first, tile_len, 0)
        return lax.cond(
            jnp.min(place_rows) <= reach_max,
            lambda state_in: process(state_in, key_rows, value_rows, place_rows),
            lambda state_in: state_in,
            state_now,
        )

    start_state = (
        jnp.full((heads_here, tok_rows), -1e30, jnp.float32),
        jnp.zeros((heads_here, tok_rows), jnp.float32),
        jnp.zeros((heads_here, tok_rows, HEAD_DIM), jnp.float32),
    )
    row_max, row_sum, running = lax.fori_loop(0, tile_count, one_tile, start_state)
    attended = (running / row_sum[..., None]).astype(jnp.bfloat16)
    attended = attended.transpose(1, 0, 2).reshape(tok_rows, head_cols)
    attention_rows = lax.psum_scatter(
        jnp.dot(attended, w_out, preferred_element_type=jnp.float32).astype(jnp.bfloat16),
        "exp",
        scatter_dimension=0,
        tiled=True,
    ).astype(jnp.float32)
    middle = (residual.astype(jnp.float32) + attention_rows).astype(jnp.bfloat16)
    wide = middle.astype(jnp.float32)
    mean_square = jnp.mean(wide * wide, axis=1, keepdims=True)
    normed = (wide * lax.rsqrt(mean_square + 1e-06) * norm_gain[None, :]).astype(jnp.bfloat16)
    local_rows = residual.shape[0]
    shares = gates / jnp.sum(gates, axis=1, keepdims=True)
    slice_expert = jnp.arange(exp_count, dtype=jnp.int32) // HID_SPLIT
    hits = routes[:, :, None] == slice_expert[None, None, :]
    coefficient = jnp.sum(jnp.where(hits, shares[:, :, None], 0.0), axis=1).astype(jnp.bfloat16)
    owner_weights = coefficient.transpose(1, 0)[:, :, None]
    copies = jnp.broadcast_to(normed[None, :, :], (exp_count, local_rows, D))
    row_block = lax.all_to_all(copies, "exp", split_axis=0, concat_axis=0, tiled=True)
    weight_block = lax.all_to_all(owner_weights, "exp", split_axis=0, concat_axis=0, tiled=True)
    slot_count = row_block.shape[1]
    produced = apply_slice(
        row_block.reshape(exp_count * slot_count, D),
        weight_block.reshape(exp_count * slot_count, 1),
        w_in,
        w_back,
    )
    produced = produced.reshape(exp_count, slot_count, D)
    arrived = lax.all_to_all(produced, "exp", split_axis=0, concat_axis=0, tiled=True)
    expert_out = jnp.sum(arrived.astype(jnp.float32), axis=0).astype(jnp.bfloat16)
    return (middle, expert_out)


def solution(mesh):
    in_specs = (
        P("ctx", "exp"),
        P("ctx", None),
        P("ctx", None),
        P("ctx"),
        P("ctx"),
        P("exp", None),
        P(("ctx", "exp"), None),
        P(),
        P(("ctx", "exp"), None),
        P(("ctx", "exp"), None),
        P("exp", None, None),
        P("exp", None, None),
    )
    out_specs = (P(("ctx", "exp"), None), P(("ctx", "exp"), None))
    one_line = mesh.shape["exp"] == HID_SPLIT and mesh.shape["ctx"] == 8
    return jax.shard_map(
        line_device if one_line else wide_device,
        mesh=mesh,
        in_specs=in_specs,
        out_specs=out_specs,
        check_vma=False,
    )
```

```python
import functools

import jax
import jax.numpy as jnp
from jax import lax
from jax.experimental import pallas as pl
from jax.experimental.pallas import tpu as pltpu
from jax.sharding import PartitionSpec as P

D = 4096
HEADS = 64
KV_HEADS = 4
HEAD_DIM = 128
HID_SPLIT = 4
STACK = 4
WIDTHS = (896, 896, 768, 768, 768)
SPANS = tuple((sum(WIDTHS[:i]), width) for i, width in enumerate(WIDTHS))
PAD_ROWS = 16
ROW_ORDER = (0, 2, 1, 3)
SHARE_WIDTHS = (1792, 2304)
ORDER = (
    ("near", 0),
    ("near", 1),
    ("total", 0),
    ("near", 2),
    ("total", 1),
    ("near", 3),
    ("absorb", 0),
    ("near", 4),
    ("total", 2),
    ("absorb", 1),
    ("total", 3),
    ("total", 4),
    ("absorb", 2),
    ("absorb", 3),
    ("absorb", 4),
)
LOG2E = 1.4426950408889634
VMEM = pl.BlockSpec(memory_space=pltpu.VMEM)
ANY = pl.BlockSpec(memory_space=pl.ANY)
LIGHT = pl.CostEstimate(flops=1024, bytes_accessed=1024, transcendentals=0)


def exchange(value, axis, offset, size):
    return lax.ppermute(value, axis, [(i, i ^ offset) for i in range(size)])


def attend_kernel(rank_ref, bound_ref, same_ref, other_ref, q_hbm, resid_hbm, w_hbm, *refs):
    outs = refs[: len(WIDTHS)]
    q_ref, resid_ref, w_buf, k_buf, v_buf, bias, attended, acc, sems, side = refs[len(WIDTHS) :]
    tok = q_ref.shape[0]
    heads = q_ref.shape[1] // HEAD_DIM
    q_copy = pltpu.make_async_copy(q_hbm, q_ref, side.at[0])
    q_copy.start()
    resid_copy = pltpu.make_async_copy(resid_hbm, resid_ref, side.at[1])
    resid_copy.start()
    copies = []
    for chunk, (first, width) in enumerate(SPANS):
        span = pl.ds(first, width)
        copy = pltpu.make_async_copy(w_hbm.at[:, span], w_buf.at[:, span], sems.at[chunk])
        copy.start()
        copies.append(copy)
    bound = jnp.broadcast_to(bound_ref[...].astype(jnp.float32), (tok, tok)).T
    lane = lax.broadcasted_iota(jnp.int32, (1, tok), 1).astype(jnp.float32)
    ones = jnp.ones((tok, HEAD_DIM), jnp.bfloat16)
    half_count = same_ref.shape[0]
    for b in range(2 * half_count):
        rows = slice(b * tok, (b + 1) * tok)
        group, row = (same_ref, b) if b < half_count else (other_ref, b - half_count)
        k_buf[rows, :] = group[row, :tok, :HEAD_DIM]
        v_buf[rows, :HEAD_DIM] = group[row, :tok, HEAD_DIM:]
        v_buf[rows, HEAD_DIM:] = ones
        start = group[row, tok : tok + PAD_ROWS, :HEAD_DIM].astype(jnp.float32)[:1]
        place = start * tok + lane
        bias[:, rows] = jnp.where(place <= bound, 0.0, -1e30)
    factor = HEAD_DIM ** (-0.5) * LOG2E
    q_copy.wait()

    def some_heads(step, carry):
        base = step * STACK * HEAD_DIM
        parts = []
        for j in range(STACK):
            start = pl.multiple_of(base + j * HEAD_DIM, HEAD_DIM)
            parts.append(q_ref[:, pl.ds(start, HEAD_DIM)])
        stacked = jnp.concatenate(parts, axis=0)
        scores = lax.dot_general(
            stacked, k_buf[...], (((1,), (1,)), ((), ())), preferred_element_type=jnp.float32
        )
        scores = scores.reshape(STACK, tok, -1) * factor + bias[...][None]
        row_max = jnp.max(scores, axis=2, keepdims=True)
        weights = jnp.exp2(scores - row_max).astype(jnp.bfloat16)
        summed = jnp.dot(
            weights.reshape(STACK * tok, -1), v_buf[...], preferred_element_type=jnp.float32
        )
        result = (summed[:, :HEAD_DIM] / summed[:, HEAD_DIM:]).astype(jnp.bfloat16)
        for j in range(STACK):
            start = pl.multiple_of(base + j * HEAD_DIM, HEAD_DIM)
            attended[:, pl.ds(start, HEAD_DIM)] = result[j * tok : (j + 1) * tok]
        return carry

    lax.fori_loop(0, heads // STACK, some_heads, 0, unroll=True)
    resid_copy.wait()
    home = resid_ref.shape[0]
    top = pl.multiple_of(rank_ref[0] * home, home)
    for chunk, (first, width) in enumerate(SPANS):
        copies[chunk].wait()
        span = slice(first, first + width)
        acc[:, span] = jnp.dot(
            attended[...], w_buf[:, span], preferred_element_type=jnp.float32
        )
        acc[pl.ds(top, home), span] += resid_ref[:, span].astype(jnp.float32)
        outs[chunk][...] = acc[:, span].astype(jnp.bfloat16)


def attend_project(rank, bounds, same, other, queries, residual, w_out):
    tok, width = queries.shape
    keys_in_all = 2 * same.shape[0] * tok
    return pl.pallas_call(
        attend_kernel,
        out_shape=[jax.ShapeDtypeStruct((tok, w), jnp.bfloat16) for w in WIDTHS],
        in_specs=[pl.BlockSpec(memory_space=pltpu.SMEM)] + [VMEM] * 3 + [ANY] * 3,
        out_specs=[VMEM] * len(WIDTHS),
        scratch_shapes=[
            pltpu.VMEM(queries.shape, jnp.bfloat16),
            pltpu.VMEM(residual.shape, jnp.bfloat16),
            pltpu.VMEM((width, D), jnp.bfloat16),
            pltpu.VMEM((keys_in_all, HEAD_DIM), jnp.bfloat16),
            pltpu.VMEM((keys_in_all, 2 * HEAD_DIM), jnp.bfloat16),
            pltpu.VMEM((tok, keys_in_all), jnp.float32),
            pltpu.VMEM((tok, width), jnp.bfloat16),
            pltpu.VMEM((tok, D), jnp.float32),
            pltpu.SemaphoreType.DMA((len(WIDTHS),)),
            pltpu.SemaphoreType.DMA((2,)),
        ],
        compiler_params=pltpu.CompilerParams(vmem_limit_bytes=52 * 1024 * 1024),
        cost_estimate=LIGHT,
        name="attend_project",
    )(rank, bounds, same, other, queries, residual, w_out)


def share_kernel(act_ref, back_ref, *outs):
    half = act_ref.shape[0] // 2
    first = 0
    for i, width in enumerate(SHARE_WIDTHS):
        product = jnp.dot(
            act_ref[...], back_ref[:, first : first + width], preferred_element_type=jnp.float32
        )
        outs[2 * i][...] = product[:half].astype(jnp.bfloat16)
        outs[2 * i + 1][...] = product[half:].astype(jnp.bfloat16)
        first += width


def make_shares(act, back):
    shapes = [
        jax.ShapeDtypeStruct((act.shape[0] // 2, width), jnp.bfloat16)
        for width in SHARE_WIDTHS
        for _ in range(2)
    ]
    return pl.pallas_call(
        share_kernel,
        out_shape=shapes,
        in_specs=[VMEM, VMEM],
        out_specs=[VMEM] * len(shapes),
        compiler_params=pltpu.CompilerParams(vmem_limit_bytes=12 * 1024 * 1024),
        cost_estimate=LIGHT,
        name="make_shares",
    )(act, back)


def pair_kernel(kept_ref, arrived_ref, after_ref, own_ref, leaving_ref):
    rows = own_ref.shape[0]
    total = kept_ref[...].astype(jnp.float32) + arrived_ref[...].astype(jnp.float32)
    own_ref[...] = total[:rows]
    leaving_ref[...] = total[rows:].astype(jnp.bfloat16)


def pair_sum(kept, arrived, after):
    shape = (kept.shape[0] // 2, kept.shape[1])
    return pl.pallas_call(
        pair_kernel,
        out_shape=[
            jax.ShapeDtypeStruct(shape, jnp.float32),
            jax.ShapeDtypeStruct(shape, jnp.bfloat16),
        ],
        in_specs=[VMEM, VMEM, ANY],
        out_specs=[VMEM, VMEM],
        compiler_params=pltpu.CompilerParams(vmem_limit_bytes=4 * 1024 * 1024),
        cost_estimate=LIGHT,
        name="pair_sum",
    )(kept, arrived, after)


def last_kernel(coef_ref, own_ref, arrived_ref, *refs):
    out_ref = refs[-1]
    first = 0
    if len(refs) > 1:
        first = refs[0].shape[1]
        out_ref[:, :first] = refs[0][...]
    total = own_ref[...] + arrived_ref[...].astype(jnp.float32)
    out_ref[:, first:] = (total * coef_ref[...]).astype(jnp.bfloat16)


def last_sum(coefficient, own, arrived, earlier):
    rows, width = own.shape
    width += sum(piece.shape[1] for piece in earlier)
    return pl.pallas_call(
        last_kernel,
        out_shape=jax.ShapeDtypeStruct((rows, width), jnp.bfloat16),
        in_specs=[VMEM] * (3 + len(earlier)),
        out_specs=VMEM,
        compiler_params=pltpu.CompilerParams(vmem_limit_bytes=4 * 1024 * 1024),
        cost_estimate=LIGHT,
        name="last_sum",
    )(coefficient, own, arrived, *earlier)


def join_kernel(*refs):
    out_ref = refs[-1]
    first = 0
    for piece in refs[1:-1]:
        rows = piece.shape[0]
        out_ref[first : first + rows, :] = piece[...]
        first += rows


def join_after(pieces, after):
    rows = sum(piece.shape[0] for piece in pieces)
    width = pieces[0].shape[1]
    return pl.pallas_call(
        join_kernel,
        out_shape=jax.ShapeDtypeStruct((rows, width), jnp.bfloat16),
        in_specs=[ANY] + [VMEM] * len(pieces),
        out_specs=VMEM,
        compiler_params=pltpu.CompilerParams(vmem_limit_bytes=8 * 1024 * 1024),
        cost_estimate=LIGHT,
        name="join_after",
    )(after, *pieces)


def add_kernel(a_ref, b_ref, after_ref, out_ref):
    out_ref[...] = (a_ref[...].astype(jnp.float32) + b_ref[...].astype(jnp.float32)).astype(
        jnp.bfloat16
    )


def add_after(left, right, after):
    return pl.pallas_call(
        add_kernel,
        out_shape=jax.ShapeDtypeStruct(left.shape, jnp.bfloat16),
        in_specs=[VMEM, VMEM, ANY],
        out_specs=VMEM,
        compiler_params=pltpu.CompilerParams(vmem_limit_bytes=4 * 1024 * 1024),
        cost_estimate=LIGHT,
        name="add_after",
    )(left, right, after)


def absorb_kernel(chunk, flag_ref, total_ref, outward_ref, gain_ref, w_ref, *refs):
    last = chunk == len(WIDTHS) - 1
    states = refs[1 : 1 if chunk == 0 else 3]
    outs = refs[1 + len(states) : -2]
    scratch, order_buf = refs[-2:]
    first, width = SPANS[chunk]
    span = slice(first, first + width)
    middle = jnp.where(flag_ref[1] == 1, outward_ref[...], total_ref[...])
    scratch[...] = middle
    home_ref = outs[0]
    home = home_ref.shape[0]
    top = pl.multiple_of(flag_ref[0] * home, home)
    home_ref[...] = scratch[pl.ds(top, home), :]
    wide = middle.astype(jnp.float32)
    gained = (wide * gain_ref[:, span]).astype(jnp.bfloat16)
    product = lax.dot_general(
        gained, w_ref[:, span], (((1,), (1,)), ((), ())), preferred_element_type=jnp.float32
    )
    square = sum(
        wide[:, i * 128 : (i + 1) * 128] * wide[:, i * 128 : (i + 1) * 128]
        for i in range(width // 128)
    )
    if chunk > 0:
        product += states[0][...]
        square += states[1][...]
    if last:
        hidden = product.shape[1] // 2
        mean_square = jnp.sum(square, axis=1, keepdims=True) / D
        product = product * lax.rsqrt(mean_square + 1e-06)
        gate = product[:, :hidden]
        act = gate / (1.0 + jnp.exp(-gate)) * product[:, hidden:]
        rows = home_ref.shape[0]
        order_buf[...] = act
        for i, offset in enumerate(ROW_ORDER):
            source = pl.multiple_of((flag_ref[0] ^ offset) * rows, rows)
            outs[1][i * rows : (i + 1) * rows, :] = order_buf[pl.ds(source, rows), :].astype(
                jnp.bfloat16
            )
    else:
        outs[1][...] = product
        outs[2][...] = square


def absorb(chunk, flags, total, outward, gain, w_in, after, states):
    tok, width = total.shape
    rows = w_in.shape[0]
    home = jax.ShapeDtypeStruct((tok // lax.axis_size("exp"), width), jnp.bfloat16)
    if chunk == len(WIDTHS) - 1:
        out_shape = [home, jax.ShapeDtypeStruct((tok, rows // 2), jnp.bfloat16)]
    else:
        out_shape = [
            home,
            jax.ShapeDtypeStruct((tok, rows), jnp.float32),
            jax.ShapeDtypeStruct((tok, 128), jnp.float32),
        ]
    return pl.pallas_call(
        functools.partial(absorb_kernel, chunk),
        out_shape=out_shape,
        in_specs=[pl.BlockSpec(memory_space=pltpu.SMEM)]
        + [VMEM] * 4
        + [ANY]
        + [VMEM] * len(states),
        out_specs=[VMEM] * len(out_shape),
        scratch_shapes=[
            pltpu.VMEM((tok, width), jnp.bfloat16),
            pltpu.VMEM((tok, rows // 2), jnp.float32),
        ],
        compiler_params=pltpu.CompilerParams(vmem_limit_bytes=12 * 1024 * 1024),
        cost_estimate=LIGHT,
        name="absorb",
    )(flags, total, outward, gain, w_in, after, *states)


def own_heads(queries, keys, values):
    heads_here = queries.shape[1] // HEAD_DIM
    kv_number = lax.axis_index("exp") * heads_here // (HEADS // KV_HEADS)
    key_head = lax.dynamic_slice_in_dim(keys, kv_number * HEAD_DIM, HEAD_DIM, 1)
    value_head = lax.dynamic_slice_in_dim(values, kv_number * HEAD_DIM, HEAD_DIM, 1)
    return key_head, value_head


def line_device(
    queries,
    keys,
    values,
    positions,
    bounds,
    w_out,
    residual,
    norm_gain,
    routes,
    gates,
    w_in,
    w_back,
):
    tok = queries.shape[0]
    home = residual.shape[0]
    hidden = w_back.shape[1]
    ctx_count = lax.axis_size("ctx")
    exp_count = lax.axis_size("exp")
    rank = lax.axis_index("exp")
    key_head, value_head = own_heads(queries, keys, values)
    block = (positions[0] // tok).astype(jnp.bfloat16)
    pair = jnp.concatenate([key_head, value_head], axis=1)
    payload = jnp.concatenate(
        [pair, jnp.full((PAD_ROWS, 2 * HEAD_DIM), block, jnp.bfloat16)], axis=0
    )
    same_rows = join_after(
        [payload] + [exchange(payload, "ctx", r, ctx_count) for r in range(2, ctx_count, 2)],
        payload,
    )
    same_keys = same_rows.reshape(ctx_count // 2, tok + PAD_ROWS, 2 * HEAD_DIM)
    other_keys = exchange(same_rows, "ctx", 1, ctx_count).reshape(same_keys.shape)
    parts = attend_project(
        rank.astype(jnp.int32).reshape(1),
        bounds.reshape(1, tok),
        same_keys,
        other_keys,
        queries,
        residual,
        w_out,
    )
    at_end = (rank == 0) | (rank == exp_count - 1)
    flags = jnp.stack([rank, at_end]).astype(jnp.int32)
    gain = norm_gain.reshape(1, D)
    flat_in = w_in.reshape(2 * hidden, D)
    count = len(parts)
    inward = [lax.ppermute(part, "exp", [(0, 1), (3, 2)]) for part in parts]
    near, across, total, outward = {}, {}, {}, {}
    homes, states, after = [], [], parts[0]
    for step, chunk in ORDER:
        if step == "near":
            after = near[chunk] = add_after(parts[chunk], inward[chunk], after)
            across[chunk] = lax.ppermute(near[chunk], "exp", [(1, 2), (2, 1)])
        elif step == "total":
            after = total[chunk] = add_after(near[chunk], across[chunk], after)
            outward[chunk] = lax.ppermute(total[chunk], "exp", [(1, 0), (2, 3)])
        else:
            own, *states = absorb(
                chunk, flags, total[chunk], outward[chunk], gain, flat_in, after, states
            )
            homes.append(own)
            after = states[0]
    middle_out = jnp.concatenate(homes, axis=1)
    activated = states[0]
    shares = gates / jnp.sum(gates, axis=1, keepdims=True)
    coefficient = jnp.sum(jnp.where(routes == 0, shares, 0.0), axis=1, keepdims=True)
    coefficient = coefficient.astype(jnp.bfloat16).astype(jnp.float32)
    share_parts = make_shares(activated, w_back.reshape(hidden, D))
    parts_count = len(SHARE_WIDTHS)
    arrivals = [exchange(share_parts[2 * i + 1], "exp", 1, exp_count) for i in range(parts_count)]
    earlier, after = [], activated
    for i in range(parts_count):
        own, leaving = pair_sum(share_parts[2 * i], arrivals[i], after)
        arrived = exchange(leaving, "exp", 2, exp_count)
        after = last_sum(coefficient, own, arrived, earlier)
        earlier = [after]
    return (middle_out, after)


def largest_divisor(row_count):
    candidate = min(row_count, 1024)
    while row_count % candidate != 0:
        candidate = candidate - 1
    return candidate


def apply_slice(row_block, coefficient, w_in, w_back):
    hidden_here = w_back.shape[1]
    flat_in = w_in.reshape(2 * hidden_here, D)
    projected = lax.dot_general(
        row_block, flat_in, (((1,), (1,)), ((), ())), preferred_element_type=jnp.float32
    )
    activated = jax.nn.silu(projected[:, :hidden_here]) * projected[:, hidden_here:]
    blended = (coefficient.astype(jnp.float32) * activated).astype(jnp.bfloat16)
    flat_back = w_back.reshape(hidden_here, D)
    return jnp.dot(blended, flat_back, preferred_element_type=jnp.float32).astype(jnp.bfloat16)


def wide_device(
    queries,
    keys,
    values,
    positions,
    bounds,
    w_out,
    residual,
    norm_gain,
    routes,
    gates,
    w_in,
    w_back,
):
    tok_rows = queries.shape[0]
    head_cols = queries.shape[1]
    heads_here = head_cols // HEAD_DIM
    exp_count = lax.axis_size("exp")
    key_head, value_head = own_heads(queries, keys, values)
    query_heads = queries.reshape(tok_rows, heads_here, HEAD_DIM).transpose(1, 0, 2)
    scale = HEAD_DIM ** (-0.5)
    reach_max = jnp.max(bounds)
    all_keys, all_values, all_places = (
        lax.all_gather(key_head, "ctx", axis=0, tiled=True),
        lax.all_gather(value_head, "ctx", axis=0, tiled=True),
        lax.all_gather(positions, "ctx", axis=0, tiled=True),
    )
    total_rows = all_keys.shape[0]
    tile_len = largest_divisor(total_rows)
    tile_count = total_rows // tile_len

    def process(state_in, key_rows, value_rows, place_rows):
        row_max, row_sum, running = state_in
        scores = (
            jnp.einsum("htd,nd->htn", query_heads, key_rows, preferred_element_type=jnp.float32)
            * scale
        )
        visible = (place_rows[None, :] <= bounds[:, None])[None, :, :]
        masked = jnp.where(visible, scores, -1e30)
        new_max = jnp.maximum(row_max, jnp.max(masked, axis=2))
        weights = jnp.exp(masked - new_max[..., None])
        rescale = jnp.exp(row_max - new_max)
        row_sum = row_sum * rescale + jnp.sum(weights, axis=2)
        running = running * rescale[..., None] + jnp.einsum(
            "htn,nd->htd",
            weights.astype(jnp.bfloat16),
            value_rows,
            preferred_element_type=jnp.float32,
        )
        return (new_max, row_sum, running)

    def one_tile(tile_number, state_now):
        first = tile_number * tile_len
        key_rows = lax.dynamic_slice_in_dim(all_keys, first, tile_len, 0)
        value_rows = lax.dynamic_slice_in_dim(all_values, first, tile_len, 0)
        place_rows = lax.dynamic_slice_in_dim(all_places, first, tile_len, 0)
        return lax.cond(
            jnp.min(place_rows) <= reach_max,
            lambda state_in: process(state_in, key_rows, value_rows, place_rows),
            lambda state_in: state_in,
            state_now,
        )

    start_state = (
        jnp.full((heads_here, tok_rows), -1e30, jnp.float32),
        jnp.zeros((heads_here, tok_rows), jnp.float32),
        jnp.zeros((heads_here, tok_rows, HEAD_DIM), jnp.float32),
    )
    row_max, row_sum, running = lax.fori_loop(0, tile_count, one_tile, start_state)
    attended = (running / row_sum[..., None]).astype(jnp.bfloat16)
    attended = attended.transpose(1, 0, 2).reshape(tok_rows, head_cols)
    attention_rows = lax.psum_scatter(
        jnp.dot(attended, w_out, preferred_element_type=jnp.float32).astype(jnp.bfloat16),
        "exp",
        scatter_dimension=0,
        tiled=True,
    ).astype(jnp.float32)
    middle = (residual.astype(jnp.float32) + attention_rows).astype(jnp.bfloat16)
    wide = middle.astype(jnp.float32)
    mean_square = jnp.mean(wide * wide, axis=1, keepdims=True)
    normed = (wide * lax.rsqrt(mean_square + 1e-06) * norm_gain[None, :]).astype(jnp.bfloat16)
    local_rows = residual.shape[0]
    shares = gates / jnp.sum(gates, axis=1, keepdims=True)
    slice_expert = jnp.arange(exp_count, dtype=jnp.int32) // HID_SPLIT
    hits = routes[:, :, None] == slice_expert[None, None, :]
    coefficient = jnp.sum(jnp.where(hits, shares[:, :, None], 0.0), axis=1).astype(jnp.bfloat16)
    owner_weights = coefficient.transpose(1, 0)[:, :, None]
    copies = jnp.broadcast_to(normed[None, :, :], (exp_count, local_rows, D))
    row_block = lax.all_to_all(copies, "exp", split_axis=0, concat_axis=0, tiled=True)
    weight_block = lax.all_to_all(owner_weights, "exp", split_axis=0, concat_axis=0, tiled=True)
    slot_count = row_block.shape[1]
    produced = apply_slice(
        row_block.reshape(exp_count * slot_count, D),
        weight_block.reshape(exp_count * slot_count, 1),
        w_in,
        w_back,
    )
    produced = produced.reshape(exp_count, slot_count, D)
    arrived = lax.all_to_all(produced, "exp", split_axis=0, concat_axis=0, tiled=True)
    expert_out = jnp.sum(arrived.astype(jnp.float32), axis=0).astype(jnp.bfloat16)
    return (middle, expert_out)


def solution(mesh):
    in_specs = (
        P("ctx", "exp"),
        P("ctx", None),
        P("ctx", None),
        P("ctx"),
        P("ctx"),
        P("exp", None),
        P(("ctx", "exp"), None),
        P(),
        P(("ctx", "exp"), None),
        P(("ctx", "exp"), None),
        P("exp", None, None),
        P("exp", None, None),
    )
    out_specs = (P(("ctx", "exp"), None), P(("ctx", "exp"), None))
    one_line = mesh.shape["exp"] == HID_SPLIT and mesh.shape["ctx"] == 8
    return jax.shard_map(
        line_device if one_line else wide_device,
        mesh=mesh,
        in_specs=in_specs,
        out_specs=out_specs,
        check_vma=False,
    )
```

```python
import functools

import jax
import jax.numpy as jnp
from jax import lax
from jax.experimental import pallas as pl
from jax.experimental.pallas import tpu as pltpu
from jax.sharding import PartitionSpec as P

D = 4096
HEADS = 64
KV_HEADS = 4
HEAD_DIM = 128
HID_SPLIT = 4
STACK = 4
WIDTHS = (2048, 2048)
SPANS = tuple((sum(WIDTHS[:i]), width) for i, width in enumerate(WIDTHS))
PAD_ROWS = 16
BASE = 64
LOG2E = 1.4426950408889634
VMEM = pl.BlockSpec(memory_space=pltpu.VMEM)
ANY = pl.BlockSpec(memory_space=pl.ANY)
LIGHT = pl.CostEstimate(flops=1024, bytes_accessed=1024, transcendentals=0)


def exchange(value, axis, offset, size):
    return lax.ppermute(value, axis, [(i, i ^ offset) for i in range(size)])


def attend_kernel(rank_ref, same_ref, other_ref, q_ref, resid_ref, w_hbm, *refs):
    outs = refs[: 2 * len(WIDTHS)]
    w_buf, k_buf, v_buf, bias, attended, acc, sems = refs[2 * len(WIDTHS) :]
    tok = q_ref.shape[0]
    heads = q_ref.shape[1] // HEAD_DIM
    copies = []
    for chunk, (first, width) in enumerate(SPANS):
        span = pl.ds(first, width)
        copy = pltpu.make_async_copy(w_hbm.at[:, span], w_buf.at[:, span], sems.at[chunk])
        copy.start()
        copies.append(copy)
    extra = same_ref[0, tok : tok + PAD_ROWS, :].astype(jnp.float32)
    bound = extra[1:2, :tok] * BASE + extra[1:2, tok:]
    bound = jnp.broadcast_to(bound, (tok, tok)).T
    lane = lax.broadcasted_iota(jnp.int32, (1, tok), 1).astype(jnp.float32)
    ones = jnp.ones((tok, HEAD_DIM), jnp.bfloat16)
    half_count = same_ref.shape[0]
    for b in range(2 * half_count):
        rows = slice(b * tok, (b + 1) * tok)
        group, row = (same_ref, b) if b < half_count else (other_ref, b - half_count)
        k_buf[rows, :] = group[row, :tok, :HEAD_DIM]
        v_buf[rows, :HEAD_DIM] = group[row, :tok, HEAD_DIM:]
        v_buf[rows, HEAD_DIM:] = ones
        start = group[row, tok : tok + PAD_ROWS, :HEAD_DIM].astype(jnp.float32)[:1]
        place = start * tok + lane
        bias[:, rows] = jnp.where(place <= bound, 0.0, -1e30)
    factor = HEAD_DIM ** (-0.5) * LOG2E

    def some_heads(step, carry):
        base = step * STACK * HEAD_DIM
        parts = []
        for j in range(STACK):
            start = pl.multiple_of(base + j * HEAD_DIM, HEAD_DIM)
            parts.append(q_ref[:, pl.ds(start, HEAD_DIM)])
        stacked = jnp.concatenate(parts, axis=0)
        scores = lax.dot_general(
            stacked, k_buf[...], (((1,), (1,)), ((), ())), preferred_element_type=jnp.float32
        )
        scores = scores.reshape(STACK, tok, -1) * factor + bias[...][None]
        row_max = jnp.max(scores, axis=2, keepdims=True)
        weights = jnp.exp2(scores - row_max).astype(jnp.bfloat16)
        summed = jnp.dot(
            weights.reshape(STACK * tok, -1), v_buf[...], preferred_element_type=jnp.float32
        )
        result = (summed[:, :HEAD_DIM] / summed[:, HEAD_DIM:]).astype(jnp.bfloat16)
        for j in range(STACK):
            start = pl.multiple_of(base + j * HEAD_DIM, HEAD_DIM)
            attended[:, pl.ds(start, HEAD_DIM)] = result[j * tok : (j + 1) * tok]
        return carry

    lax.fori_loop(0, heads // STACK, some_heads, 0, unroll=True)
    home = resid_ref.shape[0]
    rank = rank_ref[0]
    side = rank % 2
    kept = [pl.multiple_of((side + 2 * i) * home, home) for i in range(2)]
    leaving = [pl.multiple_of((1 - side + 2 * i) * home, home) for i in range(2)]
    top = pl.multiple_of(rank * home, home)
    for chunk, (first, width) in enumerate(SPANS):
        copies[chunk].wait()
        span = slice(first, first + width)
        acc[:, span] = jnp.dot(
            attended[...], w_buf[:, span], preferred_element_type=jnp.float32
        )
        acc[pl.ds(top, home), span] += resid_ref[:, span].astype(jnp.float32)
        for i in range(2):
            rows = slice(i * home, (i + 1) * home)
            outs[2 * chunk][rows, :] = acc[pl.ds(kept[i], home), span].astype(jnp.bfloat16)
            outs[2 * chunk + 1][rows, :] = acc[pl.ds(leaving[i], home), span].astype(
                jnp.bfloat16
            )


def attend_project(rank, same, other, queries, residual, w_out):
    tok, width = queries.shape
    keys_in_all = 2 * same.shape[0] * tok
    return pl.pallas_call(
        attend_kernel,
        out_shape=[
            jax.ShapeDtypeStruct((tok // 2, w), jnp.bfloat16) for w in WIDTHS for _ in range(2)
        ],
        in_specs=[pl.BlockSpec(memory_space=pltpu.SMEM)] + [VMEM] * 4 + [ANY],
        out_specs=[VMEM] * (2 * len(WIDTHS)),
        scratch_shapes=[
            pltpu.VMEM((width, D), jnp.bfloat16),
            pltpu.VMEM((keys_in_all, HEAD_DIM), jnp.bfloat16),
            pltpu.VMEM((keys_in_all, 2 * HEAD_DIM), jnp.bfloat16),
            pltpu.VMEM((tok, keys_in_all), jnp.float32),
            pltpu.VMEM((tok, width), jnp.bfloat16),
            pltpu.VMEM((tok, D), jnp.float32),
            pltpu.SemaphoreType.DMA((len(WIDTHS),)),
        ],
        compiler_params=pltpu.CompilerParams(vmem_limit_bytes=44 * 1024 * 1024),
        cost_estimate=pl.CostEstimate(
            flops=2 * tok * width * (2 * keys_in_all + D),
            bytes_accessed=2 * width * D,
            transcendentals=tok * width // HEAD_DIM * keys_in_all,
        ),
        name="attend_project",
    )(rank, same, other, queries, residual, w_out)


def stage_kernel(q_hbm, resid_hbm, q_ref, resid_ref, sems):
    copies = [
        pltpu.make_async_copy(q_hbm, q_ref, sems.at[0]),
        pltpu.make_async_copy(resid_hbm, resid_ref, sems.at[1]),
    ]
    for copy in copies:
        copy.start()
    for copy in copies:
        copy.wait()


def stage(queries, residual):
    arrays = (queries, residual)
    return pl.pallas_call(
        stage_kernel,
        out_shape=[jax.ShapeDtypeStruct(array.shape, array.dtype) for array in arrays],
        in_specs=[ANY, ANY],
        out_specs=[VMEM, VMEM],
        scratch_shapes=[pltpu.SemaphoreType.DMA((2,))],
        compiler_params=pltpu.CompilerParams(vmem_limit_bytes=4 * 1024 * 1024),
        cost_estimate=LIGHT,
        name="stage",
    )(*arrays)


def join_kernel(*refs):
    out_ref = refs[-1]
    first = 0
    for piece in refs[1:-1]:
        rows = piece.shape[0]
        out_ref[first : first + rows, :] = piece[...]
        first += rows


def join_after(pieces, after):
    rows = sum(piece.shape[0] for piece in pieces)
    width = pieces[0].shape[1]
    return pl.pallas_call(
        join_kernel,
        out_shape=jax.ShapeDtypeStruct((rows, width), jnp.bfloat16),
        in_specs=[ANY] + [VMEM] * len(pieces),
        out_specs=VMEM,
        compiler_params=pltpu.CompilerParams(vmem_limit_bytes=8 * 1024 * 1024),
        cost_estimate=LIGHT,
        name="join_after",
    )(after, *pieces)


def absorb_kernel(chunk, rank_ref, mine_ref, theirs_ref, gain_ref, w_ref, *refs):
    last = chunk == len(WIDTHS) - 1
    state_count = 0 if chunk == 0 else 2
    states = refs[:state_count]
    home_ref = refs[state_count + int(last)]
    outs = refs[state_count + int(last) + 1 :]
    first, width = SPANS[chunk]
    span = slice(first, first + width)
    home = home_ref.shape[0]
    place = rank_ref[0] // 2
    home_ref[...] = mine_ref[pl.ds(pl.multiple_of(place * home, home), home), :]
    wide = jnp.concatenate([mine_ref[...], theirs_ref[...]], axis=0).astype(jnp.float32)
    gained = (wide * gain_ref[:, span]).astype(jnp.bfloat16)
    product = lax.dot_general(
        gained, w_ref[:, span], (((1,), (1,)), ((), ())), preferred_element_type=jnp.float32
    )
    square = sum(
        wide[:, i * 128 : (i + 1) * 128] * wide[:, i * 128 : (i + 1) * 128]
        for i in range(width // 128)
    )
    if chunk > 0:
        product += states[0][...]
        square += states[1][...]
    if not last:
        outs[0][...] = product
        outs[1][...] = square
        return
    back_ref = refs[state_count]
    shares, act_buf = outs[:-1], outs[-1]
    hidden = product.shape[1] // 2
    mean_square = jnp.sum(square, axis=1, keepdims=True) / D
    product = product * lax.rsqrt(mean_square + 1e-06)
    gate = product[:, :hidden]
    act_buf[...] = gate / (1.0 + jnp.exp(-gate)) * product[:, hidden:]
    ordered = []
    for offset in range(len(shares)):
        row = (offset % 2) * 2 * home + (place ^ (offset // 2)) * home
        ordered.append(act_buf[pl.ds(pl.multiple_of(row, home), home), :])
    ordered = jnp.concatenate(ordered, axis=0).astype(jnp.bfloat16)
    for part_first, part_width in SPANS:
        part = slice(part_first, part_first + part_width)
        result = jnp.dot(ordered, back_ref[:, part], preferred_element_type=jnp.float32)
        for i, share in enumerate(shares):
            share[:, part] = result[i * home : (i + 1) * home].astype(jnp.bfloat16)


def absorb(chunk, rank, mine, theirs, gain, w_in, states, back):
    half, width = mine.shape
    rows = w_in.shape[0]
    count = lax.axis_size("exp")
    home = 2 * half // count
    out_shape = [jax.ShapeDtypeStruct((home, width), jnp.bfloat16)]
    scratch = []
    operands = [rank, mine, theirs, gain, w_in, *states]
    if chunk == len(WIDTHS) - 1:
        operands.append(back)
        out_shape += [jax.ShapeDtypeStruct((home, D), jnp.bfloat16)] * count
        scratch = [pltpu.VMEM((2 * half, rows // 2), jnp.float32)]
    else:
        out_shape += [
            jax.ShapeDtypeStruct((2 * half, rows), jnp.float32),
            jax.ShapeDtypeStruct((2 * half, 128), jnp.float32),
        ]
    return pl.pallas_call(
        functools.partial(absorb_kernel, chunk),
        out_shape=out_shape,
        in_specs=[pl.BlockSpec(memory_space=pltpu.SMEM)] + [VMEM] * (len(operands) - 1),
        out_specs=[VMEM] * len(out_shape),
        scratch_shapes=scratch,
        compiler_params=pltpu.CompilerParams(vmem_limit_bytes=16 * 1024 * 1024),
        cost_estimate=LIGHT,
        name="absorb",
    )(*operands)


def own_heads(queries, keys, values):
    heads_here = queries.shape[1] // HEAD_DIM
    kv_number = lax.axis_index("exp") * heads_here // (HEADS // KV_HEADS)
    key_head = lax.dynamic_slice_in_dim(keys, kv_number * HEAD_DIM, HEAD_DIM, 1)
    value_head = lax.dynamic_slice_in_dim(values, kv_number * HEAD_DIM, HEAD_DIM, 1)
    return key_head, value_head


def line_device(
    queries,
    keys,
    values,
    positions,
    bounds,
    w_out,
    residual,
    norm_gain,
    routes,
    gates,
    w_in,
    w_back,
):
    tok = queries.shape[0]
    home = residual.shape[0]
    hidden = w_back.shape[1]
    ctx_count = lax.axis_size("ctx")
    exp_count = lax.axis_size("exp")
    rank = lax.axis_index("exp")
    key_head, value_head = own_heads(queries, keys, values)
    staged_queries, staged_residual = stage(queries, residual)
    block = (positions[0] // tok).astype(jnp.bfloat16)
    limits = jnp.concatenate([bounds // BASE, bounds % BASE]).astype(jnp.bfloat16)
    width = 2 * HEAD_DIM
    payload = jnp.concatenate(
        [
            jnp.concatenate([key_head, value_head], axis=1),
            jnp.full((1, width), block, jnp.bfloat16),
            limits.reshape(1, width),
            jnp.zeros((PAD_ROWS - 2, width), jnp.bfloat16),
        ],
        axis=0,
    )
    same_rows = join_after(
        [payload] + [exchange(payload, "ctx", r, ctx_count) for r in range(2, ctx_count, 2)],
        payload,
    )
    same_keys = same_rows.reshape(ctx_count // 2, tok + PAD_ROWS, 2 * HEAD_DIM)
    other_keys = exchange(same_rows, "ctx", 1, ctx_count).reshape(same_keys.shape)
    ranks = rank.astype(jnp.int32).reshape(1)
    parts = attend_project(
        ranks, same_keys, other_keys, staged_queries, staged_residual, w_out
    )
    gain = norm_gain.reshape(1, D)
    flat_in = w_in.reshape(2 * hidden, D)
    flat_back = w_back.reshape(hidden, D)
    count = len(WIDTHS)
    arrived = [exchange(parts[2 * i + 1], "exp", 1, exp_count) for i in range(count)]
    near = [parts[2 * i] + arrived[i] for i in range(count)]
    across = [exchange(near[i], "exp", 2, exp_count) for i in range(count)]
    mine = [near[i] + across[i] for i in range(count)]
    theirs = [exchange(mine[i], "exp", 1, exp_count) for i in range(count)]
    homes, states = [], []
    for chunk in range(count):
        own, *states = absorb(
            chunk, ranks, mine[chunk], theirs[chunk], gain, flat_in, states, flat_back
        )
        homes.append(own)
    middle_out = jnp.concatenate(homes, axis=1)
    expert = states[0].astype(jnp.float32)
    for offset in range(1, exp_count):
        expert = expert + exchange(states[offset], "exp", offset, exp_count).astype(jnp.float32)
    shares = gates / jnp.sum(gates, axis=1, keepdims=True)
    coefficient = jnp.sum(jnp.where(routes == 0, shares, 0.0), axis=1, keepdims=True)
    coefficient = coefficient.astype(jnp.bfloat16).astype(jnp.float32)
    return (middle_out, (expert * coefficient).astype(jnp.bfloat16))


def largest_divisor(row_count):
    candidate = min(row_count, 1024)
    while row_count % candidate != 0:
        candidate = candidate - 1
    return candidate


def apply_slice(row_block, coefficient, w_in, w_back):
    hidden_here = w_back.shape[1]
    flat_in = w_in.reshape(2 * hidden_here, D)
    projected = lax.dot_general(
        row_block, flat_in, (((1,), (1,)), ((), ())), preferred_element_type=jnp.float32
    )
    activated = jax.nn.silu(projected[:, :hidden_here]) * projected[:, hidden_here:]
    blended = (coefficient.astype(jnp.float32) * activated).astype(jnp.bfloat16)
    flat_back = w_back.reshape(hidden_here, D)
    return jnp.dot(blended, flat_back, preferred_element_type=jnp.float32).astype(jnp.bfloat16)


def wide_device(
    queries,
    keys,
    values,
    positions,
    bounds,
    w_out,
    residual,
    norm_gain,
    routes,
    gates,
    w_in,
    w_back,
):
    tok_rows = queries.shape[0]
    head_cols = queries.shape[1]
    heads_here = head_cols // HEAD_DIM
    exp_count = lax.axis_size("exp")
    key_head, value_head = own_heads(queries, keys, values)
    query_heads = queries.reshape(tok_rows, heads_here, HEAD_DIM).transpose(1, 0, 2)
    scale = HEAD_DIM ** (-0.5)
    reach_max = jnp.max(bounds)
    all_keys, all_values, all_places = (
        lax.all_gather(key_head, "ctx", axis=0, tiled=True),
        lax.all_gather(value_head, "ctx", axis=0, tiled=True),
        lax.all_gather(positions, "ctx", axis=0, tiled=True),
    )
    total_rows = all_keys.shape[0]
    tile_len = largest_divisor(total_rows)
    tile_count = total_rows // tile_len

    def process(state_in, key_rows, value_rows, place_rows):
        row_max, row_sum, running = state_in
        scores = (
            jnp.einsum("htd,nd->htn", query_heads, key_rows, preferred_element_type=jnp.float32)
            * scale
        )
        visible = (place_rows[None, :] <= bounds[:, None])[None, :, :]
        masked = jnp.where(visible, scores, -1e30)
        new_max = jnp.maximum(row_max, jnp.max(masked, axis=2))
        weights = jnp.exp(masked - new_max[..., None])
        rescale = jnp.exp(row_max - new_max)
        row_sum = row_sum * rescale + jnp.sum(weights, axis=2)
        running = running * rescale[..., None] + jnp.einsum(
            "htn,nd->htd",
            weights.astype(jnp.bfloat16),
            value_rows,
            preferred_element_type=jnp.float32,
        )
        return (new_max, row_sum, running)

    def one_tile(tile_number, state_now):
        first = tile_number * tile_len
        key_rows = lax.dynamic_slice_in_dim(all_keys, first, tile_len, 0)
        value_rows = lax.dynamic_slice_in_dim(all_values, first, tile_len, 0)
        place_rows = lax.dynamic_slice_in_dim(all_places, first, tile_len, 0)
        return lax.cond(
            jnp.min(place_rows) <= reach_max,
            lambda state_in: process(state_in, key_rows, value_rows, place_rows),
            lambda state_in: state_in,
            state_now,
        )

    start_state = (
        jnp.full((heads_here, tok_rows), -1e30, jnp.float32),
        jnp.zeros((heads_here, tok_rows), jnp.float32),
        jnp.zeros((heads_here, tok_rows, HEAD_DIM), jnp.float32),
    )
    row_max, row_sum, running = lax.fori_loop(0, tile_count, one_tile, start_state)
    attended = (running / row_sum[..., None]).astype(jnp.bfloat16)
    attended = attended.transpose(1, 0, 2).reshape(tok_rows, head_cols)
    attention_rows = lax.psum_scatter(
        jnp.dot(attended, w_out, preferred_element_type=jnp.float32).astype(jnp.bfloat16),
        "exp",
        scatter_dimension=0,
        tiled=True,
    ).astype(jnp.float32)
    middle = (residual.astype(jnp.float32) + attention_rows).astype(jnp.bfloat16)
    wide = middle.astype(jnp.float32)
    mean_square = jnp.mean(wide * wide, axis=1, keepdims=True)
    normed = (wide * lax.rsqrt(mean_square + 1e-06) * norm_gain[None, :]).astype(jnp.bfloat16)
    local_rows = residual.shape[0]
    shares = gates / jnp.sum(gates, axis=1, keepdims=True)
    slice_expert = jnp.arange(exp_count, dtype=jnp.int32) // HID_SPLIT
    hits = routes[:, :, None] == slice_expert[None, None, :]
    coefficient = jnp.sum(jnp.where(hits, shares[:, :, None], 0.0), axis=1).astype(jnp.bfloat16)
    owner_weights = coefficient.transpose(1, 0)[:, :, None]
    copies = jnp.broadcast_to(normed[None, :, :], (exp_count, local_rows, D))
    row_block = lax.all_to_all(copies, "exp", split_axis=0, concat_axis=0, tiled=True)
    weight_block = lax.all_to_all(owner_weights, "exp", split_axis=0, concat_axis=0, tiled=True)
    slot_count = row_block.shape[1]
    produced = apply_slice(
        row_block.reshape(exp_count * slot_count, D),
        weight_block.reshape(exp_count * slot_count, 1),
        w_in,
        w_back,
    )
    produced = produced.reshape(exp_count, slot_count, D)
    arrived = lax.all_to_all(produced, "exp", split_axis=0, concat_axis=0, tiled=True)
    expert_out = jnp.sum(arrived.astype(jnp.float32), axis=0).astype(jnp.bfloat16)
    return (middle, expert_out)


def solution(mesh):
    in_specs = (
        P("ctx", "exp"),
        P("ctx", None),
        P("ctx", None),
        P("ctx"),
        P("ctx"),
        P("exp", None),
        P(("ctx", "exp"), None),
        P(),
        P(("ctx", "exp"), None),
        P(("ctx", "exp"), None),
        P("exp", None, None),
        P("exp", None, None),
    )
    out_specs = (P(("ctx", "exp"), None), P(("ctx", "exp"), None))
    one_line = mesh.shape["exp"] == HID_SPLIT and mesh.shape["ctx"] == 8
    return jax.shard_map(
        line_device if one_line else wide_device,
        mesh=mesh,
        in_specs=in_specs,
        out_specs=out_specs,
        check_vma=False,
    )
```

```python
import functools

import jax
import jax.numpy as jnp
from jax import lax
from jax.experimental import pallas as pl
from jax.experimental.pallas import tpu as pltpu
from jax.sharding import PartitionSpec as P

D = 4096
HEADS = 64
KV_HEADS = 4
HEAD_DIM = 128
HID_SPLIT = 4
STACK = 4
WIDTHS = (1024, 1024, 1024, 1024)
SPANS = tuple((sum(WIDTHS[:i]), width) for i, width in enumerate(WIDTHS))
PAD_ROWS = 16
BASE = 64
IN_FLIGHT = 2
LOG2E = 1.4426950408889634
VMEM = pl.BlockSpec(memory_space=pltpu.VMEM)
ANY = pl.BlockSpec(memory_space=pl.ANY)
LIGHT = pl.CostEstimate(flops=1024, bytes_accessed=1024, transcendentals=0)


def exchange(value, axis, offset, size):
    return lax.ppermute(value, axis, [(i, i ^ offset) for i in range(size)])


def attend_kernel(rank_ref, same_ref, other_ref, q_ref, resid_ref, w_hbm, *refs):
    outs = refs[: 2 * len(WIDTHS)]
    w_buf, k_buf, v_buf, bias, attended, acc, sems = refs[2 * len(WIDTHS) :]
    tok = q_ref.shape[0]
    heads = q_ref.shape[1] // HEAD_DIM
    copies = []
    for chunk, (first, width) in enumerate(SPANS):
        span = pl.ds(first, width)
        copy = pltpu.make_async_copy(w_hbm.at[:, span], w_buf.at[:, span], sems.at[chunk])
        copy.start()
        copies.append(copy)
    extra = same_ref[0, tok : tok + PAD_ROWS, :].astype(jnp.float32)
    bound = extra[1:2, :tok] * BASE + extra[1:2, tok:]
    bound = jnp.broadcast_to(bound, (tok, tok)).T
    lane = lax.broadcasted_iota(jnp.int32, (1, tok), 1).astype(jnp.float32)
    ones = jnp.ones((tok, HEAD_DIM), jnp.bfloat16)
    half_count = same_ref.shape[0]
    for b in range(2 * half_count):
        rows = slice(b * tok, (b + 1) * tok)
        group, row = (same_ref, b) if b < half_count else (other_ref, b - half_count)
        k_buf[rows, :] = group[row, :tok, :HEAD_DIM]
        v_buf[rows, :HEAD_DIM] = group[row, :tok, HEAD_DIM:]
        v_buf[rows, HEAD_DIM:] = ones
        start = group[row, tok : tok + PAD_ROWS, :HEAD_DIM].astype(jnp.float32)[:1]
        place = start * tok + lane
        bias[:, rows] = jnp.where(place <= bound, 0.0, -1e30)
    factor = HEAD_DIM ** (-0.5) * LOG2E

    def some_heads(step, carry):
        base = step * STACK * HEAD_DIM
        parts = []
        for j in range(STACK):
            start = pl.multiple_of(base + j * HEAD_DIM, HEAD_DIM)
            parts.append(q_ref[:, pl.ds(start, HEAD_DIM)])
        stacked = jnp.concatenate(parts, axis=0)
        scores = lax.dot_general(
            stacked, k_buf[...], (((1,), (1,)), ((), ())), preferred_element_type=jnp.float32
        )
        scores = scores.reshape(STACK, tok, -1) * factor + bias[...][None]
        row_max = jnp.max(scores, axis=2, keepdims=True)
        weights = jnp.exp2(scores - row_max).astype(jnp.bfloat16)
        summed = jnp.dot(
            weights.reshape(STACK * tok, -1), v_buf[...], preferred_element_type=jnp.float32
        )
        result = (summed[:, :HEAD_DIM] / summed[:, HEAD_DIM:]).astype(jnp.bfloat16)
        for j in range(STACK):
            start = pl.multiple_of(base + j * HEAD_DIM, HEAD_DIM)
            attended[:, pl.ds(start, HEAD_DIM)] = result[j * tok : (j + 1) * tok]
        return carry

    lax.fori_loop(0, heads // STACK, some_heads, 0, unroll=True)
    home = resid_ref.shape[0]
    rank = rank_ref[0]
    side = rank % 2
    kept = [pl.multiple_of((side + 2 * i) * home, home) for i in range(2)]
    leaving = [pl.multiple_of((1 - side + 2 * i) * home, home) for i in range(2)]
    top = pl.multiple_of(rank * home, home)
    for chunk, (first, width) in enumerate(SPANS):
        copies[chunk].wait()
        span = slice(first, first + width)
        acc[:, span] = jnp.dot(
            attended[...], w_buf[:, span], preferred_element_type=jnp.float32
        )
        acc[pl.ds(top, home), span] += resid_ref[:, span].astype(jnp.float32)
        for i in range(2):
            rows = slice(i * home, (i + 1) * home)
            outs[2 * chunk][rows, :] = acc[pl.ds(kept[i], home), span].astype(jnp.bfloat16)
            outs[2 * chunk + 1][rows, :] = acc[pl.ds(leaving[i], home), span].astype(
                jnp.bfloat16
            )


def attend_project(rank, same, other, queries, residual, w_out):
    tok, width = queries.shape
    keys_in_all = 2 * same.shape[0] * tok
    return pl.pallas_call(
        attend_kernel,
        out_shape=[
            jax.ShapeDtypeStruct((tok // 2, w), jnp.bfloat16) for w in WIDTHS for _ in range(2)
        ],
        in_specs=[pl.BlockSpec(memory_space=pltpu.SMEM)] + [VMEM] * 4 + [ANY],
        out_specs=[VMEM] * (2 * len(WIDTHS)),
        scratch_shapes=[
            pltpu.VMEM((width, D), jnp.bfloat16),
            pltpu.VMEM((keys_in_all, HEAD_DIM), jnp.bfloat16),
            pltpu.VMEM((keys_in_all, 2 * HEAD_DIM), jnp.bfloat16),
            pltpu.VMEM((tok, keys_in_all), jnp.float32),
            pltpu.VMEM((tok, width), jnp.bfloat16),
            pltpu.VMEM((tok, D), jnp.float32),
            pltpu.SemaphoreType.DMA((len(WIDTHS),)),
        ],
        compiler_params=pltpu.CompilerParams(vmem_limit_bytes=44 * 1024 * 1024),
        cost_estimate=pl.CostEstimate(
            flops=2 * tok * width * (2 * keys_in_all + D),
            bytes_accessed=2 * width * D,
            transcendentals=tok * width // HEAD_DIM * keys_in_all,
        ),
        name="attend_project",
    )(rank, same, other, queries, residual, w_out)


def stage_kernel(q_hbm, resid_hbm, q_ref, resid_ref, sems):
    copies = [
        pltpu.make_async_copy(q_hbm, q_ref, sems.at[0]),
        pltpu.make_async_copy(resid_hbm, resid_ref, sems.at[1]),
    ]
    for copy in copies:
        copy.start()
    for copy in copies:
        copy.wait()


def stage(queries, residual):
    arrays = (queries, residual)
    return pl.pallas_call(
        stage_kernel,
        out_shape=[jax.ShapeDtypeStruct(array.shape, array.dtype) for array in arrays],
        in_specs=[ANY, ANY],
        out_specs=[VMEM, VMEM],
        scratch_shapes=[pltpu.SemaphoreType.DMA((2,))],
        compiler_params=pltpu.CompilerParams(vmem_limit_bytes=4 * 1024 * 1024),
        cost_estimate=LIGHT,
        name="stage",
    )(*arrays)


def join_kernel(*refs):
    out_ref = refs[-1]
    first = 0
    for piece in refs[1:-1]:
        rows = piece.shape[0]
        out_ref[first : first + rows, :] = piece[...]
        first += rows


def join_after(pieces, after):
    rows = sum(piece.shape[0] for piece in pieces)
    width = pieces[0].shape[1]
    return pl.pallas_call(
        join_kernel,
        out_shape=jax.ShapeDtypeStruct((rows, width), jnp.bfloat16),
        in_specs=[ANY] + [VMEM] * len(pieces),
        out_specs=VMEM,
        compiler_params=pltpu.CompilerParams(vmem_limit_bytes=8 * 1024 * 1024),
        cost_estimate=LIGHT,
        name="join_after",
    )(after, *pieces)


def absorb_kernel(chunk, rank_ref, mine_ref, theirs_ref, gain_ref, w_ref, *refs):
    last = chunk == len(WIDTHS) - 1
    state_count = 0 if chunk == 0 else 2
    states = refs[:state_count]
    home_ref = refs[state_count + int(last)]
    outs = refs[state_count + int(last) + 1 :]
    first, width = SPANS[chunk]
    span = slice(first, first + width)
    home = home_ref.shape[0]
    place = rank_ref[0] // 2
    home_ref[...] = mine_ref[pl.ds(pl.multiple_of(place * home, home), home), :]
    wide = jnp.concatenate([mine_ref[...], theirs_ref[...]], axis=0).astype(jnp.float32)
    gained = (wide * gain_ref[:, span]).astype(jnp.bfloat16)
    product = lax.dot_general(
        gained, w_ref[:, span], (((1,), (1,)), ((), ())), preferred_element_type=jnp.float32
    )
    square = sum(
        wide[:, i * 128 : (i + 1) * 128] * wide[:, i * 128 : (i + 1) * 128]
        for i in range(width // 128)
    )
    if chunk > 0:
        product += states[0][...]
        square += states[1][...]
    if not last:
        outs[0][...] = product
        outs[1][...] = square
        return
    back_ref = refs[state_count]
    shares, act_buf = outs[:-1], outs[-1]
    hidden = product.shape[1] // 2
    mean_square = jnp.sum(square, axis=1, keepdims=True) / D
    product = product * lax.rsqrt(mean_square + 1e-06)
    gate = product[:, :hidden]
    act_buf[...] = gate / (1.0 + jnp.exp(-gate)) * product[:, hidden:]
    ordered = []
    for offset in range(len(shares)):
        row = (offset % 2) * 2 * home + (place ^ (offset // 2)) * home
        ordered.append(act_buf[pl.ds(pl.multiple_of(row, home), home), :])
    ordered = jnp.concatenate(ordered, axis=0).astype(jnp.bfloat16)
    for part_first, part_width in SPANS:
        part = slice(part_first, part_first + part_width)
        result = jnp.dot(ordered, back_ref[:, part], preferred_element_type=jnp.float32)
        for i, share in enumerate(shares):
            share[:, part] = result[i * home : (i + 1) * home].astype(jnp.bfloat16)


def absorb(chunk, rank, mine, theirs, gain, w_in, states, back):
    half, width = mine.shape
    rows = w_in.shape[0]
    count = lax.axis_size("exp")
    home = 2 * half // count
    out_shape = [jax.ShapeDtypeStruct((home, width), jnp.bfloat16)]
    scratch = []
    operands = [rank, mine, theirs, gain, w_in, *states]
    if chunk == len(WIDTHS) - 1:
        operands.append(back)
        out_shape += [jax.ShapeDtypeStruct((home, D), jnp.bfloat16)] * count
        scratch = [pltpu.VMEM((2 * half, rows // 2), jnp.float32)]
    else:
        out_shape += [
            jax.ShapeDtypeStruct((2 * half, rows), jnp.float32),
            jax.ShapeDtypeStruct((2 * half, 128), jnp.float32),
        ]
    return pl.pallas_call(
        functools.partial(absorb_kernel, chunk),
        out_shape=out_shape,
        in_specs=[pl.BlockSpec(memory_space=pltpu.SMEM)] + [VMEM] * (len(operands) - 1),
        out_specs=[VMEM] * len(out_shape),
        scratch_shapes=scratch,
        compiler_params=pltpu.CompilerParams(vmem_limit_bytes=16 * 1024 * 1024),
        cost_estimate=LIGHT,
        name="absorb",
    )(*operands)


def own_heads(queries, keys, values):
    heads_here = queries.shape[1] // HEAD_DIM
    kv_number = lax.axis_index("exp") * heads_here // (HEADS // KV_HEADS)
    key_head = lax.dynamic_slice_in_dim(keys, kv_number * HEAD_DIM, HEAD_DIM, 1)
    value_head = lax.dynamic_slice_in_dim(values, kv_number * HEAD_DIM, HEAD_DIM, 1)
    return key_head, value_head


def line_device(
    queries,
    keys,
    values,
    positions,
    bounds,
    w_out,
    residual,
    norm_gain,
    routes,
    gates,
    w_in,
    w_back,
):
    tok = queries.shape[0]
    home = residual.shape[0]
    hidden = w_back.shape[1]
    ctx_count = lax.axis_size("ctx")
    exp_count = lax.axis_size("exp")
    rank = lax.axis_index("exp")
    key_head, value_head = own_heads(queries, keys, values)
    staged_queries, staged_residual = stage(queries, residual)
    block = (positions[0] // tok).astype(jnp.bfloat16)
    limits = jnp.concatenate([bounds // BASE, bounds % BASE]).astype(jnp.bfloat16)
    width = 2 * HEAD_DIM
    payload = jnp.concatenate(
        [
            jnp.concatenate([key_head, value_head], axis=1),
            jnp.full((1, width), block, jnp.bfloat16),
            limits.reshape(1, width),
            jnp.zeros((PAD_ROWS - 2, width), jnp.bfloat16),
        ],
        axis=0,
    )
    same_rows = join_after(
        [payload] + [exchange(payload, "ctx", r, ctx_count) for r in range(2, ctx_count, 2)],
        payload,
    )
    same_keys = same_rows.reshape(ctx_count // 2, tok + PAD_ROWS, 2 * HEAD_DIM)
    other_keys = exchange(same_rows, "ctx", 1, ctx_count).reshape(same_keys.shape)
    ranks = rank.astype(jnp.int32).reshape(1)
    parts = attend_project(
        ranks, same_keys, other_keys, staged_queries, staged_residual, w_out
    )
    gain = norm_gain.reshape(1, D)
    flat_in = w_in.reshape(2 * hidden, D)
    flat_back = w_back.reshape(hidden, D)
    count = len(WIDTHS)

    def swap(values, offset):
        results = []
        for i, value in enumerate(values):
            if i >= IN_FLIGHT:
                value, _ = lax.optimization_barrier((value, results[i - IN_FLIGHT]))
            results.append(exchange(value, "exp", offset, exp_count))
        return results

    arrived = swap(parts[1::2], 1)
    near = [kept + other for kept, other in zip(parts[::2], arrived)]
    across = swap(near, 2)
    mine = [own + other for own, other in zip(near, across)]
    theirs = swap(mine, 1)
    homes, states = [], []
    for chunk in range(count):
        own, *states = absorb(
            chunk, ranks, mine[chunk], theirs[chunk], gain, flat_in, states, flat_back
        )
        homes.append(own)
    middle_out = jnp.concatenate(homes, axis=1)
    expert = states[0].astype(jnp.float32)
    for offset in range(1, exp_count):
        expert = expert + exchange(states[offset], "exp", offset, exp_count).astype(jnp.float32)
    shares = gates / jnp.sum(gates, axis=1, keepdims=True)
    coefficient = jnp.sum(jnp.where(routes == 0, shares, 0.0), axis=1, keepdims=True)
    coefficient = coefficient.astype(jnp.bfloat16).astype(jnp.float32)
    return (middle_out, (expert * coefficient).astype(jnp.bfloat16))


def largest_divisor(row_count):
    candidate = min(row_count, 1024)
    while row_count % candidate != 0:
        candidate = candidate - 1
    return candidate


def apply_slice(row_block, coefficient, w_in, w_back):
    hidden_here = w_back.shape[1]
    flat_in = w_in.reshape(2 * hidden_here, D)
    projected = lax.dot_general(
        row_block, flat_in, (((1,), (1,)), ((), ())), preferred_element_type=jnp.float32
    )
    activated = jax.nn.silu(projected[:, :hidden_here]) * projected[:, hidden_here:]
    blended = (coefficient.astype(jnp.float32) * activated).astype(jnp.bfloat16)
    flat_back = w_back.reshape(hidden_here, D)
    return jnp.dot(blended, flat_back, preferred_element_type=jnp.float32).astype(jnp.bfloat16)


def wide_device(
    queries,
    keys,
    values,
    positions,
    bounds,
    w_out,
    residual,
    norm_gain,
    routes,
    gates,
    w_in,
    w_back,
):
    tok_rows = queries.shape[0]
    head_cols = queries.shape[1]
    heads_here = head_cols // HEAD_DIM
    exp_count = lax.axis_size("exp")
    key_head, value_head = own_heads(queries, keys, values)
    query_heads = queries.reshape(tok_rows, heads_here, HEAD_DIM).transpose(1, 0, 2)
    scale = HEAD_DIM ** (-0.5)
    reach_max = jnp.max(bounds)
    all_keys, all_values, all_places = (
        lax.all_gather(key_head, "ctx", axis=0, tiled=True),
        lax.all_gather(value_head, "ctx", axis=0, tiled=True),
        lax.all_gather(positions, "ctx", axis=0, tiled=True),
    )
    total_rows = all_keys.shape[0]
    tile_len = largest_divisor(total_rows)
    tile_count = total_rows // tile_len

    def process(state_in, key_rows, value_rows, place_rows):
        row_max, row_sum, running = state_in
        scores = (
            jnp.einsum("htd,nd->htn", query_heads, key_rows, preferred_element_type=jnp.float32)
            * scale
        )
        visible = (place_rows[None, :] <= bounds[:, None])[None, :, :]
        masked = jnp.where(visible, scores, -1e30)
        new_max = jnp.maximum(row_max, jnp.max(masked, axis=2))
        weights = jnp.exp(masked - new_max[..., None])
        rescale = jnp.exp(row_max - new_max)
        row_sum = row_sum * rescale + jnp.sum(weights, axis=2)
        running = running * rescale[..., None] + jnp.einsum(
            "htn,nd->htd",
            weights.astype(jnp.bfloat16),
            value_rows,
            preferred_element_type=jnp.float32,
        )
        return (new_max, row_sum, running)

    def one_tile(tile_number, state_now):
        first = tile_number * tile_len
        key_rows = lax.dynamic_slice_in_dim(all_keys, first, tile_len, 0)
        value_rows = lax.dynamic_slice_in_dim(all_values, first, tile_len, 0)
        place_rows = lax.dynamic_slice_in_dim(all_places, first, tile_len, 0)
        return lax.cond(
            jnp.min(place_rows) <= reach_max,
            lambda state_in: process(state_in, key_rows, value_rows, place_rows),
            lambda state_in: state_in,
            state_now,
        )

    start_state = (
        jnp.full((heads_here, tok_rows), -1e30, jnp.float32),
        jnp.zeros((heads_here, tok_rows), jnp.float32),
        jnp.zeros((heads_here, tok_rows, HEAD_DIM), jnp.float32),
    )
    row_max, row_sum, running = lax.fori_loop(0, tile_count, one_tile, start_state)
    attended = (running / row_sum[..., None]).astype(jnp.bfloat16)
    attended = attended.transpose(1, 0, 2).reshape(tok_rows, head_cols)
    attention_rows = lax.psum_scatter(
        jnp.dot(attended, w_out, preferred_element_type=jnp.float32).astype(jnp.bfloat16),
        "exp",
        scatter_dimension=0,
        tiled=True,
    ).astype(jnp.float32)
    middle = (residual.astype(jnp.float32) + attention_rows).astype(jnp.bfloat16)
    wide = middle.astype(jnp.float32)
    mean_square = jnp.mean(wide * wide, axis=1, keepdims=True)
    normed = (wide * lax.rsqrt(mean_square + 1e-06) * norm_gain[None, :]).astype(jnp.bfloat16)
    local_rows = residual.shape[0]
    shares = gates / jnp.sum(gates, axis=1, keepdims=True)
    slice_expert = jnp.arange(exp_count, dtype=jnp.int32) // HID_SPLIT
    hits = routes[:, :, None] == slice_expert[None, None, :]
    coefficient = jnp.sum(jnp.where(hits, shares[:, :, None], 0.0), axis=1).astype(jnp.bfloat16)
    owner_weights = coefficient.transpose(1, 0)[:, :, None]
    copies = jnp.broadcast_to(normed[None, :, :], (exp_count, local_rows, D))
    row_block = lax.all_to_all(copies, "exp", split_axis=0, concat_axis=0, tiled=True)
    weight_block = lax.all_to_all(owner_weights, "exp", split_axis=0, concat_axis=0, tiled=True)
    slot_count = row_block.shape[1]
    produced = apply_slice(
        row_block.reshape(exp_count * slot_count, D),
        weight_block.reshape(exp_count * slot_count, 1),
        w_in,
        w_back,
    )
    produced = produced.reshape(exp_count, slot_count, D)
    arrived = lax.all_to_all(produced, "exp", split_axis=0, concat_axis=0, tiled=True)
    expert_out = jnp.sum(arrived.astype(jnp.float32), axis=0).astype(jnp.bfloat16)
    return (middle, expert_out)


def solution(mesh):
    in_specs = (
        P("ctx", "exp"),
        P("ctx", None),
        P("ctx", None),
        P("ctx"),
        P("ctx"),
        P("exp", None),
        P(("ctx", "exp"), None),
        P(),
        P(("ctx", "exp"), None),
        P(("ctx", "exp"), None),
        P("exp", None, None),
        P("exp", None, None),
    )
    out_specs = (P(("ctx", "exp"), None), P(("ctx", "exp"), None))
    one_line = mesh.shape["exp"] == HID_SPLIT and mesh.shape["ctx"] == 8
    return jax.shard_map(
        line_device if one_line else wide_device,
        mesh=mesh,
        in_specs=in_specs,
        out_specs=out_specs,
        check_vma=False,
    )
```

```python
import functools

import jax
import jax.numpy as jnp
from jax import lax
from jax.experimental import pallas as pl
from jax.experimental.pallas import tpu as pltpu
from jax.sharding import PartitionSpec as P

D = 4096
HEADS = 64
KV_HEADS = 4
HEAD_DIM = 128
HID_SPLIT = 4
STACK = 4
WIDTHS = (1024, 1024, 1024, 1024)
SPANS = tuple((sum(WIDTHS[:i]), width) for i, width in enumerate(WIDTHS))
PAD_ROWS = 16
BASE = 64
IN_FLIGHT = 2
EARLY = 2
LOG2E = 1.4426950408889634
VMEM = pl.BlockSpec(memory_space=pltpu.VMEM)
ANY = pl.BlockSpec(memory_space=pl.ANY)
LIGHT = pl.CostEstimate(flops=1024, bytes_accessed=1024, transcendentals=0)


def exchange(value, axis, offset, size):
    return lax.ppermute(value, axis, [(i, i ^ offset) for i in range(size)])


def start_weights(w_hbm, w_buf, sems, spans):
    copies = []
    for i, (first, width) in enumerate(spans):
        target = pl.ds(first - spans[0][0], width)
        copy = pltpu.make_async_copy(
            w_hbm.at[:, pl.ds(first, width)], w_buf.at[:, target], sems.at[i]
        )
        copy.start()
        copies.append(copy)
    return copies


def attend_kernel(rank_ref, limit_ref, same_ref, other_ref, q_ref, resid_ref, w_hbm, *refs):
    spans = SPANS[:EARLY]
    outs = refs[: 2 * EARLY]
    attended, w_buf, k_buf, v_buf, bias, acc, sems = refs[2 * EARLY :]
    tok = q_ref.shape[0]
    heads = q_ref.shape[1] // HEAD_DIM
    copies = start_weights(w_hbm, w_buf, sems, spans)
    extra = limit_ref[...].astype(jnp.float32)
    bound = extra[:1, :tok] * BASE + extra[:1, tok:]
    bound = jnp.broadcast_to(bound, (tok, tok)).T
    lane = lax.broadcasted_iota(jnp.int32, (1, tok), 1).astype(jnp.float32)
    ones = jnp.ones((tok, HEAD_DIM), jnp.bfloat16)
    block_rows = tok + PAD_ROWS
    half_count = same_ref.shape[0] // block_rows
    for b in range(2 * half_count):
        rows = slice(b * tok, (b + 1) * tok)
        group, row = (same_ref, b) if b < half_count else (other_ref, b - half_count)
        top = row * block_rows
        k_buf[rows, :] = group[top : top + tok, :HEAD_DIM]
        v_buf[rows, :HEAD_DIM] = group[top : top + tok, HEAD_DIM:]
        v_buf[rows, HEAD_DIM:] = ones
        start = group[top + tok : top + block_rows, :HEAD_DIM].astype(jnp.float32)[:1]
        place = start * tok + lane
        bias[:, rows] = jnp.where(place <= bound, 0.0, -1e30)
    factor = HEAD_DIM ** (-0.5) * LOG2E

    def some_heads(step, carry):
        base = step * STACK * HEAD_DIM
        parts = []
        for j in range(STACK):
            start = pl.multiple_of(base + j * HEAD_DIM, HEAD_DIM)
            parts.append(q_ref[:, pl.ds(start, HEAD_DIM)])
        stacked = jnp.concatenate(parts, axis=0)
        scores = lax.dot_general(
            stacked, k_buf[...], (((1,), (1,)), ((), ())), preferred_element_type=jnp.float32
        )
        scores = scores.reshape(STACK, tok, -1) * factor + bias[...][None]
        row_max = jnp.max(scores, axis=2, keepdims=True)
        weights = jnp.exp2(scores - row_max).astype(jnp.bfloat16)
        summed = jnp.dot(
            weights.reshape(STACK * tok, -1), v_buf[...], preferred_element_type=jnp.float32
        )
        result = (summed[:, :HEAD_DIM] / summed[:, HEAD_DIM:]).astype(jnp.bfloat16)
        for j in range(STACK):
            start = pl.multiple_of(base + j * HEAD_DIM, HEAD_DIM)
            attended[:, pl.ds(start, HEAD_DIM)] = result[j * tok : (j + 1) * tok]
        return carry

    lax.fori_loop(0, heads // STACK, some_heads, 0, unroll=True)
    project_spans(spans, copies, rank_ref[0], attended, w_buf, resid_ref, acc, outs)


def project_spans(spans, copies, rank, attended, w_buf, resid_ref, acc, outs):
    home = resid_ref.shape[0]
    side = rank % 2
    kept = [pl.multiple_of((side + 2 * i) * home, home) for i in range(2)]
    leaving = [pl.multiple_of((1 - side + 2 * i) * home, home) for i in range(2)]
    top = pl.multiple_of(rank * home, home)
    for chunk, (first, width) in enumerate(spans):
        copies[chunk].wait()
        span = slice(first - spans[0][0], first - spans[0][0] + width)
        acc[:, span] = jnp.dot(
            attended[...], w_buf[:, span], preferred_element_type=jnp.float32
        )
        acc[pl.ds(top, home), span] += resid_ref[:, first : first + width].astype(jnp.float32)
        for i in range(2):
            rows = slice(i * home, (i + 1) * home)
            outs[2 * chunk][rows, :] = acc[pl.ds(kept[i], home), span].astype(jnp.bfloat16)
            outs[2 * chunk + 1][rows, :] = acc[pl.ds(leaving[i], home), span].astype(
                jnp.bfloat16
            )


def part_shapes(tok, spans):
    return [
        jax.ShapeDtypeStruct((tok // 2, width), jnp.bfloat16) for _, width in spans for _ in range(2)
    ]


def attend_project(rank, limits, same, other, queries, residual, w_out):
    tok, width = queries.shape
    keys_in_all = 2 * same.shape[0] // (tok + PAD_ROWS) * tok
    spans = SPANS[:EARLY]
    columns = sum(w for _, w in spans)
    return pl.pallas_call(
        attend_kernel,
        out_shape=part_shapes(tok, spans) + [jax.ShapeDtypeStruct((tok, width), jnp.bfloat16)],
        in_specs=[pl.BlockSpec(memory_space=pltpu.SMEM)] + [VMEM] * 5 + [ANY],
        out_specs=[VMEM] * (2 * len(spans) + 1),
        scratch_shapes=[
            pltpu.VMEM((width, columns), jnp.bfloat16),
            pltpu.VMEM((keys_in_all, HEAD_DIM), jnp.bfloat16),
            pltpu.VMEM((keys_in_all, 2 * HEAD_DIM), jnp.bfloat16),
            pltpu.VMEM((tok, keys_in_all), jnp.float32),
            pltpu.VMEM((tok, columns), jnp.float32),
            pltpu.SemaphoreType.DMA((len(spans),)),
        ],
        compiler_params=pltpu.CompilerParams(vmem_limit_bytes=48 * 1024 * 1024),
        cost_estimate=pl.CostEstimate(
            flops=2 * tok * width * (2 * keys_in_all + columns),
            bytes_accessed=2 * width * columns,
            transcendentals=tok * width // HEAD_DIM * keys_in_all,
        ),
        name="attend_project",
    )(rank, limits, same, other, queries, residual, w_out)


def project_kernel(rank_ref, attended, resid_ref, w_hbm, *refs):
    spans = SPANS[EARLY:]
    outs = refs[: 2 * len(spans)]
    w_buf, acc, sems = refs[2 * len(spans) :]
    copies = start_weights(w_hbm, w_buf, sems, spans)
    project_spans(spans, copies, rank_ref[0], attended, w_buf, resid_ref, acc, outs)


def project(rank, attended, residual, w_out):
    tok, width = attended.shape
    spans = SPANS[EARLY:]
    columns = sum(w for _, w in spans)
    return pl.pallas_call(
        project_kernel,
        out_shape=part_shapes(tok, spans),
        in_specs=[pl.BlockSpec(memory_space=pltpu.SMEM)] + [VMEM] * 2 + [ANY],
        out_specs=[VMEM] * (2 * len(spans)),
        scratch_shapes=[
            pltpu.VMEM((width, columns), jnp.bfloat16),
            pltpu.VMEM((tok, columns), jnp.float32),
            pltpu.SemaphoreType.DMA((len(spans),)),
        ],
        compiler_params=pltpu.CompilerParams(vmem_limit_bytes=48 * 1024 * 1024),
        cost_estimate=pl.CostEstimate(
            flops=2 * tok * width * columns,
            bytes_accessed=2 * width * columns,
            transcendentals=0,
        ),
        name="project",
    )(rank, attended, residual, w_out)


def stage_kernel(q_hbm, resid_hbm, q_ref, resid_ref, sems):
    copies = [
        pltpu.make_async_copy(q_hbm, q_ref, sems.at[0]),
        pltpu.make_async_copy(resid_hbm, resid_ref, sems.at[1]),
    ]
    for copy in copies:
        copy.start()
    for copy in copies:
        copy.wait()


def stage(queries, residual):
    arrays = (queries, residual)
    return pl.pallas_call(
        stage_kernel,
        out_shape=[jax.ShapeDtypeStruct(array.shape, array.dtype) for array in arrays],
        in_specs=[ANY, ANY],
        out_specs=[VMEM, VMEM],
        scratch_shapes=[pltpu.SemaphoreType.DMA((2,))],
        compiler_params=pltpu.CompilerParams(vmem_limit_bytes=4 * 1024 * 1024),
        cost_estimate=LIGHT,
        name="stage",
    )(*arrays)


def join_kernel(*refs):
    out_ref = refs[-1]
    first = 0
    for piece in refs[1:-1]:
        rows = piece.shape[0]
        out_ref[first : first + rows, :] = piece[...]
        first += rows


def join_after(pieces, after):
    rows = sum(piece.shape[0] for piece in pieces)
    width = pieces[0].shape[1]
    return pl.pallas_call(
        join_kernel,
        out_shape=jax.ShapeDtypeStruct((rows, width), jnp.bfloat16),
        in_specs=[ANY] + [VMEM] * len(pieces),
        out_specs=VMEM,
        compiler_params=pltpu.CompilerParams(vmem_limit_bytes=8 * 1024 * 1024),
        cost_estimate=LIGHT,
        name="join_after",
    )(after, *pieces)


def absorb_kernel(chunk, rank_ref, mine_ref, theirs_ref, gain_ref, w_ref, *refs):
    last = chunk == len(WIDTHS) - 1
    state_count = 0 if chunk == 0 else 2
    states = refs[:state_count]
    home_ref = refs[state_count + int(last)]
    outs = refs[state_count + int(last) + 1 :]
    first, width = SPANS[chunk]
    span = slice(first, first + width)
    home = home_ref.shape[0]
    place = rank_ref[0] // 2
    home_ref[...] = mine_ref[pl.ds(pl.multiple_of(place * home, home), home), :]
    wide = jnp.concatenate([mine_ref[...], theirs_ref[...]], axis=0).astype(jnp.float32)
    gained = (wide * gain_ref[:, span]).astype(jnp.bfloat16)
    product = lax.dot_general(
        gained, w_ref[:, span], (((1,), (1,)), ((), ())), preferred_element_type=jnp.float32
    )
    square = sum(
        wide[:, i * 128 : (i + 1) * 128] * wide[:, i * 128 : (i + 1) * 128]
        for i in range(width // 128)
    )
    if chunk > 0:
        product += states[0][...]
        square += states[1][...]
    if not last:
        outs[0][...] = product
        outs[1][...] = square
        return
    back_ref = refs[state_count]
    shares, act_buf = outs[:-1], outs[-1]
    hidden = product.shape[1] // 2
    mean_square = jnp.sum(square, axis=1, keepdims=True) / D
    product = product * lax.rsqrt(mean_square + 1e-06)
    gate = product[:, :hidden]
    act_buf[...] = gate / (1.0 + jnp.exp(-gate)) * product[:, hidden:]
    ordered = []
    for offset in range(len(shares)):
        row = (offset % 2) * 2 * home + (place ^ (offset // 2)) * home
        ordered.append(act_buf[pl.ds(pl.multiple_of(row, home), home), :])
    ordered = jnp.concatenate(ordered, axis=0).astype(jnp.bfloat16)
    for part_first, part_width in SPANS:
        part = slice(part_first, part_first + part_width)
        result = jnp.dot(ordered, back_ref[:, part], preferred_element_type=jnp.float32)
        for i, share in enumerate(shares):
            share[:, part] = result[i * home : (i + 1) * home].astype(jnp.bfloat16)


def absorb(chunk, rank, mine, theirs, gain, w_in, states, back):
    half, width = mine.shape
    rows = w_in.shape[0]
    count = lax.axis_size("exp")
    home = 2 * half // count
    out_shape = [jax.ShapeDtypeStruct((home, width), jnp.bfloat16)]
    scratch = []
    operands = [rank, mine, theirs, gain, w_in, *states]
    if chunk == len(WIDTHS) - 1:
        operands.append(back)
        out_shape += [jax.ShapeDtypeStruct((home, D), jnp.bfloat16)] * count
        scratch = [pltpu.VMEM((2 * half, rows // 2), jnp.float32)]
    else:
        out_shape += [
            jax.ShapeDtypeStruct((2 * half, rows), jnp.float32),
            jax.ShapeDtypeStruct((2 * half, 128), jnp.float32),
        ]
    return pl.pallas_call(
        functools.partial(absorb_kernel, chunk),
        out_shape=out_shape,
        in_specs=[pl.BlockSpec(memory_space=pltpu.SMEM)] + [VMEM] * (len(operands) - 1),
        out_specs=[VMEM] * len(out_shape),
        scratch_shapes=scratch,
        compiler_params=pltpu.CompilerParams(vmem_limit_bytes=16 * 1024 * 1024),
        cost_estimate=LIGHT,
        name="absorb",
    )(*operands)


def own_heads(queries, keys, values):
    heads_here = queries.shape[1] // HEAD_DIM
    kv_number = lax.axis_index("exp") * heads_here // (HEADS // KV_HEADS)
    key_head = lax.dynamic_slice_in_dim(keys, kv_number * HEAD_DIM, HEAD_DIM, 1)
    value_head = lax.dynamic_slice_in_dim(values, kv_number * HEAD_DIM, HEAD_DIM, 1)
    return key_head, value_head


def line_device(
    queries,
    keys,
    values,
    positions,
    bounds,
    w_out,
    residual,
    norm_gain,
    routes,
    gates,
    w_in,
    w_back,
):
    tok = queries.shape[0]
    home = residual.shape[0]
    hidden = w_back.shape[1]
    ctx_count = lax.axis_size("ctx")
    exp_count = lax.axis_size("exp")
    rank = lax.axis_index("exp")
    key_head, value_head = own_heads(queries, keys, values)
    staged_queries, staged_residual = stage(queries, residual)
    block = (positions[0] // tok).astype(jnp.bfloat16)
    width = 2 * HEAD_DIM
    payload = jnp.concatenate(
        [
            jnp.concatenate([key_head, value_head], axis=1),
            jnp.full((PAD_ROWS, width), block, jnp.bfloat16),
        ],
        axis=0,
    )
    limits = jnp.concatenate([bounds // BASE, bounds % BASE]).astype(jnp.bfloat16)
    limits = jnp.broadcast_to(limits.reshape(1, width), (PAD_ROWS, width))
    same_keys = join_after(
        [payload] + [exchange(payload, "ctx", r, ctx_count) for r in range(2, ctx_count, 2)],
        payload,
    )
    other_keys = exchange(same_keys, "ctx", 1, ctx_count)

    ranks = rank.astype(jnp.int32).reshape(1)
    *parts, attended = attend_project(
        ranks, limits, same_keys, other_keys, staged_queries, staged_residual, w_out
    )
    parts += project(ranks, attended, staged_residual, w_out)
    shares = gates / jnp.sum(gates, axis=1, keepdims=True)
    coefficient = jnp.sum(jnp.where(routes == 0, shares, 0.0), axis=1, keepdims=True)
    coefficient = coefficient.astype(jnp.bfloat16).astype(jnp.float32)
    gain = norm_gain.reshape(1, D)
    flat_in = w_in.reshape(2 * hidden, D)
    flat_back = w_back.reshape(hidden, D)
    count = len(WIDTHS)

    def swap(values, offset):
        results = []
        for i, value in enumerate(values):
            if i >= IN_FLIGHT:
                value, _ = lax.optimization_barrier((value, results[i - IN_FLIGHT]))
            results.append(exchange(value, "exp", offset, exp_count))
        return results

    arrived = swap(parts[1::2], 1)
    near = [kept + other for kept, other in zip(parts[::2], arrived)]
    across = swap(near, 2)
    mine = [own + other for own, other in zip(near, across)]
    homes, states, theirs, done = [], [], [], [coefficient]
    for chunk in range(count):
        value = mine[chunk]
        if chunk >= IN_FLIGHT:
            own, *states = absorb(
                chunk - IN_FLIGHT,
                ranks,
                mine[chunk - IN_FLIGHT],
                theirs[chunk - IN_FLIGHT],
                gain,
                flat_in,
                states,
                flat_back,
            )
            homes.append(own)
            done = [states[0]]
        if chunk >= IN_FLIGHT or chunk == 1:
            value, *done = lax.optimization_barrier((value, *done))
            if chunk == 1:
                coefficient = done[0]
            else:
                states[0] = done[0]
        theirs.append(exchange(value, "exp", 1, exp_count))
    for chunk in range(count - IN_FLIGHT, count):
        own, *states = absorb(
            chunk, ranks, mine[chunk], theirs[chunk], gain, flat_in, states, flat_back
        )
        homes.append(own)
    middle_out = jnp.concatenate(homes, axis=1)
    expert = states[0].astype(jnp.float32)
    for offset in range(1, exp_count):
        expert = expert + exchange(states[offset], "exp", offset, exp_count).astype(jnp.float32)
    return (middle_out, (expert * coefficient).astype(jnp.bfloat16))


def largest_divisor(row_count):
    candidate = min(row_count, 1024)
    while row_count % candidate != 0:
        candidate = candidate - 1
    return candidate


def apply_slice(row_block, coefficient, w_in, w_back):
    hidden_here = w_back.shape[1]
    flat_in = w_in.reshape(2 * hidden_here, D)
    projected = lax.dot_general(
        row_block, flat_in, (((1,), (1,)), ((), ())), preferred_element_type=jnp.float32
    )
    activated = jax.nn.silu(projected[:, :hidden_here]) * projected[:, hidden_here:]
    blended = (coefficient.astype(jnp.float32) * activated).astype(jnp.bfloat16)
    flat_back = w_back.reshape(hidden_here, D)
    return jnp.dot(blended, flat_back, preferred_element_type=jnp.float32).astype(jnp.bfloat16)


def wide_device(
    queries,
    keys,
    values,
    positions,
    bounds,
    w_out,
    residual,
    norm_gain,
    routes,
    gates,
    w_in,
    w_back,
):
    tok_rows = queries.shape[0]
    head_cols = queries.shape[1]
    heads_here = head_cols // HEAD_DIM
    exp_count = lax.axis_size("exp")
    key_head, value_head = own_heads(queries, keys, values)
    query_heads = queries.reshape(tok_rows, heads_here, HEAD_DIM).transpose(1, 0, 2)
    scale = HEAD_DIM ** (-0.5)
    reach_max = jnp.max(bounds)
    all_keys, all_values, all_places = (
        lax.all_gather(key_head, "ctx", axis=0, tiled=True),
        lax.all_gather(value_head, "ctx", axis=0, tiled=True),
        lax.all_gather(positions, "ctx", axis=0, tiled=True),
    )
    total_rows = all_keys.shape[0]
    tile_len = largest_divisor(total_rows)
    tile_count = total_rows // tile_len

    def process(state_in, key_rows, value_rows, place_rows):
        row_max, row_sum, running = state_in
        scores = (
            jnp.einsum("htd,nd->htn", query_heads, key_rows, preferred_element_type=jnp.float32)
            * scale
        )
        visible = (place_rows[None, :] <= bounds[:, None])[None, :, :]
        masked = jnp.where(visible, scores, -1e30)
        new_max = jnp.maximum(row_max, jnp.max(masked, axis=2))
        weights = jnp.exp(masked - new_max[..., None])
        rescale = jnp.exp(row_max - new_max)
        row_sum = row_sum * rescale + jnp.sum(weights, axis=2)
        running = running * rescale[..., None] + jnp.einsum(
            "htn,nd->htd",
            weights.astype(jnp.bfloat16),
            value_rows,
            preferred_element_type=jnp.float32,
        )
        return (new_max, row_sum, running)

    def one_tile(tile_number, state_now):
        first = tile_number * tile_len
        key_rows = lax.dynamic_slice_in_dim(all_keys, first, tile_len, 0)
        value_rows = lax.dynamic_slice_in_dim(all_values, first, tile_len, 0)
        place_rows = lax.dynamic_slice_in_dim(all_places, first, tile_len, 0)
        return lax.cond(
            jnp.min(place_rows) <= reach_max,
            lambda state_in: process(state_in, key_rows, value_rows, place_rows),
            lambda state_in: state_in,
            state_now,
        )

    start_state = (
        jnp.full((heads_here, tok_rows), -1e30, jnp.float32),
        jnp.zeros((heads_here, tok_rows), jnp.float32),
        jnp.zeros((heads_here, tok_rows, HEAD_DIM), jnp.float32),
    )
    row_max, row_sum, running = lax.fori_loop(0, tile_count, one_tile, start_state)
    attended = (running / row_sum[..., None]).astype(jnp.bfloat16)
    attended = attended.transpose(1, 0, 2).reshape(tok_rows, head_cols)
    attention_rows = lax.psum_scatter(
        jnp.dot(attended, w_out, preferred_element_type=jnp.float32).astype(jnp.bfloat16),
        "exp",
        scatter_dimension=0,
        tiled=True,
    ).astype(jnp.float32)
    middle = (residual.astype(jnp.float32) + attention_rows).astype(jnp.bfloat16)
    wide = middle.astype(jnp.float32)
    mean_square = jnp.mean(wide * wide, axis=1, keepdims=True)
    normed = (wide * lax.rsqrt(mean_square + 1e-06) * norm_gain[None, :]).astype(jnp.bfloat16)
    local_rows = residual.shape[0]
    shares = gates / jnp.sum(gates, axis=1, keepdims=True)
    slice_expert = jnp.arange(exp_count, dtype=jnp.int32) // HID_SPLIT
    hits = routes[:, :, None] == slice_expert[None, None, :]
    coefficient = jnp.sum(jnp.where(hits, shares[:, :, None], 0.0), axis=1).astype(jnp.bfloat16)
    owner_weights = coefficient.transpose(1, 0)[:, :, None]
    copies = jnp.broadcast_to(normed[None, :, :], (exp_count, local_rows, D))
    row_block = lax.all_to_all(copies, "exp", split_axis=0, concat_axis=0, tiled=True)
    weight_block = lax.all_to_all(owner_weights, "exp", split_axis=0, concat_axis=0, tiled=True)
    slot_count = row_block.shape[1]
    produced = apply_slice(
        row_block.reshape(exp_count * slot_count, D),
        weight_block.reshape(exp_count * slot_count, 1),
        w_in,
        w_back,
    )
    produced = produced.reshape(exp_count, slot_count, D)
    arrived = lax.all_to_all(produced, "exp", split_axis=0, concat_axis=0, tiled=True)
    expert_out = jnp.sum(arrived.astype(jnp.float32), axis=0).astype(jnp.bfloat16)
    return (middle, expert_out)


def solution(mesh):
    in_specs = (
        P("ctx", "exp"),
        P("ctx", None),
        P("ctx", None),
        P("ctx"),
        P("ctx"),
        P("exp", None),
        P(("ctx", "exp"), None),
        P(),
        P(("ctx", "exp"), None),
        P(("ctx", "exp"), None),
        P("exp", None, None),
        P("exp", None, None),
    )
    out_specs = (P(("ctx", "exp"), None), P(("ctx", "exp"), None))
    one_line = mesh.shape["exp"] == HID_SPLIT and mesh.shape["ctx"] == 8
    return jax.shard_map(
        line_device if one_line else wide_device,
        mesh=mesh,
        in_specs=in_specs,
        out_specs=out_specs,
        check_vma=False,
    )
```

```python
import functools

import jax
import jax.numpy as jnp
from jax import lax
from jax.experimental import pallas as pl
from jax.experimental.pallas import tpu as pltpu
from jax.sharding import PartitionSpec as P

D = 4096
HEADS = 64
KV_HEADS = 4
HEAD_DIM = 128
HID_SPLIT = 4
STACK = 4
WIDTHS = (1024, 1024, 1024, 1024)
SPANS = tuple((sum(WIDTHS[:i]), width) for i, width in enumerate(WIDTHS))
PAD_ROWS = 16
BASE = 64
IN_FLIGHT = 2
EARLY = 2
XY_START = 0
XY_NEXT = 3
XY_LAST = 2
ADD_ORDER = (
    ("near", 0),
    ("near", 1),
    ("mine", 0),
    ("near", 2),
    ("mine", 1),
    ("near", 3),
    ("mine", 2),
    ("mine", 3),
)
LOG2E = 1.4426950408889634
VMEM = pl.BlockSpec(memory_space=pltpu.VMEM)
ANY = pl.BlockSpec(memory_space=pl.ANY)
LIGHT = pl.CostEstimate(flops=1024, bytes_accessed=1024, transcendentals=0)


def exchange(value, axis, offset, size):
    return lax.ppermute(value, axis, [(i, i ^ offset) for i in range(size)])


def start_weights(w_hbm, w_buf, sems, spans):
    copies = []
    for i, (first, width) in enumerate(spans):
        target = pl.ds(first - spans[0][0], width)
        copy = pltpu.make_async_copy(
            w_hbm.at[:, pl.ds(first, width)], w_buf.at[:, target], sems.at[i]
        )
        copy.start()
        copies.append(copy)
    return copies


def attend_kernel(rank_ref, limit_ref, same_ref, other_ref, q_ref, resid_ref, w_hbm, *refs):
    spans = SPANS[:EARLY]
    outs = refs[: 2 * EARLY]
    attended, w_buf, k_buf, v_buf, bias, acc, sems = refs[2 * EARLY :]
    tok = q_ref.shape[0]
    heads = q_ref.shape[1] // HEAD_DIM
    copies = start_weights(w_hbm, w_buf, sems, spans)
    extra = limit_ref[...].astype(jnp.float32)
    bound = extra[:1, :tok] * BASE + extra[:1, tok:]
    bound = jnp.broadcast_to(bound, (tok, tok)).T
    lane = lax.broadcasted_iota(jnp.int32, (1, tok), 1).astype(jnp.float32)
    ones = jnp.ones((tok, HEAD_DIM), jnp.bfloat16)
    block_rows = tok + PAD_ROWS
    half_count = same_ref.shape[0] // block_rows
    for b in range(2 * half_count):
        rows = slice(b * tok, (b + 1) * tok)
        group, row = (same_ref, b) if b < half_count else (other_ref, b - half_count)
        top = row * block_rows
        k_buf[rows, :] = group[top : top + tok, :HEAD_DIM]
        v_buf[rows, :HEAD_DIM] = group[top : top + tok, HEAD_DIM:]
        v_buf[rows, HEAD_DIM:] = ones
        start = group[top + tok : top + block_rows, :HEAD_DIM].astype(jnp.float32)[:1]
        place = start * tok + lane
        bias[:, rows] = jnp.where(place <= bound, 0.0, -1e30)
    factor = HEAD_DIM ** (-0.5) * LOG2E

    def some_heads(step, carry):
        base = step * STACK * HEAD_DIM
        parts = []
        for j in range(STACK):
            start = pl.multiple_of(base + j * HEAD_DIM, HEAD_DIM)
            parts.append(q_ref[:, pl.ds(start, HEAD_DIM)])
        stacked = jnp.concatenate(parts, axis=0)
        scores = lax.dot_general(
            stacked, k_buf[...], (((1,), (1,)), ((), ())), preferred_element_type=jnp.float32
        )
        scores = scores.reshape(STACK, tok, -1) * factor + bias[...][None]
        row_max = jnp.max(scores, axis=2, keepdims=True)
        weights = jnp.exp2(scores - row_max).astype(jnp.bfloat16)
        summed = jnp.dot(
            weights.reshape(STACK * tok, -1), v_buf[...], preferred_element_type=jnp.float32
        )
        result = (summed[:, :HEAD_DIM] / summed[:, HEAD_DIM:]).astype(jnp.bfloat16)
        for j in range(STACK):
            start = pl.multiple_of(base + j * HEAD_DIM, HEAD_DIM)
            attended[:, pl.ds(start, HEAD_DIM)] = result[j * tok : (j + 1) * tok]
        return carry

    lax.fori_loop(0, heads // STACK, some_heads, 0, unroll=True)
    project_spans(spans, copies, rank_ref[0], attended, w_buf, resid_ref, acc, outs)


def project_spans(spans, copies, rank, attended, w_buf, resid_ref, acc, outs):
    home = resid_ref.shape[0]
    side = rank % 2
    kept = [pl.multiple_of((side + 2 * i) * home, home) for i in range(2)]
    leaving = [pl.multiple_of((1 - side + 2 * i) * home, home) for i in range(2)]
    top = pl.multiple_of(rank * home, home)
    for chunk, (first, width) in enumerate(spans):
        copies[chunk].wait()
        span = slice(first - spans[0][0], first - spans[0][0] + width)
        acc[:, span] = jnp.dot(
            attended[...], w_buf[:, span], preferred_element_type=jnp.float32
        )
        acc[pl.ds(top, home), span] += resid_ref[:, first : first + width].astype(jnp.float32)
        for i in range(2):
            rows = slice(i * home, (i + 1) * home)
            outs[2 * chunk][rows, :] = acc[pl.ds(kept[i], home), span].astype(jnp.bfloat16)
            outs[2 * chunk + 1][rows, :] = acc[pl.ds(leaving[i], home), span].astype(
                jnp.bfloat16
            )


def part_shapes(tok, spans):
    return [
        jax.ShapeDtypeStruct((tok // 2, width), jnp.bfloat16) for _, width in spans for _ in range(2)
    ]


def attend_project(rank, limits, same, other, queries, residual, w_out):
    tok, width = queries.shape
    keys_in_all = 2 * same.shape[0] // (tok + PAD_ROWS) * tok
    spans = SPANS[:EARLY]
    columns = sum(w for _, w in spans)
    return pl.pallas_call(
        attend_kernel,
        out_shape=part_shapes(tok, spans) + [jax.ShapeDtypeStruct((tok, width), jnp.bfloat16)],
        in_specs=[pl.BlockSpec(memory_space=pltpu.SMEM)] + [VMEM] * 5 + [ANY],
        out_specs=[VMEM] * (2 * len(spans) + 1),
        scratch_shapes=[
            pltpu.VMEM((width, columns), jnp.bfloat16),
            pltpu.VMEM((keys_in_all, HEAD_DIM), jnp.bfloat16),
            pltpu.VMEM((keys_in_all, 2 * HEAD_DIM), jnp.bfloat16),
            pltpu.VMEM((tok, keys_in_all), jnp.float32),
            pltpu.VMEM((tok, columns), jnp.float32),
            pltpu.SemaphoreType.DMA((len(spans),)),
        ],
        compiler_params=pltpu.CompilerParams(vmem_limit_bytes=48 * 1024 * 1024),
        cost_estimate=pl.CostEstimate(
            flops=2 * tok * width * (2 * keys_in_all + columns),
            bytes_accessed=2 * width * columns,
            transcendentals=tok * width // HEAD_DIM * keys_in_all,
        ),
        name="attend_project",
    )(rank, limits, same, other, queries, residual, w_out)


def project_kernel(rank_ref, attended, resid_ref, w_hbm, *refs):
    spans = SPANS[EARLY:]
    outs = refs[: 2 * len(spans)]
    w_buf, acc, sems = refs[2 * len(spans) :]
    copies = start_weights(w_hbm, w_buf, sems, spans)
    project_spans(spans, copies, rank_ref[0], attended, w_buf, resid_ref, acc, outs)


def project(rank, attended, residual, w_out):
    tok, width = attended.shape
    spans = SPANS[EARLY:]
    columns = sum(w for _, w in spans)
    return pl.pallas_call(
        project_kernel,
        out_shape=part_shapes(tok, spans),
        in_specs=[pl.BlockSpec(memory_space=pltpu.SMEM)] + [VMEM] * 2 + [ANY],
        out_specs=[VMEM] * (2 * len(spans)),
        scratch_shapes=[
            pltpu.VMEM((width, columns), jnp.bfloat16),
            pltpu.VMEM((tok, columns), jnp.float32),
            pltpu.SemaphoreType.DMA((len(spans),)),
        ],
        compiler_params=pltpu.CompilerParams(vmem_limit_bytes=48 * 1024 * 1024),
        cost_estimate=pl.CostEstimate(
            flops=2 * tok * width * columns,
            bytes_accessed=2 * width * columns,
            transcendentals=0,
        ),
        name="project",
    )(rank, attended, residual, w_out)


def stage_kernel(q_hbm, resid_hbm, q_ref, resid_ref, sems):
    copies = [
        pltpu.make_async_copy(q_hbm, q_ref, sems.at[0]),
        pltpu.make_async_copy(resid_hbm, resid_ref, sems.at[1]),
    ]
    for copy in copies:
        copy.start()
    for copy in copies:
        copy.wait()


def stage(queries, residual):
    arrays = (queries, residual)
    return pl.pallas_call(
        stage_kernel,
        out_shape=[jax.ShapeDtypeStruct(array.shape, array.dtype) for array in arrays],
        in_specs=[ANY, ANY],
        out_specs=[VMEM, VMEM],
        scratch_shapes=[pltpu.SemaphoreType.DMA((2,))],
        compiler_params=pltpu.CompilerParams(vmem_limit_bytes=4 * 1024 * 1024),
        cost_estimate=LIGHT,
        name="stage",
    )(*arrays)


def join_kernel(*refs):
    out_ref = refs[-1]
    first = 0
    for piece in refs[1:-1]:
        rows = piece.shape[0]
        out_ref[first : first + rows, :] = piece[...]
        first += rows


def join_after(pieces, after):
    rows = sum(piece.shape[0] for piece in pieces)
    width = pieces[0].shape[1]
    return pl.pallas_call(
        join_kernel,
        out_shape=jax.ShapeDtypeStruct((rows, width), jnp.bfloat16),
        in_specs=[ANY] + [VMEM] * len(pieces),
        out_specs=VMEM,
        compiler_params=pltpu.CompilerParams(vmem_limit_bytes=8 * 1024 * 1024),
        cost_estimate=LIGHT,
        name="join_after",
    )(after, *pieces)


def shard_kernel(place_ref, in_hbm, back_hbm, out_ref, sems):
    width = out_ref.shape[1]
    rows = in_hbm.shape[0]
    span = pl.ds(pl.multiple_of(place_ref[1] * width, width), width)
    copies = [
        pltpu.make_async_copy(in_hbm.at[:, span], out_ref.at[:rows], sems.at[0]),
        pltpu.make_async_copy(back_hbm.at[:, span], out_ref.at[rows:], sems.at[1]),
    ]
    for copy in copies:
        copy.start()
    for copy in copies:
        copy.wait()


def make_shard(places, w_in, w_back, width):
    rows = w_in.shape[0] + w_back.shape[0]
    return pl.pallas_call(
        shard_kernel,
        out_shape=jax.ShapeDtypeStruct((rows, width), jnp.bfloat16),
        in_specs=[pl.BlockSpec(memory_space=pltpu.SMEM), ANY, ANY],
        out_specs=VMEM,
        scratch_shapes=[pltpu.SemaphoreType.DMA((2,))],
        compiler_params=pltpu.CompilerParams(vmem_limit_bytes=60 * 1024 * 1024),
        cost_estimate=LIGHT,
        name="make_shard",
    )(places, w_in, w_back)


def expert_kernel(place_ref, gain_ref, in_ref, back_ref, *refs):
    count = len(WIDTHS)
    mine = refs[:count]
    groups = (refs[count : count + 2], refs[count + 2 : count + 4])
    home_ref, own_ref, leaving_ref, gained, result = refs[count + 4 :]
    home = home_ref.shape[0]
    index = place_ref[0] // 2
    near_row = pl.multiple_of(index * home, home)
    far_row = pl.multiple_of((1 - index) * home, home)
    rows_in, hidden = in_ref.shape[0], back_ref.shape[0]
    block_rows = rows_in + hidden
    square = 0.0
    for (first, width), part in zip(SPANS, mine):
        span = slice(first, first + width)
        home_ref[:, span] = part[pl.ds(near_row, home), :]
        wide = part[...].astype(jnp.float32)
        for i in range(width // 128):
            piece = wide[:, i * 128 : (i + 1) * 128]
            square = square + piece * piece
        gained[:, span] = (wide * gain_ref[:, span]).astype(jnp.bfloat16)
    scale = lax.rsqrt(jnp.sum(square, axis=1, keepdims=True) / D + 1e-06)
    blocks = []
    for g, (three, one) in enumerate(groups):
        shard = three.shape[1]
        for j in range(4):
            buf, top = (three, j * block_rows) if j < 3 else (one, 0)
            cols = pl.multiple_of((place_ref[1] ^ (2 * j + g)) * shard, shard)
            blocks.append((buf, top, pl.ds(cols, shard)))
    contract = (((1,), (1,)), ((), ()))
    product = lax.dot_general(
        gained[...], in_ref[...], contract, preferred_element_type=jnp.float32
    )
    other = jnp.zeros_like(product)
    for buf, top, cols in blocks:
        other += lax.dot_general(
            gained[:, cols],
            buf[top : top + rows_in, :],
            contract,
            preferred_element_type=jnp.float32,
        )

    def activate(value):
        value = value * scale
        gate = value[:, :hidden]
        return (gate / (1.0 + jnp.exp(-gate)) * value[:, hidden:]).astype(jnp.bfloat16)

    act, act_other = activate(product), activate(other)
    for buf, top, cols in blocks:
        result[:, cols] = jnp.dot(
            act, back_ref[:, cols], preferred_element_type=jnp.float32
        ) + jnp.dot(
            act_other,
            buf[top + rows_in : top + block_rows, :],
            preferred_element_type=jnp.float32,
        )
    own_ref[...] = result[pl.ds(near_row, home), :]
    leaving_ref[...] = result[pl.ds(far_row, home), :].astype(jnp.bfloat16)


def experts(places, gain, w_in, w_back, mine, weights):
    half = mine[0].shape[0]
    operands = [places, gain, w_in, w_back, *mine, *weights]
    return pl.pallas_call(
        expert_kernel,
        out_shape=[
            jax.ShapeDtypeStruct((half // 2, D), jnp.bfloat16),
            jax.ShapeDtypeStruct((half // 2, D), jnp.float32),
            jax.ShapeDtypeStruct((half // 2, D), jnp.bfloat16),
        ],
        in_specs=[pl.BlockSpec(memory_space=pltpu.SMEM)] + [VMEM] * (len(operands) - 1),
        out_specs=[VMEM] * 3,
        scratch_shapes=[
            pltpu.VMEM((half, D), jnp.bfloat16),
            pltpu.VMEM((half, D), jnp.float32),
        ],
        compiler_params=pltpu.CompilerParams(vmem_limit_bytes=16 * 1024 * 1024),
        cost_estimate=LIGHT,
        name="experts",
    )(*operands)


def own_heads(queries, keys, values):
    heads_here = queries.shape[1] // HEAD_DIM
    kv_number = lax.axis_index("exp") * heads_here // (HEADS // KV_HEADS)
    key_head = lax.dynamic_slice_in_dim(keys, kv_number * HEAD_DIM, HEAD_DIM, 1)
    value_head = lax.dynamic_slice_in_dim(values, kv_number * HEAD_DIM, HEAD_DIM, 1)
    return key_head, value_head


def line_device(
    queries,
    keys,
    values,
    positions,
    bounds,
    w_out,
    residual,
    norm_gain,
    routes,
    gates,
    w_in,
    w_back,
):
    tok = queries.shape[0]
    home = residual.shape[0]
    hidden = w_back.shape[1]
    ctx_count = lax.axis_size("ctx")
    exp_count = lax.axis_size("exp")
    rank = lax.axis_index("exp")
    key_head, value_head = own_heads(queries, keys, values)
    staged_queries, staged_residual = stage(queries, residual)
    block = (positions[0] // tok).astype(jnp.bfloat16)
    width = 2 * HEAD_DIM
    payload = jnp.concatenate(
        [
            jnp.concatenate([key_head, value_head], axis=1),
            jnp.full((PAD_ROWS, width), block, jnp.bfloat16),
        ],
        axis=0,
    )
    limits = jnp.concatenate([bounds // BASE, bounds % BASE]).astype(jnp.bfloat16)
    limits = jnp.broadcast_to(limits.reshape(1, width), (PAD_ROWS, width))
    same_keys = join_after(
        [payload] + [exchange(payload, "ctx", r, ctx_count) for r in range(2, ctx_count, 2)],
        payload,
    )
    other_keys = exchange(same_keys, "ctx", 1, ctx_count)

    ranks = rank.astype(jnp.int32).reshape(1)
    places = jnp.stack([rank, lax.axis_index("ctx")]).astype(jnp.int32)
    flat_in = w_in.reshape(2 * hidden, D)
    flat_back = w_back.reshape(hidden, D)
    shard = make_shard(places, flat_in, flat_back, D // ctx_count)
    shard = exchange(shard, "exp", 1, exp_count)
    *parts, attended = attend_project(
        ranks, limits, same_keys, other_keys, staged_queries, staged_residual, w_out
    )
    parts += project(ranks, attended, staged_residual, w_out)
    shares = gates / jnp.sum(gates, axis=1, keepdims=True)
    coefficient = jnp.sum(jnp.where(routes == 0, shares, 0.0), axis=1, keepdims=True)
    coefficient = coefficient.astype(jnp.bfloat16).astype(jnp.float32)
    gain = norm_gain.reshape(1, D)

    def swap(values, offset):
        results = []
        for i, value in enumerate(values):
            if i >= IN_FLIGHT:
                value, _ = lax.optimization_barrier((value, results[i - IN_FLIGHT]))
            results.append(exchange(value, "exp", offset, exp_count))
        return results

    arrived = swap(parts[1::2], 1)
    near, across, mine, last = [], [], [], []

    def add_next(left, right):
        if last:
            right, _ = lax.optimization_barrier((right, last[-1]))
        last.append(left + right)
        return last[-1]

    for kind, chunk in ADD_ORDER:
        if kind == "near":
            near.append(add_next(parts[2 * chunk], arrived[chunk]))
            value = near[chunk]
            if chunk >= IN_FLIGHT:
                value, _ = lax.optimization_barrier((value, across[chunk - IN_FLIGHT]))
            across.append(exchange(value, "exp", 2, exp_count))
        else:
            mine.append(add_next(near[chunk], across[chunk]))
    shard, _ = lax.optimization_barrier((shard, near[XY_START]))
    from_x = exchange(shard, "ctx", 2, ctx_count)
    from_y = exchange(shard, "ctx", 4, ctx_count)
    middle_row = shard.shape[0] // 2
    same = join_after([shard, from_x, from_y], near[XY_NEXT])
    upper = exchange(same[shard.shape[0] :][:middle_row], "ctx", 4, ctx_count)
    lower = exchange(same[2 * shard.shape[0] + middle_row :], "ctx", 2, ctx_count)
    other = exchange(same, "ctx", 1, ctx_count)
    corner = join_after([upper, lower], mine[XY_LAST])
    other_corner = exchange(corner, "ctx", 1, ctx_count)
    middle_out, own, leaving = experts(
        places, gain, flat_in, flat_back, mine, [same, corner, other, other_corner]
    )
    expert = own + exchange(leaving, "exp", 2, exp_count).astype(jnp.float32)
    return (middle_out, (expert * coefficient).astype(jnp.bfloat16))


def largest_divisor(row_count):
    candidate = min(row_count, 1024)
    while row_count % candidate != 0:
        candidate = candidate - 1
    return candidate


def apply_slice(row_block, coefficient, w_in, w_back):
    hidden_here = w_back.shape[1]
    flat_in = w_in.reshape(2 * hidden_here, D)
    projected = lax.dot_general(
        row_block, flat_in, (((1,), (1,)), ((), ())), preferred_element_type=jnp.float32
    )
    activated = jax.nn.silu(projected[:, :hidden_here]) * projected[:, hidden_here:]
    blended = (coefficient.astype(jnp.float32) * activated).astype(jnp.bfloat16)
    flat_back = w_back.reshape(hidden_here, D)
    return jnp.dot(blended, flat_back, preferred_element_type=jnp.float32).astype(jnp.bfloat16)


def wide_device(
    queries,
    keys,
    values,
    positions,
    bounds,
    w_out,
    residual,
    norm_gain,
    routes,
    gates,
    w_in,
    w_back,
):
    tok_rows = queries.shape[0]
    head_cols = queries.shape[1]
    heads_here = head_cols // HEAD_DIM
    exp_count = lax.axis_size("exp")
    key_head, value_head = own_heads(queries, keys, values)
    query_heads = queries.reshape(tok_rows, heads_here, HEAD_DIM).transpose(1, 0, 2)
    scale = HEAD_DIM ** (-0.5)
    reach_max = jnp.max(bounds)
    all_keys, all_values, all_places = (
        lax.all_gather(key_head, "ctx", axis=0, tiled=True),
        lax.all_gather(value_head, "ctx", axis=0, tiled=True),
        lax.all_gather(positions, "ctx", axis=0, tiled=True),
    )
    total_rows = all_keys.shape[0]
    tile_len = largest_divisor(total_rows)
    tile_count = total_rows // tile_len

    def process(state_in, key_rows, value_rows, place_rows):
        row_max, row_sum, running = state_in
        scores = (
            jnp.einsum("htd,nd->htn", query_heads, key_rows, preferred_element_type=jnp.float32)
            * scale
        )
        visible = (place_rows[None, :] <= bounds[:, None])[None, :, :]
        masked = jnp.where(visible, scores, -1e30)
        new_max = jnp.maximum(row_max, jnp.max(masked, axis=2))
        weights = jnp.exp(masked - new_max[..., None])
        rescale = jnp.exp(row_max - new_max)
        row_sum = row_sum * rescale + jnp.sum(weights, axis=2)
        running = running * rescale[..., None] + jnp.einsum(
            "htn,nd->htd",
            weights.astype(jnp.bfloat16),
            value_rows,
            preferred_element_type=jnp.float32,
        )
        return (new_max, row_sum, running)

    def one_tile(tile_number, state_now):
        first = tile_number * tile_len
        key_rows = lax.dynamic_slice_in_dim(all_keys, first, tile_len, 0)
        value_rows = lax.dynamic_slice_in_dim(all_values, first, tile_len, 0)
        place_rows = lax.dynamic_slice_in_dim(all_places, first, tile_len, 0)
        return lax.cond(
            jnp.min(place_rows) <= reach_max,
            lambda state_in: process(state_in, key_rows, value_rows, place_rows),
            lambda state_in: state_in,
            state_now,
        )

    start_state = (
        jnp.full((heads_here, tok_rows), -1e30, jnp.float32),
        jnp.zeros((heads_here, tok_rows), jnp.float32),
        jnp.zeros((heads_here, tok_rows, HEAD_DIM), jnp.float32),
    )
    row_max, row_sum, running = lax.fori_loop(0, tile_count, one_tile, start_state)
    attended = (running / row_sum[..., None]).astype(jnp.bfloat16)
    attended = attended.transpose(1, 0, 2).reshape(tok_rows, head_cols)
    attention_rows = lax.psum_scatter(
        jnp.dot(attended, w_out, preferred_element_type=jnp.float32).astype(jnp.bfloat16),
        "exp",
        scatter_dimension=0,
        tiled=True,
    ).astype(jnp.float32)
    middle = (residual.astype(jnp.float32) + attention_rows).astype(jnp.bfloat16)
    wide = middle.astype(jnp.float32)
    mean_square = jnp.mean(wide * wide, axis=1, keepdims=True)
    normed = (wide * lax.rsqrt(mean_square + 1e-06) * norm_gain[None, :]).astype(jnp.bfloat16)
    local_rows = residual.shape[0]
    shares = gates / jnp.sum(gates, axis=1, keepdims=True)
    slice_expert = jnp.arange(exp_count, dtype=jnp.int32) // HID_SPLIT
    hits = routes[:, :, None] == slice_expert[None, None, :]
    coefficient = jnp.sum(jnp.where(hits, shares[:, :, None], 0.0), axis=1).astype(jnp.bfloat16)
    owner_weights = coefficient.transpose(1, 0)[:, :, None]
    copies = jnp.broadcast_to(normed[None, :, :], (exp_count, local_rows, D))
    row_block = lax.all_to_all(copies, "exp", split_axis=0, concat_axis=0, tiled=True)
    weight_block = lax.all_to_all(owner_weights, "exp", split_axis=0, concat_axis=0, tiled=True)
    slot_count = row_block.shape[1]
    produced = apply_slice(
        row_block.reshape(exp_count * slot_count, D),
        weight_block.reshape(exp_count * slot_count, 1),
        w_in,
        w_back,
    )
    produced = produced.reshape(exp_count, slot_count, D)
    arrived = lax.all_to_all(produced, "exp", split_axis=0, concat_axis=0, tiled=True)
    expert_out = jnp.sum(arrived.astype(jnp.float32), axis=0).astype(jnp.bfloat16)
    return (middle, expert_out)


def solution(mesh):
    in_specs = (
        P("ctx", "exp"),
        P("ctx", None),
        P("ctx", None),
        P("ctx"),
        P("ctx"),
        P("exp", None),
        P(("ctx", "exp"), None),
        P(),
        P(("ctx", "exp"), None),
        P(("ctx", "exp"), None),
        P("exp", None, None),
        P("exp", None, None),
    )
    out_specs = (P(("ctx", "exp"), None), P(("ctx", "exp"), None))
    one_line = mesh.shape["exp"] == HID_SPLIT and mesh.shape["ctx"] == 8
    return jax.shard_map(
        line_device if one_line else wide_device,
        mesh=mesh,
        in_specs=in_specs,
        out_specs=out_specs,
        check_vma=False,
    )
```

```python
import functools

import jax
import jax.numpy as jnp
from jax import lax
from jax.experimental import pallas as pl
from jax.experimental.pallas import tpu as pltpu
from jax.sharding import PartitionSpec as P

D = 4096
HEADS = 64
KV_HEADS = 4
HEAD_DIM = 128
HID_SPLIT = 4
STACK = 4
WIDTHS = (1024, 1024, 1024, 1024)
SPANS = tuple((sum(WIDTHS[:i]), width) for i, width in enumerate(WIDTHS))
PAD_ROWS = 16
BASE = 64
IN_FLIGHT = 2
EARLY = 2
ADD_ORDER = (
    ("near", 0),
    ("near", 1),
    ("mine", 0),
    ("near", 2),
    ("mine", 1),
    ("near", 3),
    ("mine", 2),
    ("mine", 3),
)
LOG2E = 1.4426950408889634
VMEM = pl.BlockSpec(memory_space=pltpu.VMEM)
ANY = pl.BlockSpec(memory_space=pl.ANY)
LIGHT = pl.CostEstimate(flops=1024, bytes_accessed=1024, transcendentals=0)


def exchange(value, axis, offset, size):
    return lax.ppermute(value, axis, [(i, i ^ offset) for i in range(size)])


def start_weights(w_hbm, w_buf, sems, spans):
    copies = []
    for i, (first, width) in enumerate(spans):
        target = pl.ds(first - spans[0][0], width)
        copy = pltpu.make_async_copy(
            w_hbm.at[:, pl.ds(first, width)], w_buf.at[:, target], sems.at[i]
        )
        copy.start()
        copies.append(copy)
    return copies


def attend_kernel(rank_ref, limit_ref, same_ref, other_ref, q_ref, resid_ref, w_hbm, *refs):
    spans = SPANS[:EARLY]
    outs = refs[: 2 * EARLY]
    attended, w_buf, k_buf, v_buf, bias, acc, sems = refs[2 * EARLY :]
    tok = q_ref.shape[0]
    heads = q_ref.shape[1] // HEAD_DIM
    copies = start_weights(w_hbm, w_buf, sems, spans)
    extra = limit_ref[...].astype(jnp.float32)
    bound = extra[:1, :tok] * BASE + extra[:1, tok:]
    bound = jnp.broadcast_to(bound, (tok, tok)).T
    lane = lax.broadcasted_iota(jnp.int32, (1, tok), 1).astype(jnp.float32)
    ones = jnp.ones((tok, HEAD_DIM), jnp.bfloat16)
    block_rows = tok + PAD_ROWS
    half_count = same_ref.shape[0] // block_rows
    for b in range(2 * half_count):
        rows = slice(b * tok, (b + 1) * tok)
        group, row = (same_ref, b) if b < half_count else (other_ref, b - half_count)
        top = row * block_rows
        k_buf[rows, :] = group[top : top + tok, :HEAD_DIM]
        v_buf[rows, :HEAD_DIM] = group[top : top + tok, HEAD_DIM:]
        v_buf[rows, HEAD_DIM:] = ones
        start = group[top + tok : top + block_rows, :HEAD_DIM].astype(jnp.float32)[:1]
        place = start * tok + lane
        bias[:, rows] = jnp.where(place <= bound, 0.0, -1e30)
    factor = HEAD_DIM ** (-0.5) * LOG2E

    def some_heads(step, carry):
        base = step * STACK * HEAD_DIM
        parts = []
        for j in range(STACK):
            start = pl.multiple_of(base + j * HEAD_DIM, HEAD_DIM)
            parts.append(q_ref[:, pl.ds(start, HEAD_DIM)])
        stacked = jnp.concatenate(parts, axis=0)
        scores = lax.dot_general(
            stacked, k_buf[...], (((1,), (1,)), ((), ())), preferred_element_type=jnp.float32
        )
        scores = scores.reshape(STACK, tok, -1) * factor + bias[...][None]
        row_max = jnp.max(scores, axis=2, keepdims=True)
        weights = jnp.exp2(scores - row_max).astype(jnp.bfloat16)
        summed = jnp.dot(
            weights.reshape(STACK * tok, -1), v_buf[...], preferred_element_type=jnp.float32
        )
        result = (summed[:, :HEAD_DIM] / summed[:, HEAD_DIM:]).astype(jnp.bfloat16)
        for j in range(STACK):
            start = pl.multiple_of(base + j * HEAD_DIM, HEAD_DIM)
            attended[:, pl.ds(start, HEAD_DIM)] = result[j * tok : (j + 1) * tok]
        return carry

    lax.fori_loop(0, heads // STACK, some_heads, 0, unroll=True)
    project_spans(spans, copies, rank_ref[0], attended, w_buf, resid_ref, acc, outs)


def project_spans(spans, copies, rank, attended, w_buf, resid_ref, acc, outs):
    home = resid_ref.shape[0]
    side = rank % 2
    kept = [pl.multiple_of((side + 2 * i) * home, home) for i in range(2)]
    leaving = [pl.multiple_of((1 - side + 2 * i) * home, home) for i in range(2)]
    top = pl.multiple_of(rank * home, home)
    for chunk, (first, width) in enumerate(spans):
        copies[chunk].wait()
        span = slice(first - spans[0][0], first - spans[0][0] + width)
        acc[:, span] = jnp.dot(
            attended[...], w_buf[:, span], preferred_element_type=jnp.float32
        )
        acc[pl.ds(top, home), span] += resid_ref[:, first : first + width].astype(jnp.float32)
        for i in range(2):
            rows = slice(i * home, (i + 1) * home)
            outs[2 * chunk][rows, :] = acc[pl.ds(kept[i], home), span].astype(jnp.bfloat16)
            outs[2 * chunk + 1][rows, :] = acc[pl.ds(leaving[i], home), span].astype(
                jnp.bfloat16
            )


def part_shapes(tok, spans):
    return [
        jax.ShapeDtypeStruct((tok // 2, width), jnp.bfloat16) for _, width in spans for _ in range(2)
    ]


def attend_project(rank, limits, same, other, queries, residual, w_out):
    tok, width = queries.shape
    keys_in_all = 2 * same.shape[0] // (tok + PAD_ROWS) * tok
    spans = SPANS[:EARLY]
    columns = sum(w for _, w in spans)
    return pl.pallas_call(
        attend_kernel,
        out_shape=part_shapes(tok, spans) + [jax.ShapeDtypeStruct((tok, width), jnp.bfloat16)],
        in_specs=[pl.BlockSpec(memory_space=pltpu.SMEM)] + [VMEM] * 5 + [ANY],
        out_specs=[VMEM] * (2 * len(spans) + 1),
        scratch_shapes=[
            pltpu.VMEM((width, columns), jnp.bfloat16),
            pltpu.VMEM((keys_in_all, HEAD_DIM), jnp.bfloat16),
            pltpu.VMEM((keys_in_all, 2 * HEAD_DIM), jnp.bfloat16),
            pltpu.VMEM((tok, keys_in_all), jnp.float32),
            pltpu.VMEM((tok, columns), jnp.float32),
            pltpu.SemaphoreType.DMA((len(spans),)),
        ],
        compiler_params=pltpu.CompilerParams(vmem_limit_bytes=48 * 1024 * 1024),
        cost_estimate=pl.CostEstimate(
            flops=2 * tok * width * (2 * keys_in_all + columns),
            bytes_accessed=2 * width * columns,
            transcendentals=tok * width // HEAD_DIM * keys_in_all,
        ),
        name="attend_project",
    )(rank, limits, same, other, queries, residual, w_out)


def project_kernel(rank_ref, attended, resid_ref, w_hbm, *refs):
    spans = SPANS[EARLY:]
    outs = refs[: 2 * len(spans)]
    w_buf, acc, sems = refs[2 * len(spans) :]
    copies = start_weights(w_hbm, w_buf, sems, spans)
    project_spans(spans, copies, rank_ref[0], attended, w_buf, resid_ref, acc, outs)


def project(rank, attended, residual, w_out):
    tok, width = attended.shape
    spans = SPANS[EARLY:]
    columns = sum(w for _, w in spans)
    return pl.pallas_call(
        project_kernel,
        out_shape=part_shapes(tok, spans),
        in_specs=[pl.BlockSpec(memory_space=pltpu.SMEM)] + [VMEM] * 2 + [ANY],
        out_specs=[VMEM] * (2 * len(spans)),
        scratch_shapes=[
            pltpu.VMEM((width, columns), jnp.bfloat16),
            pltpu.VMEM((tok, columns), jnp.float32),
            pltpu.SemaphoreType.DMA((len(spans),)),
        ],
        compiler_params=pltpu.CompilerParams(vmem_limit_bytes=48 * 1024 * 1024),
        cost_estimate=pl.CostEstimate(
            flops=2 * tok * width * columns,
            bytes_accessed=2 * width * columns,
            transcendentals=0,
        ),
        name="project",
    )(rank, attended, residual, w_out)


def stage_kernel(q_hbm, resid_hbm, q_ref, resid_ref, sems):
    copies = [
        pltpu.make_async_copy(q_hbm, q_ref, sems.at[0]),
        pltpu.make_async_copy(resid_hbm, resid_ref, sems.at[1]),
    ]
    for copy in copies:
        copy.start()
    for copy in copies:
        copy.wait()


def stage(queries, residual):
    arrays = (queries, residual)
    return pl.pallas_call(
        stage_kernel,
        out_shape=[jax.ShapeDtypeStruct(array.shape, array.dtype) for array in arrays],
        in_specs=[ANY, ANY],
        out_specs=[VMEM, VMEM],
        scratch_shapes=[pltpu.SemaphoreType.DMA((2,))],
        compiler_params=pltpu.CompilerParams(vmem_limit_bytes=4 * 1024 * 1024),
        cost_estimate=LIGHT,
        name="stage",
    )(*arrays)


def join_kernel(*refs):
    out_ref = refs[-1]
    first = 0
    for piece in refs[1:-1]:
        rows = piece.shape[0]
        out_ref[first : first + rows, :] = piece[...]
        first += rows


def join_after(pieces, after):
    rows = sum(piece.shape[0] for piece in pieces)
    width = pieces[0].shape[1]
    return pl.pallas_call(
        join_kernel,
        out_shape=jax.ShapeDtypeStruct((rows, width), jnp.bfloat16),
        in_specs=[ANY] + [VMEM] * len(pieces),
        out_specs=VMEM,
        compiler_params=pltpu.CompilerParams(vmem_limit_bytes=8 * 1024 * 1024),
        cost_estimate=LIGHT,
        name="join_after",
    )(after, *pieces)


def shard_kernel(place_ref, in_hbm, back_hbm, out_ref, sems):
    width = out_ref.shape[1]
    rows = in_hbm.shape[0]
    span = pl.ds(pl.multiple_of(place_ref[1] * width, width), width)
    copies = [
        pltpu.make_async_copy(in_hbm.at[:, span], out_ref.at[:rows], sems.at[0]),
        pltpu.make_async_copy(back_hbm.at[:, span], out_ref.at[rows:], sems.at[1]),
    ]
    for copy in copies:
        copy.start()
    for copy in copies:
        copy.wait()


def make_shard(places, w_in, w_back, width):
    rows = w_in.shape[0] + w_back.shape[0]
    return pl.pallas_call(
        shard_kernel,
        out_shape=jax.ShapeDtypeStruct((rows, width), jnp.bfloat16),
        in_specs=[pl.BlockSpec(memory_space=pltpu.SMEM), ANY, ANY],
        out_specs=VMEM,
        scratch_shapes=[pltpu.SemaphoreType.DMA((2,))],
        compiler_params=pltpu.CompilerParams(vmem_limit_bytes=60 * 1024 * 1024),
        cost_estimate=LIGHT,
        name="make_shard",
    )(places, w_in, w_back)


def expert_kernel(place_ref, gain_ref, in_ref, back_ref, *refs):
    count = len(WIDTHS)
    mine = refs[:count]
    groups = (refs[count : count + 2], refs[count + 2 : count + 4])
    home_ref, own_ref, leaving_ref, gained, result = refs[count + 4 :]
    home = home_ref.shape[0]
    index = place_ref[0] // 2
    near_row = pl.multiple_of(index * home, home)
    far_row = pl.multiple_of((1 - index) * home, home)
    rows_in, hidden = in_ref.shape[0], back_ref.shape[0]
    block_rows = rows_in + hidden
    square = 0.0
    for (first, width), part in zip(SPANS, mine):
        span = slice(first, first + width)
        home_ref[:, span] = part[pl.ds(near_row, home), :]
        wide = part[...].astype(jnp.float32)
        for i in range(width // 128):
            piece = wide[:, i * 128 : (i + 1) * 128]
            square = square + piece * piece
        gained[:, span] = (wide * gain_ref[:, span]).astype(jnp.bfloat16)
    scale = lax.rsqrt(jnp.sum(square, axis=1, keepdims=True) / D + 1e-06)
    blocks = []
    for g, (three, one) in enumerate(groups):
        shard = three.shape[1]
        for j in range(4):
            buf, top = (three, j * block_rows) if j < 3 else (one, 0)
            cols = pl.multiple_of((place_ref[1] ^ (2 * j + g)) * shard, shard)
            blocks.append((buf, top, pl.ds(cols, shard)))
    contract = (((1,), (1,)), ((), ()))
    product = lax.dot_general(
        gained[...], in_ref[...], contract, preferred_element_type=jnp.float32
    )
    other = jnp.zeros_like(product)
    for buf, top, cols in blocks:
        other += lax.dot_general(
            gained[:, cols],
            buf[top : top + rows_in, :],
            contract,
            preferred_element_type=jnp.float32,
        )

    def activate(value):
        value = value * scale
        gate = value[:, :hidden]
        return (gate / (1.0 + jnp.exp(-gate)) * value[:, hidden:]).astype(jnp.bfloat16)

    act, act_other = activate(product), activate(other)
    for buf, top, cols in blocks:
        result[:, cols] = jnp.dot(
            act, back_ref[:, cols], preferred_element_type=jnp.float32
        ) + jnp.dot(
            act_other,
            buf[top + rows_in : top + block_rows, :],
            preferred_element_type=jnp.float32,
        )
    own_ref[...] = result[pl.ds(near_row, home), :]
    leaving_ref[...] = result[pl.ds(far_row, home), :].astype(jnp.bfloat16)


def experts(places, gain, w_in, w_back, mine, weights):
    half = mine[0].shape[0]
    operands = [places, gain, w_in, w_back, *mine, *weights]
    return pl.pallas_call(
        expert_kernel,
        out_shape=[
            jax.ShapeDtypeStruct((half // 2, D), jnp.bfloat16),
            jax.ShapeDtypeStruct((half // 2, D), jnp.float32),
            jax.ShapeDtypeStruct((half // 2, D), jnp.bfloat16),
        ],
        in_specs=[pl.BlockSpec(memory_space=pltpu.SMEM)] + [VMEM] * (len(operands) - 1),
        out_specs=[VMEM] * 3,
        scratch_shapes=[
            pltpu.VMEM((half, D), jnp.bfloat16),
            pltpu.VMEM((half, D), jnp.float32),
        ],
        compiler_params=pltpu.CompilerParams(vmem_limit_bytes=16 * 1024 * 1024),
        cost_estimate=LIGHT,
        name="experts",
    )(*operands)


def own_heads(queries, keys, values):
    heads_here = queries.shape[1] // HEAD_DIM
    kv_number = lax.axis_index("exp") * heads_here // (HEADS // KV_HEADS)
    key_head = lax.dynamic_slice_in_dim(keys, kv_number * HEAD_DIM, HEAD_DIM, 1)
    value_head = lax.dynamic_slice_in_dim(values, kv_number * HEAD_DIM, HEAD_DIM, 1)
    return key_head, value_head


def line_device(
    queries,
    keys,
    values,
    positions,
    bounds,
    w_out,
    residual,
    norm_gain,
    routes,
    gates,
    w_in,
    w_back,
):
    tok = queries.shape[0]
    home = residual.shape[0]
    hidden = w_back.shape[1]
    ctx_count = lax.axis_size("ctx")
    exp_count = lax.axis_size("exp")
    rank = lax.axis_index("exp")
    key_head, value_head = own_heads(queries, keys, values)
    staged_queries, staged_residual = stage(queries, residual)
    block = (positions[0] // tok).astype(jnp.bfloat16)
    width = 2 * HEAD_DIM
    payload = jnp.concatenate(
        [
            jnp.concatenate([key_head, value_head], axis=1),
            jnp.full((PAD_ROWS, width), block, jnp.bfloat16),
        ],
        axis=0,
    )
    limits = jnp.concatenate([bounds // BASE, bounds % BASE]).astype(jnp.bfloat16)
    limits = jnp.broadcast_to(limits.reshape(1, width), (PAD_ROWS, width))
    same_keys = join_after(
        [payload] + [exchange(payload, "ctx", r, ctx_count) for r in range(2, ctx_count, 2)],
        payload,
    )
    other_keys = exchange(same_keys, "ctx", 1, ctx_count)

    ranks = rank.astype(jnp.int32).reshape(1)
    places = jnp.stack([rank, lax.axis_index("ctx")]).astype(jnp.int32)
    flat_in = w_in.reshape(2 * hidden, D)
    flat_back = w_back.reshape(hidden, D)
    shard = make_shard(places, flat_in, flat_back, D // ctx_count)
    shard = exchange(shard, "exp", 1, exp_count)
    *parts, attended = attend_project(
        ranks, limits, same_keys, other_keys, staged_queries, staged_residual, w_out
    )
    parts += project(ranks, attended, staged_residual, w_out)
    shares = gates / jnp.sum(gates, axis=1, keepdims=True)
    coefficient = jnp.sum(jnp.where(routes == 0, shares, 0.0), axis=1, keepdims=True)
    coefficient = coefficient.astype(jnp.bfloat16).astype(jnp.float32)
    gain = norm_gain.reshape(1, D)

    def swap(values, offset):
        results = []
        for i, value in enumerate(values):
            if i >= IN_FLIGHT:
                value, _ = lax.optimization_barrier((value, results[i - IN_FLIGHT]))
            results.append(exchange(value, "exp", offset, exp_count))
        return results

    arrived = swap(parts[1::2], 1)
    near, across, mine, last = [], [], [], []

    def add_next(left, right):
        if last:
            right, _ = lax.optimization_barrier((right, last[-1]))
        last.append(left + right)
        return last[-1]

    for kind, chunk in ADD_ORDER:
        if kind == "near":
            near.append(add_next(parts[2 * chunk], arrived[chunk]))
            value = near[chunk]
            if chunk >= IN_FLIGHT:
                value, _ = lax.optimization_barrier((value, across[chunk - IN_FLIGHT]))
            across.append(exchange(value, "exp", 2, exp_count))
        else:
            mine.append(add_next(near[chunk], across[chunk]))
    shard, _ = lax.optimization_barrier((shard, parts[0]))
    from_x = exchange(shard, "ctx", 2, ctx_count)
    from_y = exchange(shard, "ctx", 4, ctx_count)
    middle_row = shard.shape[0] // 2
    same = join_after([shard, from_x, from_y], mine[1])
    upper = exchange(same[shard.shape[0] :][:middle_row], "ctx", 4, ctx_count)
    lower = exchange(same[2 * shard.shape[0] + middle_row :], "ctx", 2, ctx_count)
    crossing, _ = lax.optimization_barrier((same, mine[2]))
    other = exchange(crossing, "ctx", 1, ctx_count)
    corner = join_after([upper, lower], mine[3])
    other_corner = exchange(corner, "ctx", 1, ctx_count)
    middle_out, own, leaving = experts(
        places, gain, flat_in, flat_back, mine, [same, corner, other, other_corner]
    )
    expert = own + exchange(leaving, "exp", 2, exp_count).astype(jnp.float32)
    return (middle_out, (expert * coefficient).astype(jnp.bfloat16))


def largest_divisor(row_count):
    candidate = min(row_count, 1024)
    while row_count % candidate != 0:
        candidate = candidate - 1
    return candidate


def apply_slice(row_block, coefficient, w_in, w_back):
    hidden_here = w_back.shape[1]
    flat_in = w_in.reshape(2 * hidden_here, D)
    projected = lax.dot_general(
        row_block, flat_in, (((1,), (1,)), ((), ())), preferred_element_type=jnp.float32
    )
    activated = jax.nn.silu(projected[:, :hidden_here]) * projected[:, hidden_here:]
    blended = (coefficient.astype(jnp.float32) * activated).astype(jnp.bfloat16)
    flat_back = w_back.reshape(hidden_here, D)
    return jnp.dot(blended, flat_back, preferred_element_type=jnp.float32).astype(jnp.bfloat16)


def wide_device(
    queries,
    keys,
    values,
    positions,
    bounds,
    w_out,
    residual,
    norm_gain,
    routes,
    gates,
    w_in,
    w_back,
):
    tok_rows = queries.shape[0]
    head_cols = queries.shape[1]
    heads_here = head_cols // HEAD_DIM
    exp_count = lax.axis_size("exp")
    key_head, value_head = own_heads(queries, keys, values)
    query_heads = queries.reshape(tok_rows, heads_here, HEAD_DIM).transpose(1, 0, 2)
    scale = HEAD_DIM ** (-0.5)
    reach_max = jnp.max(bounds)
    all_keys, all_values, all_places = (
        lax.all_gather(key_head, "ctx", axis=0, tiled=True),
        lax.all_gather(value_head, "ctx", axis=0, tiled=True),
        lax.all_gather(positions, "ctx", axis=0, tiled=True),
    )
    total_rows = all_keys.shape[0]
    tile_len = largest_divisor(total_rows)
    tile_count = total_rows // tile_len

    def process(state_in, key_rows, value_rows, place_rows):
        row_max, row_sum, running = state_in
        scores = (
            jnp.einsum("htd,nd->htn", query_heads, key_rows, preferred_element_type=jnp.float32)
            * scale
        )
        visible = (place_rows[None, :] <= bounds[:, None])[None, :, :]
        masked = jnp.where(visible, scores, -1e30)
        new_max = jnp.maximum(row_max, jnp.max(masked, axis=2))
        weights = jnp.exp(masked - new_max[..., None])
        rescale = jnp.exp(row_max - new_max)
        row_sum = row_sum * rescale + jnp.sum(weights, axis=2)
        running = running * rescale[..., None] + jnp.einsum(
            "htn,nd->htd",
            weights.astype(jnp.bfloat16),
            value_rows,
            preferred_element_type=jnp.float32,
        )
        return (new_max, row_sum, running)

    def one_tile(tile_number, state_now):
        first = tile_number * tile_len
        key_rows = lax.dynamic_slice_in_dim(all_keys, first, tile_len, 0)
        value_rows = lax.dynamic_slice_in_dim(all_values, first, tile_len, 0)
        place_rows = lax.dynamic_slice_in_dim(all_places, first, tile_len, 0)
        return lax.cond(
            jnp.min(place_rows) <= reach_max,
            lambda state_in: process(state_in, key_rows, value_rows, place_rows),
            lambda state_in: state_in,
            state_now,
        )

    start_state = (
        jnp.full((heads_here, tok_rows), -1e30, jnp.float32),
        jnp.zeros((heads_here, tok_rows), jnp.float32),
        jnp.zeros((heads_here, tok_rows, HEAD_DIM), jnp.float32),
    )
    row_max, row_sum, running = lax.fori_loop(0, tile_count, one_tile, start_state)
    attended = (running / row_sum[..., None]).astype(jnp.bfloat16)
    attended = attended.transpose(1, 0, 2).reshape(tok_rows, head_cols)
    attention_rows = lax.psum_scatter(
        jnp.dot(attended, w_out, preferred_element_type=jnp.float32).astype(jnp.bfloat16),
        "exp",
        scatter_dimension=0,
        tiled=True,
    ).astype(jnp.float32)
    middle = (residual.astype(jnp.float32) + attention_rows).astype(jnp.bfloat16)
    wide = middle.astype(jnp.float32)
    mean_square = jnp.mean(wide * wide, axis=1, keepdims=True)
    normed = (wide * lax.rsqrt(mean_square + 1e-06) * norm_gain[None, :]).astype(jnp.bfloat16)
    local_rows = residual.shape[0]
    shares = gates / jnp.sum(gates, axis=1, keepdims=True)
    slice_expert = jnp.arange(exp_count, dtype=jnp.int32) // HID_SPLIT
    hits = routes[:, :, None] == slice_expert[None, None, :]
    coefficient = jnp.sum(jnp.where(hits, shares[:, :, None], 0.0), axis=1).astype(jnp.bfloat16)
    owner_weights = coefficient.transpose(1, 0)[:, :, None]
    copies = jnp.broadcast_to(normed[None, :, :], (exp_count, local_rows, D))
    row_block = lax.all_to_all(copies, "exp", split_axis=0, concat_axis=0, tiled=True)
    weight_block = lax.all_to_all(owner_weights, "exp", split_axis=0, concat_axis=0, tiled=True)
    slot_count = row_block.shape[1]
    produced = apply_slice(
        row_block.reshape(exp_count * slot_count, D),
        weight_block.reshape(exp_count * slot_count, 1),
        w_in,
        w_back,
    )
    produced = produced.reshape(exp_count, slot_count, D)
    arrived = lax.all_to_all(produced, "exp", split_axis=0, concat_axis=0, tiled=True)
    expert_out = jnp.sum(arrived.astype(jnp.float32), axis=0).astype(jnp.bfloat16)
    return (middle, expert_out)


def solution(mesh):
    in_specs = (
        P("ctx", "exp"),
        P("ctx", None),
        P("ctx", None),
        P("ctx"),
        P("ctx"),
        P("exp", None),
        P(("ctx", "exp"), None),
        P(),
        P(("ctx", "exp"), None),
        P(("ctx", "exp"), None),
        P("exp", None, None),
        P("exp", None, None),
    )
    out_specs = (P(("ctx", "exp"), None), P(("ctx", "exp"), None))
    one_line = mesh.shape["exp"] == HID_SPLIT and mesh.shape["ctx"] == 8
    return jax.shard_map(
        line_device if one_line else wide_device,
        mesh=mesh,
        in_specs=in_specs,
        out_specs=out_specs,
        check_vma=False,
    )
```

```python
import functools

import jax
import jax.numpy as jnp
from jax import lax
from jax.experimental import pallas as pl
from jax.experimental.pallas import tpu as pltpu
from jax.sharding import PartitionSpec as P

D = 4096
HEADS = 64
KV_HEADS = 4
HEAD_DIM = 128
HID_SPLIT = 4
STACK = 4
WIDTHS = (1024, 1024, 1024, 1024)
SPANS = tuple((sum(WIDTHS[:i]), width) for i, width in enumerate(WIDTHS))
PAD_ROWS = 16
BASE = 64
IN_FLIGHT = 2
EARLY = 2
LOG2E = 1.4426950408889634
VMEM = pl.BlockSpec(memory_space=pltpu.VMEM)
ANY = pl.BlockSpec(memory_space=pl.ANY)
LIGHT = pl.CostEstimate(flops=1024, bytes_accessed=1024, transcendentals=0)


def exchange(value, axis, offset, size):
    return lax.ppermute(value, axis, [(i, i ^ offset) for i in range(size)])


def start_weights(w_hbm, w_buf, sems, spans):
    copies = []
    for i, (first, width) in enumerate(spans):
        target = pl.ds(first - spans[0][0], width)
        copy = pltpu.make_async_copy(
            w_hbm.at[:, pl.ds(first, width)], w_buf.at[:, target], sems.at[i]
        )
        copy.start()
        copies.append(copy)
    return copies


def attend_kernel(rank_ref, limit_ref, same_ref, other_ref, q_ref, resid_ref, w_hbm, *refs):
    spans = SPANS[:EARLY]
    outs = refs[: 2 * EARLY]
    attended, w_buf, k_buf, v_buf, bias, acc, sems = refs[2 * EARLY :]
    tok = q_ref.shape[0]
    heads = q_ref.shape[1] // HEAD_DIM
    copies = start_weights(w_hbm, w_buf, sems, spans)
    extra = limit_ref[...].astype(jnp.float32)
    bound = extra[:1, :tok] * BASE + extra[:1, tok:]
    bound = jnp.broadcast_to(bound, (tok, tok)).T
    lane = lax.broadcasted_iota(jnp.int32, (1, tok), 1).astype(jnp.float32)
    ones = jnp.ones((tok, HEAD_DIM), jnp.bfloat16)
    block_rows = tok + PAD_ROWS
    half_count = same_ref.shape[0] // block_rows
    for b in range(2 * half_count):
        rows = slice(b * tok, (b + 1) * tok)
        group, row = (same_ref, b) if b < half_count else (other_ref, b - half_count)
        top = row * block_rows
        k_buf[rows, :] = group[top : top + tok, :HEAD_DIM]
        v_buf[rows, :HEAD_DIM] = group[top : top + tok, HEAD_DIM:]
        v_buf[rows, HEAD_DIM:] = ones
        start = group[top + tok : top + block_rows, :HEAD_DIM].astype(jnp.float32)[:1]
        place = start * tok + lane
        bias[:, rows] = jnp.where(place <= bound, 0.0, -1e30)
    factor = HEAD_DIM ** (-0.5) * LOG2E

    def some_heads(step, carry):
        base = step * STACK * HEAD_DIM
        parts = []
        for j in range(STACK):
            start = pl.multiple_of(base + j * HEAD_DIM, HEAD_DIM)
            parts.append(q_ref[:, pl.ds(start, HEAD_DIM)])
        stacked = jnp.concatenate(parts, axis=0)
        scores = lax.dot_general(
            stacked, k_buf[...], (((1,), (1,)), ((), ())), preferred_element_type=jnp.float32
        )
        scores = scores.reshape(STACK, tok, -1) * factor + bias[...][None]
        row_max = jnp.max(scores, axis=2, keepdims=True)
        weights = jnp.exp2(scores - row_max).astype(jnp.bfloat16)
        summed = jnp.dot(
            weights.reshape(STACK * tok, -1), v_buf[...], preferred_element_type=jnp.float32
        )
        result = (summed[:, :HEAD_DIM] / summed[:, HEAD_DIM:]).astype(jnp.bfloat16)
        for j in range(STACK):
            start = pl.multiple_of(base + j * HEAD_DIM, HEAD_DIM)
            attended[:, pl.ds(start, HEAD_DIM)] = result[j * tok : (j + 1) * tok]
        return carry

    lax.fori_loop(0, heads // STACK, some_heads, 0, unroll=True)
    project_spans(spans, copies, rank_ref[0], attended, w_buf, resid_ref, acc, outs)


def project_spans(spans, copies, rank, attended, w_buf, resid_ref, acc, outs):
    home = resid_ref.shape[0]
    side = rank % 2
    kept = [pl.multiple_of((side + 2 * i) * home, home) for i in range(2)]
    leaving = [pl.multiple_of((1 - side + 2 * i) * home, home) for i in range(2)]
    top = pl.multiple_of(rank * home, home)
    for chunk, (first, width) in enumerate(spans):
        copies[chunk].wait()
        span = slice(first - spans[0][0], first - spans[0][0] + width)
        acc[:, span] = jnp.dot(
            attended[...], w_buf[:, span], preferred_element_type=jnp.float32
        )
        acc[pl.ds(top, home), span] += resid_ref[:, first : first + width].astype(jnp.float32)
        for i in range(2):
            rows = slice(i * home, (i + 1) * home)
            outs[2 * chunk][rows, :] = acc[pl.ds(kept[i], home), span].astype(jnp.bfloat16)
            outs[2 * chunk + 1][rows, :] = acc[pl.ds(leaving[i], home), span].astype(
                jnp.bfloat16
            )


def part_shapes(tok, spans):
    return [
        jax.ShapeDtypeStruct((tok // 2, width), jnp.bfloat16) for _, width in spans for _ in range(2)
    ]


def attend_project(rank, limits, same, other, queries, residual, w_out):
    tok, width = queries.shape
    keys_in_all = 2 * same.shape[0] // (tok + PAD_ROWS) * tok
    spans = SPANS[:EARLY]
    columns = sum(w for _, w in spans)
    return pl.pallas_call(
        attend_kernel,
        out_shape=part_shapes(tok, spans) + [jax.ShapeDtypeStruct((tok, width), jnp.bfloat16)],
        in_specs=[pl.BlockSpec(memory_space=pltpu.SMEM)] + [VMEM] * 5 + [ANY],
        out_specs=[VMEM] * (2 * len(spans) + 1),
        scratch_shapes=[
            pltpu.VMEM((width, columns), jnp.bfloat16),
            pltpu.VMEM((keys_in_all, HEAD_DIM), jnp.bfloat16),
            pltpu.VMEM((keys_in_all, 2 * HEAD_DIM), jnp.bfloat16),
            pltpu.VMEM((tok, keys_in_all), jnp.float32),
            pltpu.VMEM((tok, columns), jnp.float32),
            pltpu.SemaphoreType.DMA((len(spans),)),
        ],
        compiler_params=pltpu.CompilerParams(vmem_limit_bytes=48 * 1024 * 1024),
        cost_estimate=pl.CostEstimate(
            flops=2 * tok * width * (2 * keys_in_all + columns),
            bytes_accessed=2 * width * columns,
            transcendentals=tok * width // HEAD_DIM * keys_in_all,
        ),
        name="attend_project",
    )(rank, limits, same, other, queries, residual, w_out)


def project_kernel(rank_ref, attended, resid_ref, w_hbm, *refs):
    spans = SPANS[EARLY:]
    outs = refs[: 2 * len(spans)]
    w_buf, acc, sems = refs[2 * len(spans) :]
    copies = start_weights(w_hbm, w_buf, sems, spans)
    project_spans(spans, copies, rank_ref[0], attended, w_buf, resid_ref, acc, outs)


def project(rank, attended, residual, w_out):
    tok, width = attended.shape
    spans = SPANS[EARLY:]
    columns = sum(w for _, w in spans)
    return pl.pallas_call(
        project_kernel,
        out_shape=part_shapes(tok, spans),
        in_specs=[pl.BlockSpec(memory_space=pltpu.SMEM)] + [VMEM] * 2 + [ANY],
        out_specs=[VMEM] * (2 * len(spans)),
        scratch_shapes=[
            pltpu.VMEM((width, columns), jnp.bfloat16),
            pltpu.VMEM((tok, columns), jnp.float32),
            pltpu.SemaphoreType.DMA((len(spans),)),
        ],
        compiler_params=pltpu.CompilerParams(vmem_limit_bytes=48 * 1024 * 1024),
        cost_estimate=pl.CostEstimate(
            flops=2 * tok * width * columns,
            bytes_accessed=2 * width * columns,
            transcendentals=0,
        ),
        name="project",
    )(rank, attended, residual, w_out)


def stage_kernel(q_hbm, resid_hbm, q_ref, resid_ref, sems):
    copies = [
        pltpu.make_async_copy(q_hbm, q_ref, sems.at[0]),
        pltpu.make_async_copy(resid_hbm, resid_ref, sems.at[1]),
    ]
    for copy in copies:
        copy.start()
    for copy in copies:
        copy.wait()


def stage(queries, residual):
    arrays = (queries, residual)
    return pl.pallas_call(
        stage_kernel,
        out_shape=[jax.ShapeDtypeStruct(array.shape, array.dtype) for array in arrays],
        in_specs=[ANY, ANY],
        out_specs=[VMEM, VMEM],
        scratch_shapes=[pltpu.SemaphoreType.DMA((2,))],
        compiler_params=pltpu.CompilerParams(vmem_limit_bytes=4 * 1024 * 1024),
        cost_estimate=LIGHT,
        name="stage",
    )(*arrays)


def join_kernel(*refs):
    out_ref = refs[-1]
    first = 0
    for piece in refs[1:-1]:
        rows = piece.shape[0]
        out_ref[first : first + rows, :] = piece[...]
        first += rows


def join_after(pieces, after):
    rows = sum(piece.shape[0] for piece in pieces)
    width = pieces[0].shape[1]
    return pl.pallas_call(
        join_kernel,
        out_shape=jax.ShapeDtypeStruct((rows, width), jnp.bfloat16),
        in_specs=[ANY] + [VMEM] * len(pieces),
        out_specs=VMEM,
        compiler_params=pltpu.CompilerParams(vmem_limit_bytes=8 * 1024 * 1024),
        cost_estimate=LIGHT,
        name="join_after",
    )(after, *pieces)


def absorb_kernel(chunk, rank_ref, mine_ref, theirs_ref, gain_ref, w_ref, *refs):
    last = chunk == len(WIDTHS) - 1
    state_count = 0 if chunk == 0 else 2
    states = refs[:state_count]
    home_ref = refs[state_count + int(last)]
    outs = refs[state_count + int(last) + 1 :]
    first, width = SPANS[chunk]
    span = slice(first, first + width)
    home = home_ref.shape[0]
    place = rank_ref[0] // 2
    home_ref[...] = mine_ref[pl.ds(pl.multiple_of(place * home, home), home), :]
    wide = jnp.concatenate([mine_ref[...], theirs_ref[...]], axis=0).astype(jnp.float32)
    gained = (wide * gain_ref[:, span]).astype(jnp.bfloat16)
    product = lax.dot_general(
        gained, w_ref[:, span], (((1,), (1,)), ((), ())), preferred_element_type=jnp.float32
    )
    square = sum(
        wide[:, i * 128 : (i + 1) * 128] * wide[:, i * 128 : (i + 1) * 128]
        for i in range(width // 128)
    )
    if chunk > 0:
        product += states[0][...]
        square += states[1][...]
    if not last:
        outs[0][...] = product
        outs[1][...] = square
        return
    back_ref = refs[state_count]
    shares, act_buf = outs[:-1], outs[-1]
    hidden = product.shape[1] // 2
    mean_square = jnp.sum(square, axis=1, keepdims=True) / D
    product = product * lax.rsqrt(mean_square + 1e-06)
    gate = product[:, :hidden]
    act_buf[...] = gate / (1.0 + jnp.exp(-gate)) * product[:, hidden:]
    ordered = []
    for offset in range(len(shares)):
        row = (offset % 2) * 2 * home + (place ^ (offset // 2)) * home
        ordered.append(act_buf[pl.ds(pl.multiple_of(row, home), home), :])
    ordered = jnp.concatenate(ordered, axis=0).astype(jnp.bfloat16)
    for part_first, part_width in SPANS:
        part = slice(part_first, part_first + part_width)
        result = jnp.dot(ordered, back_ref[:, part], preferred_element_type=jnp.float32)
        for i, share in enumerate(shares):
            share[:, part] = result[i * home : (i + 1) * home].astype(jnp.bfloat16)


def absorb(chunk, rank, mine, theirs, gain, w_in, states, back):
    half, width = mine.shape
    rows = w_in.shape[0]
    count = lax.axis_size("exp")
    home = 2 * half // count
    out_shape = [jax.ShapeDtypeStruct((home, width), jnp.bfloat16)]
    scratch = []
    operands = [rank, mine, theirs, gain, w_in, *states]
    if chunk == len(WIDTHS) - 1:
        operands.append(back)
        out_shape += [jax.ShapeDtypeStruct((home, D), jnp.bfloat16)] * count
        scratch = [pltpu.VMEM((2 * half, rows // 2), jnp.float32)]
    else:
        out_shape += [
            jax.ShapeDtypeStruct((2 * half, rows), jnp.float32),
            jax.ShapeDtypeStruct((2 * half, 128), jnp.float32),
        ]
    return pl.pallas_call(
        functools.partial(absorb_kernel, chunk),
        out_shape=out_shape,
        in_specs=[pl.BlockSpec(memory_space=pltpu.SMEM)] + [VMEM] * (len(operands) - 1),
        out_specs=[VMEM] * len(out_shape),
        scratch_shapes=scratch,
        compiler_params=pltpu.CompilerParams(vmem_limit_bytes=16 * 1024 * 1024),
        cost_estimate=LIGHT,
        name="absorb",
    )(*operands)


def own_heads(queries, keys, values):
    heads_here = queries.shape[1] // HEAD_DIM
    kv_number = lax.axis_index("exp") * heads_here // (HEADS // KV_HEADS)
    key_head = lax.dynamic_slice_in_dim(keys, kv_number * HEAD_DIM, HEAD_DIM, 1)
    value_head = lax.dynamic_slice_in_dim(values, kv_number * HEAD_DIM, HEAD_DIM, 1)
    return key_head, value_head


def line_device(
    queries,
    keys,
    values,
    positions,
    bounds,
    w_out,
    residual,
    norm_gain,
    routes,
    gates,
    w_in,
    w_back,
):
    tok = queries.shape[0]
    home = residual.shape[0]
    hidden = w_back.shape[1]
    ctx_count = lax.axis_size("ctx")
    exp_count = lax.axis_size("exp")
    rank = lax.axis_index("exp")
    key_head, value_head = own_heads(queries, keys, values)
    staged_queries, staged_residual = stage(queries, residual)
    block = (positions[0] // tok).astype(jnp.bfloat16)
    width = 2 * HEAD_DIM
    payload = jnp.concatenate(
        [
            jnp.concatenate([key_head, value_head], axis=1),
            jnp.full((PAD_ROWS, width), block, jnp.bfloat16),
        ],
        axis=0,
    )
    limits = jnp.concatenate([bounds // BASE, bounds % BASE]).astype(jnp.bfloat16)
    limits = jnp.broadcast_to(limits.reshape(1, width), (PAD_ROWS, width))
    same_keys = join_after(
        [payload] + [exchange(payload, "ctx", r, ctx_count) for r in range(ctx_count - 2, 0, -2)],
        payload,
    )
    other_keys = exchange(same_keys, "ctx", 1, ctx_count)

    ranks = rank.astype(jnp.int32).reshape(1)
    *parts, attended = attend_project(
        ranks, limits, same_keys, other_keys, staged_queries, staged_residual, w_out
    )
    parts += project(ranks, attended, staged_residual, w_out)
    shares = gates / jnp.sum(gates, axis=1, keepdims=True)
    coefficient = jnp.sum(jnp.where(routes == 0, shares, 0.0), axis=1, keepdims=True)
    coefficient = coefficient.astype(jnp.bfloat16).astype(jnp.float32)
    gain = norm_gain.reshape(1, D)
    flat_in = w_in.reshape(2 * hidden, D)
    flat_back = w_back.reshape(hidden, D)
    count = len(WIDTHS)

    def swap(values, offset):
        results = []
        for i, value in enumerate(values):
            if i >= IN_FLIGHT:
                value, _ = lax.optimization_barrier((value, results[i - IN_FLIGHT]))
            results.append(exchange(value, "exp", offset, exp_count))
        return results

    arrived = swap(parts[1::2], 1)
    near = [kept + other for kept, other in zip(parts[::2], arrived)]
    across = swap(near, 2)
    mine = [own + other for own, other in zip(near, across)]
    homes, states, theirs, done = [], [], [], [coefficient]
    for chunk in range(count):
        value = mine[chunk]
        if chunk == IN_FLIGHT:
            own, *states = absorb(
                chunk - IN_FLIGHT,
                ranks,
                mine[chunk - IN_FLIGHT],
                theirs[chunk - IN_FLIGHT],
                gain,
                flat_in,
                states,
                flat_back,
            )
            homes.append(own)
            done = [states[0]]
        if chunk == IN_FLIGHT or chunk == 1:
            value, *done = lax.optimization_barrier((value, *done))
            if chunk == 1:
                coefficient = done[0]
            else:
                states[0] = done[0]
        theirs.append(exchange(value, "exp", 1, exp_count))
    for chunk in range(1, count):
        own, *states = absorb(
            chunk, ranks, mine[chunk], theirs[chunk], gain, flat_in, states, flat_back
        )
        homes.append(own)
    middle_out = jnp.concatenate(homes, axis=1)
    expert = states[0].astype(jnp.float32)
    for offset in range(1, exp_count):
        expert = expert + exchange(states[offset], "exp", offset, exp_count).astype(jnp.float32)
    return (middle_out, (expert * coefficient).astype(jnp.bfloat16))


def largest_divisor(row_count):
    candidate = min(row_count, 1024)
    while row_count % candidate != 0:
        candidate = candidate - 1
    return candidate


def apply_slice(row_block, coefficient, w_in, w_back):
    hidden_here = w_back.shape[1]
    flat_in = w_in.reshape(2 * hidden_here, D)
    projected = lax.dot_general(
        row_block, flat_in, (((1,), (1,)), ((), ())), preferred_element_type=jnp.float32
    )
    activated = jax.nn.silu(projected[:, :hidden_here]) * projected[:, hidden_here:]
    blended = (coefficient.astype(jnp.float32) * activated).astype(jnp.bfloat16)
    flat_back = w_back.reshape(hidden_here, D)
    return jnp.dot(blended, flat_back, preferred_element_type=jnp.float32).astype(jnp.bfloat16)


def wide_device(
    queries,
    keys,
    values,
    positions,
    bounds,
    w_out,
    residual,
    norm_gain,
    routes,
    gates,
    w_in,
    w_back,
):
    tok_rows = queries.shape[0]
    head_cols = queries.shape[1]
    heads_here = head_cols // HEAD_DIM
    exp_count = lax.axis_size("exp")
    key_head, value_head = own_heads(queries, keys, values)
    query_heads = queries.reshape(tok_rows, heads_here, HEAD_DIM).transpose(1, 0, 2)
    scale = HEAD_DIM ** (-0.5)
    reach_max = jnp.max(bounds)
    all_keys, all_values, all_places = (
        lax.all_gather(key_head, "ctx", axis=0, tiled=True),
        lax.all_gather(value_head, "ctx", axis=0, tiled=True),
        lax.all_gather(positions, "ctx", axis=0, tiled=True),
    )
    total_rows = all_keys.shape[0]
    tile_len = largest_divisor(total_rows)
    tile_count = total_rows // tile_len

    def process(state_in, key_rows, value_rows, place_rows):
        row_max, row_sum, running = state_in
        scores = (
            jnp.einsum("htd,nd->htn", query_heads, key_rows, preferred_element_type=jnp.float32)
            * scale
        )
        visible = (place_rows[None, :] <= bounds[:, None])[None, :, :]
        masked = jnp.where(visible, scores, -1e30)
        new_max = jnp.maximum(row_max, jnp.max(masked, axis=2))
        weights = jnp.exp(masked - new_max[..., None])
        rescale = jnp.exp(row_max - new_max)
        row_sum = row_sum * rescale + jnp.sum(weights, axis=2)
        running = running * rescale[..., None] + jnp.einsum(
            "htn,nd->htd",
            weights.astype(jnp.bfloat16),
            value_rows,
            preferred_element_type=jnp.float32,
        )
        return (new_max, row_sum, running)

    def one_tile(tile_number, state_now):
        first = tile_number * tile_len
        key_rows = lax.dynamic_slice_in_dim(all_keys, first, tile_len, 0)
        value_rows = lax.dynamic_slice_in_dim(all_values, first, tile_len, 0)
        place_rows = lax.dynamic_slice_in_dim(all_places, first, tile_len, 0)
        return lax.cond(
            jnp.min(place_rows) <= reach_max,
            lambda state_in: process(state_in, key_rows, value_rows, place_rows),
            lambda state_in: state_in,
            state_now,
        )

    start_state = (
        jnp.full((heads_here, tok_rows), -1e30, jnp.float32),
        jnp.zeros((heads_here, tok_rows), jnp.float32),
        jnp.zeros((heads_here, tok_rows, HEAD_DIM), jnp.float32),
    )
    row_max, row_sum, running = lax.fori_loop(0, tile_count, one_tile, start_state)
    attended = (running / row_sum[..., None]).astype(jnp.bfloat16)
    attended = attended.transpose(1, 0, 2).reshape(tok_rows, head_cols)
    attention_rows = lax.psum_scatter(
        jnp.dot(attended, w_out, preferred_element_type=jnp.float32).astype(jnp.bfloat16),
        "exp",
        scatter_dimension=0,
        tiled=True,
    ).astype(jnp.float32)
    middle = (residual.astype(jnp.float32) + attention_rows).astype(jnp.bfloat16)
    wide = middle.astype(jnp.float32)
    mean_square = jnp.mean(wide * wide, axis=1, keepdims=True)
    normed = (wide * lax.rsqrt(mean_square + 1e-06) * norm_gain[None, :]).astype(jnp.bfloat16)
    local_rows = residual.shape[0]
    shares = gates / jnp.sum(gates, axis=1, keepdims=True)
    slice_expert = jnp.arange(exp_count, dtype=jnp.int32) // HID_SPLIT
    hits = routes[:, :, None] == slice_expert[None, None, :]
    coefficient = jnp.sum(jnp.where(hits, shares[:, :, None], 0.0), axis=1).astype(jnp.bfloat16)
    owner_weights = coefficient.transpose(1, 0)[:, :, None]
    copies = jnp.broadcast_to(normed[None, :, :], (exp_count, local_rows, D))
    row_block = lax.all_to_all(copies, "exp", split_axis=0, concat_axis=0, tiled=True)
    weight_block = lax.all_to_all(owner_weights, "exp", split_axis=0, concat_axis=0, tiled=True)
    slot_count = row_block.shape[1]
    produced = apply_slice(
        row_block.reshape(exp_count * slot_count, D),
        weight_block.reshape(exp_count * slot_count, 1),
        w_in,
        w_back,
    )
    produced = produced.reshape(exp_count, slot_count, D)
    arrived = lax.all_to_all(produced, "exp", split_axis=0, concat_axis=0, tiled=True)
    expert_out = jnp.sum(arrived.astype(jnp.float32), axis=0).astype(jnp.bfloat16)
    return (middle, expert_out)


def solution(mesh):
    in_specs = (
        P("ctx", "exp"),
        P("ctx", None),
        P("ctx", None),
        P("ctx"),
        P("ctx"),
        P("exp", None),
        P(("ctx", "exp"), None),
        P(),
        P(("ctx", "exp"), None),
        P(("ctx", "exp"), None),
        P("exp", None, None),
        P("exp", None, None),
    )
    out_specs = (P(("ctx", "exp"), None), P(("ctx", "exp"), None))
    one_line = mesh.shape["exp"] == HID_SPLIT and mesh.shape["ctx"] == 8
    return jax.shard_map(
        line_device if one_line else wide_device,
        mesh=mesh,
        in_specs=in_specs,
        out_specs=out_specs,
        check_vma=False,
    )
```

```python
import functools

import jax
import jax.numpy as jnp
from jax import lax
from jax.experimental import pallas as pl
from jax.experimental.pallas import tpu as pltpu
from jax.sharding import PartitionSpec as P

D = 4096
HEADS = 64
KV_HEADS = 4
HEAD_DIM = 128
HID_SPLIT = 4
STACK = 4
WIDTHS = (1024, 1024, 1024, 1024)
SPANS = tuple((sum(WIDTHS[:i]), width) for i, width in enumerate(WIDTHS))
PAD_ROWS = 16
BASE = 64
IN_FLIGHT = 2
EARLY = 2
LOG2E = 1.4426950408889634
VMEM = pl.BlockSpec(memory_space=pltpu.VMEM)
ANY = pl.BlockSpec(memory_space=pl.ANY)
LIGHT = pl.CostEstimate(flops=1024, bytes_accessed=1024, transcendentals=0)


def exchange(value, axis, offset, size):
    return lax.ppermute(value, axis, [(i, i ^ offset) for i in range(size)])


def start_weights(w_hbm, w_buf, sems, spans):
    copies = []
    for i, (first, width) in enumerate(spans):
        target = pl.ds(first - spans[0][0], width)
        copy = pltpu.make_async_copy(
            w_hbm.at[:, pl.ds(first, width)], w_buf.at[:, target], sems.at[i]
        )
        copy.start()
        copies.append(copy)
    return copies


def attend_kernel(rank_ref, limit_ref, same_ref, other_ref, q_ref, resid_ref, w_hbm, *refs):
    spans = SPANS[:EARLY]
    outs = refs[: 2 * EARLY]
    attended, w_buf, k_buf, v_buf, bias, acc, sems = refs[2 * EARLY :]
    tok = q_ref.shape[0]
    heads = q_ref.shape[1] // HEAD_DIM
    copies = start_weights(w_hbm, w_buf, sems, spans)
    extra = limit_ref[...].astype(jnp.float32)
    bound = extra[:1, :tok] * BASE + extra[:1, tok:]
    bound = jnp.broadcast_to(bound, (tok, tok)).T
    lane = lax.broadcasted_iota(jnp.int32, (1, tok), 1).astype(jnp.float32)
    ones = jnp.ones((tok, HEAD_DIM), jnp.bfloat16)
    block_rows = tok + PAD_ROWS
    half_count = same_ref.shape[0] // block_rows
    for b in range(2 * half_count):
        rows = slice(b * tok, (b + 1) * tok)
        group, row = (same_ref, b) if b < half_count else (other_ref, b - half_count)
        top = row * block_rows
        k_buf[rows, :] = group[top : top + tok, :HEAD_DIM]
        v_buf[rows, :HEAD_DIM] = group[top : top + tok, HEAD_DIM:]
        v_buf[rows, HEAD_DIM:] = ones
        start = group[top + tok : top + block_rows, :HEAD_DIM].astype(jnp.float32)[:1]
        place = start * tok + lane
        bias[:, rows] = jnp.where(place <= bound, 0.0, -1e30)
    factor = HEAD_DIM ** (-0.5) * LOG2E

    def some_heads(step, carry):
        base = step * STACK * HEAD_DIM
        parts = []
        for j in range(STACK):
            start = pl.multiple_of(base + j * HEAD_DIM, HEAD_DIM)
            parts.append(q_ref[:, pl.ds(start, HEAD_DIM)])
        stacked = jnp.concatenate(parts, axis=0)
        scores = lax.dot_general(
            stacked, k_buf[...], (((1,), (1,)), ((), ())), preferred_element_type=jnp.float32
        )
        scores = scores.reshape(STACK, tok, -1) * factor + bias[...][None]
        row_max = jnp.max(scores, axis=2, keepdims=True)
        weights = jnp.exp2(scores - row_max).astype(jnp.bfloat16)
        summed = jnp.dot(
            weights.reshape(STACK * tok, -1), v_buf[...], preferred_element_type=jnp.float32
        )
        result = (summed[:, :HEAD_DIM] / summed[:, HEAD_DIM:]).astype(jnp.bfloat16)
        for j in range(STACK):
            start = pl.multiple_of(base + j * HEAD_DIM, HEAD_DIM)
            attended[:, pl.ds(start, HEAD_DIM)] = result[j * tok : (j + 1) * tok]
        return carry

    lax.fori_loop(0, heads // STACK, some_heads, 0, unroll=True)
    project_spans(spans, copies, rank_ref[0], attended, w_buf, resid_ref, acc, outs)


def project_spans(spans, copies, rank, attended, w_buf, resid_ref, acc, outs):
    home = resid_ref.shape[0]
    side = rank % 2
    kept = [pl.multiple_of((side + 2 * i) * home, home) for i in range(2)]
    leaving = [pl.multiple_of((1 - side + 2 * i) * home, home) for i in range(2)]
    top = pl.multiple_of(rank * home, home)
    for chunk, (first, width) in enumerate(spans):
        copies[chunk].wait()
        span = slice(first - spans[0][0], first - spans[0][0] + width)
        acc[:, span] = jnp.dot(
            attended[...], w_buf[:, span], preferred_element_type=jnp.float32
        )
        acc[pl.ds(top, home), span] += resid_ref[:, first : first + width].astype(jnp.float32)
        for i in range(2):
            rows = slice(i * home, (i + 1) * home)
            outs[2 * chunk][rows, :] = acc[pl.ds(kept[i], home), span].astype(jnp.bfloat16)
            outs[2 * chunk + 1][rows, :] = acc[pl.ds(leaving[i], home), span].astype(
                jnp.bfloat16
            )


def part_shapes(tok, spans):
    return [
        jax.ShapeDtypeStruct((tok // 2, width), jnp.bfloat16) for _, width in spans for _ in range(2)
    ]


def attend_project(rank, limits, same, other, queries, residual, w_out):
    tok, width = queries.shape
    keys_in_all = 2 * same.shape[0] // (tok + PAD_ROWS) * tok
    spans = SPANS[:EARLY]
    columns = sum(w for _, w in spans)
    return pl.pallas_call(
        attend_kernel,
        out_shape=part_shapes(tok, spans) + [jax.ShapeDtypeStruct((tok, width), jnp.bfloat16)],
        in_specs=[pl.BlockSpec(memory_space=pltpu.SMEM)] + [VMEM] * 5 + [ANY],
        out_specs=[VMEM] * (2 * len(spans) + 1),
        scratch_shapes=[
            pltpu.VMEM((width, columns), jnp.bfloat16),
            pltpu.VMEM((keys_in_all, HEAD_DIM), jnp.bfloat16),
            pltpu.VMEM((keys_in_all, 2 * HEAD_DIM), jnp.bfloat16),
            pltpu.VMEM((tok, keys_in_all), jnp.float32),
            pltpu.VMEM((tok, columns), jnp.float32),
            pltpu.SemaphoreType.DMA((len(spans),)),
        ],
        compiler_params=pltpu.CompilerParams(vmem_limit_bytes=48 * 1024 * 1024),
        cost_estimate=pl.CostEstimate(
            flops=2 * tok * width * (2 * keys_in_all + columns),
            bytes_accessed=2 * width * columns,
            transcendentals=tok * width // HEAD_DIM * keys_in_all,
        ),
        name="attend_project",
    )(rank, limits, same, other, queries, residual, w_out)


def project_kernel(rank_ref, attended, resid_ref, w_hbm, *refs):
    spans = SPANS[EARLY:]
    outs = refs[: 2 * len(spans)]
    w_buf, acc, sems = refs[2 * len(spans) :]
    copies = start_weights(w_hbm, w_buf, sems, spans)
    project_spans(spans, copies, rank_ref[0], attended, w_buf, resid_ref, acc, outs)


def project(rank, attended, residual, w_out):
    tok, width = attended.shape
    spans = SPANS[EARLY:]
    columns = sum(w for _, w in spans)
    return pl.pallas_call(
        project_kernel,
        out_shape=part_shapes(tok, spans),
        in_specs=[pl.BlockSpec(memory_space=pltpu.SMEM)] + [VMEM] * 2 + [ANY],
        out_specs=[VMEM] * (2 * len(spans)),
        scratch_shapes=[
            pltpu.VMEM((width, columns), jnp.bfloat16),
            pltpu.VMEM((tok, columns), jnp.float32),
            pltpu.SemaphoreType.DMA((len(spans),)),
        ],
        compiler_params=pltpu.CompilerParams(vmem_limit_bytes=48 * 1024 * 1024),
        cost_estimate=pl.CostEstimate(
            flops=2 * tok * width * columns,
            bytes_accessed=2 * width * columns,
            transcendentals=0,
        ),
        name="project",
    )(rank, attended, residual, w_out)


def stage_kernel(q_hbm, resid_hbm, q_ref, resid_ref, sems):
    copies = [
        pltpu.make_async_copy(q_hbm, q_ref, sems.at[0]),
        pltpu.make_async_copy(resid_hbm, resid_ref, sems.at[1]),
    ]
    for copy in copies:
        copy.start()
    for copy in copies:
        copy.wait()


def stage(queries, residual):
    arrays = (queries, residual)
    return pl.pallas_call(
        stage_kernel,
        out_shape=[jax.ShapeDtypeStruct(array.shape, array.dtype) for array in arrays],
        in_specs=[ANY, ANY],
        out_specs=[VMEM, VMEM],
        scratch_shapes=[pltpu.SemaphoreType.DMA((2,))],
        compiler_params=pltpu.CompilerParams(vmem_limit_bytes=4 * 1024 * 1024),
        cost_estimate=LIGHT,
        name="stage",
    )(*arrays)


def join_kernel(*refs):
    out_ref = refs[-1]
    first = 0
    for piece in refs[1:-1]:
        rows = piece.shape[0]
        out_ref[first : first + rows, :] = piece[...]
        first += rows


def join_after(pieces, after):
    rows = sum(piece.shape[0] for piece in pieces)
    width = pieces[0].shape[1]
    return pl.pallas_call(
        join_kernel,
        out_shape=jax.ShapeDtypeStruct((rows, width), jnp.bfloat16),
        in_specs=[ANY] + [VMEM] * len(pieces),
        out_specs=VMEM,
        compiler_params=pltpu.CompilerParams(vmem_limit_bytes=8 * 1024 * 1024),
        cost_estimate=LIGHT,
        name="join_after",
    )(after, *pieces)


def absorb_kernel(chunk, rank_ref, mine_ref, theirs_ref, gain_ref, w_ref, *refs):
    last = chunk == len(WIDTHS) - 1
    state_count = 0 if chunk == 0 else 2
    states = refs[:state_count]
    home_ref = refs[state_count + int(last)]
    outs = refs[state_count + int(last) + 1 :]
    first, width = SPANS[chunk]
    span = slice(first, first + width)
    home = home_ref.shape[0]
    place = rank_ref[0] // 2
    home_ref[...] = mine_ref[pl.ds(pl.multiple_of(place * home, home), home), :]
    wide = jnp.concatenate([mine_ref[...], theirs_ref[...]], axis=0).astype(jnp.float32)
    gained = (wide * gain_ref[:, span]).astype(jnp.bfloat16)
    product = lax.dot_general(
        gained, w_ref[:, span], (((1,), (1,)), ((), ())), preferred_element_type=jnp.float32
    )
    square = sum(
        wide[:, i * 128 : (i + 1) * 128] * wide[:, i * 128 : (i + 1) * 128]
        for i in range(width // 128)
    )
    if chunk > 0:
        product += states[0][...]
        square += states[1][...]
    if not last:
        outs[0][...] = product
        outs[1][...] = square
        return
    back_ref = refs[state_count]
    shares, act_buf = outs[:-1], outs[-1]
    hidden = product.shape[1] // 2
    mean_square = jnp.sum(square, axis=1, keepdims=True) / D
    product = product * lax.rsqrt(mean_square + 1e-06)
    gate = product[:, :hidden]
    act_buf[...] = gate / (1.0 + jnp.exp(-gate)) * product[:, hidden:]
    ordered = []
    for offset in range(len(shares)):
        row = (offset % 2) * 2 * home + (place ^ (offset // 2)) * home
        ordered.append(act_buf[pl.ds(pl.multiple_of(row, home), home), :])
    ordered = jnp.concatenate(ordered, axis=0).astype(jnp.bfloat16)
    for part_first, part_width in SPANS:
        part = slice(part_first, part_first + part_width)
        result = jnp.dot(ordered, back_ref[:, part], preferred_element_type=jnp.float32)
        for i, share in enumerate(shares):
            share[:, part] = result[i * home : (i + 1) * home].astype(jnp.bfloat16)


def absorb(chunk, rank, mine, theirs, gain, w_in, states, back):
    half, width = mine.shape
    rows = w_in.shape[0]
    count = lax.axis_size("exp")
    home = 2 * half // count
    out_shape = [jax.ShapeDtypeStruct((home, width), jnp.bfloat16)]
    scratch = []
    operands = [rank, mine, theirs, gain, w_in, *states]
    if chunk == len(WIDTHS) - 1:
        operands.append(back)
        out_shape += [jax.ShapeDtypeStruct((home, D), jnp.bfloat16)] * count
        scratch = [pltpu.VMEM((2 * half, rows // 2), jnp.float32)]
    else:
        out_shape += [
            jax.ShapeDtypeStruct((2 * half, rows), jnp.float32),
            jax.ShapeDtypeStruct((2 * half, 128), jnp.float32),
        ]
    return pl.pallas_call(
        functools.partial(absorb_kernel, chunk),
        out_shape=out_shape,
        in_specs=[pl.BlockSpec(memory_space=pltpu.SMEM)] + [VMEM] * (len(operands) - 1),
        out_specs=[VMEM] * len(out_shape),
        scratch_shapes=scratch,
        compiler_params=pltpu.CompilerParams(vmem_limit_bytes=16 * 1024 * 1024),
        cost_estimate=LIGHT,
        name="absorb",
    )(*operands)


def own_heads(queries, keys, values):
    heads_here = queries.shape[1] // HEAD_DIM
    kv_number = lax.axis_index("exp") * heads_here // (HEADS // KV_HEADS)
    key_head = lax.dynamic_slice_in_dim(keys, kv_number * HEAD_DIM, HEAD_DIM, 1)
    value_head = lax.dynamic_slice_in_dim(values, kv_number * HEAD_DIM, HEAD_DIM, 1)
    return key_head, value_head


def line_device(
    queries,
    keys,
    values,
    positions,
    bounds,
    w_out,
    residual,
    norm_gain,
    routes,
    gates,
    w_in,
    w_back,
):
    tok = queries.shape[0]
    home = residual.shape[0]
    hidden = w_back.shape[1]
    ctx_count = lax.axis_size("ctx")
    exp_count = lax.axis_size("exp")
    rank = lax.axis_index("exp")
    key_head, value_head = own_heads(queries, keys, values)
    staged_queries, staged_residual = stage(queries, residual)
    block = (positions[0] // tok).astype(jnp.bfloat16)
    width = 2 * HEAD_DIM
    payload = jnp.concatenate(
        [
            jnp.concatenate([key_head, value_head], axis=1),
            jnp.full((PAD_ROWS, width), block, jnp.bfloat16),
        ],
        axis=0,
    )
    limits = jnp.concatenate([bounds // BASE, bounds % BASE]).astype(jnp.bfloat16)
    limits = jnp.broadcast_to(limits.reshape(1, width), (PAD_ROWS, width))
    same_keys = join_after(
        [payload] + [exchange(payload, "ctx", r, ctx_count) for r in range(2, ctx_count, 2)],
        payload,
    )
    other_keys = exchange(same_keys, "ctx", 1, ctx_count)

    ranks = rank.astype(jnp.int32).reshape(1)
    *parts, attended = attend_project(
        ranks, limits, same_keys, other_keys, staged_queries, staged_residual, w_out
    )
    parts += project(ranks, attended, staged_residual, w_out)
    shares = gates / jnp.sum(gates, axis=1, keepdims=True)
    coefficient = jnp.sum(jnp.where(routes == 0, shares, 0.0), axis=1, keepdims=True)
    coefficient = coefficient.astype(jnp.bfloat16).astype(jnp.float32)
    gain = norm_gain.reshape(1, D)
    flat_in = w_in.reshape(2 * hidden, D)
    flat_back = w_back.reshape(hidden, D)
    count = len(WIDTHS)

    def swap(values, offset):
        results = []
        for i, value in enumerate(values):
            if i >= IN_FLIGHT:
                value, _ = lax.optimization_barrier((value, results[i - IN_FLIGHT]))
            results.append(exchange(value, "exp", offset, exp_count))
        return results

    arrived = swap(parts[1::2], 1)
    near = [kept + other for kept, other in zip(parts[::2], arrived)]
    across = swap(near, 2)
    mine = [own + other for own, other in zip(near, across)]
    homes, states, theirs, done = [], [], [], [coefficient]
    for chunk in range(count):
        value = mine[chunk]
        if chunk == IN_FLIGHT:
            own, *states = absorb(
                chunk - IN_FLIGHT,
                ranks,
                mine[chunk - IN_FLIGHT],
                theirs[chunk - IN_FLIGHT],
                gain,
                flat_in,
                states,
                flat_back,
            )
            homes.append(own)
            done = [states[0]]
        if chunk == IN_FLIGHT or chunk == 1:
            value, *done = lax.optimization_barrier((value, *done))
            if chunk == 1:
                coefficient = done[0]
            else:
                states[0] = done[0]
        theirs.append(exchange(value, "exp", 1, exp_count))
    for chunk in range(1, count):
        own, *states = absorb(
            chunk, ranks, mine[chunk], theirs[chunk], gain, flat_in, states, flat_back
        )
        homes.append(own)
    middle_out = jnp.concatenate(homes, axis=1)
    expert = states[0].astype(jnp.float32)
    for offset in range(1, exp_count):
        expert = expert + exchange(states[offset], "exp", offset, exp_count).astype(jnp.float32)
    return (middle_out, (expert * coefficient).astype(jnp.bfloat16))


def largest_divisor(row_count):
    candidate = min(row_count, 1024)
    while row_count % candidate != 0:
        candidate = candidate - 1
    return candidate


def apply_slice(row_block, coefficient, w_in, w_back):
    hidden_here = w_back.shape[1]
    flat_in = w_in.reshape(2 * hidden_here, D)
    projected = lax.dot_general(
        row_block, flat_in, (((1,), (1,)), ((), ())), preferred_element_type=jnp.float32
    )
    activated = jax.nn.silu(projected[:, :hidden_here]) * projected[:, hidden_here:]
    blended = (coefficient.astype(jnp.float32) * activated).astype(jnp.bfloat16)
    flat_back = w_back.reshape(hidden_here, D)
    return jnp.dot(blended, flat_back, preferred_element_type=jnp.float32).astype(jnp.bfloat16)


def wide_device(
    queries,
    keys,
    values,
    positions,
    bounds,
    w_out,
    residual,
    norm_gain,
    routes,
    gates,
    w_in,
    w_back,
):
    tok_rows = queries.shape[0]
    head_cols = queries.shape[1]
    heads_here = head_cols // HEAD_DIM
    exp_count = lax.axis_size("exp")
    key_head, value_head = own_heads(queries, keys, values)
    query_heads = queries.reshape(tok_rows, heads_here, HEAD_DIM).transpose(1, 0, 2)
    scale = HEAD_DIM ** (-0.5)
    reach_max = jnp.max(bounds)
    all_keys, all_values, all_places = (
        lax.all_gather(key_head, "ctx", axis=0, tiled=True),
        lax.all_gather(value_head, "ctx", axis=0, tiled=True),
        lax.all_gather(positions, "ctx", axis=0, tiled=True),
    )
    total_rows = all_keys.shape[0]
    tile_len = largest_divisor(total_rows)
    tile_count = total_rows // tile_len

    def process(state_in, key_rows, value_rows, place_rows):
        row_max, row_sum, running = state_in
        scores = (
            jnp.einsum("htd,nd->htn", query_heads, key_rows, preferred_element_type=jnp.float32)
            * scale
        )
        visible = (place_rows[None, :] <= bounds[:, None])[None, :, :]
        masked = jnp.where(visible, scores, -1e30)
        new_max = jnp.maximum(row_max, jnp.max(masked, axis=2))
        weights = jnp.exp(masked - new_max[..., None])
        rescale = jnp.exp(row_max - new_max)
        row_sum = row_sum * rescale + jnp.sum(weights, axis=2)
        running = running * rescale[..., None] + jnp.einsum(
            "htn,nd->htd",
            weights.astype(jnp.bfloat16),
            value_rows,
            preferred_element_type=jnp.float32,
        )
        return (new_max, row_sum, running)

    def one_tile(tile_number, state_now):
        first = tile_number * tile_len
        key_rows = lax.dynamic_slice_in_dim(all_keys, first, tile_len, 0)
        value_rows = lax.dynamic_slice_in_dim(all_values, first, tile_len, 0)
        place_rows = lax.dynamic_slice_in_dim(all_places, first, tile_len, 0)
        return lax.cond(
            jnp.min(place_rows) <= reach_max,
            lambda state_in: process(state_in, key_rows, value_rows, place_rows),
            lambda state_in: state_in,
            state_now,
        )

    start_state = (
        jnp.full((heads_here, tok_rows), -1e30, jnp.float32),
        jnp.zeros((heads_here, tok_rows), jnp.float32),
        jnp.zeros((heads_here, tok_rows, HEAD_DIM), jnp.float32),
    )
    row_max, row_sum, running = lax.fori_loop(0, tile_count, one_tile, start_state)
    attended = (running / row_sum[..., None]).astype(jnp.bfloat16)
    attended = attended.transpose(1, 0, 2).reshape(tok_rows, head_cols)
    attention_rows = lax.psum_scatter(
        jnp.dot(attended, w_out, preferred_element_type=jnp.float32).astype(jnp.bfloat16),
        "exp",
        scatter_dimension=0,
        tiled=True,
    ).astype(jnp.float32)
    middle = (residual.astype(jnp.float32) + attention_rows).astype(jnp.bfloat16)
    wide = middle.astype(jnp.float32)
    mean_square = jnp.mean(wide * wide, axis=1, keepdims=True)
    normed = (wide * lax.rsqrt(mean_square + 1e-06) * norm_gain[None, :]).astype(jnp.bfloat16)
    local_rows = residual.shape[0]
    shares = gates / jnp.sum(gates, axis=1, keepdims=True)
    slice_expert = jnp.arange(exp_count, dtype=jnp.int32) // HID_SPLIT
    hits = routes[:, :, None] == slice_expert[None, None, :]
    coefficient = jnp.sum(jnp.where(hits, shares[:, :, None], 0.0), axis=1).astype(jnp.bfloat16)
    owner_weights = coefficient.transpose(1, 0)[:, :, None]
    copies = jnp.broadcast_to(normed[None, :, :], (exp_count, local_rows, D))
    row_block = lax.all_to_all(copies, "exp", split_axis=0, concat_axis=0, tiled=True)
    weight_block = lax.all_to_all(owner_weights, "exp", split_axis=0, concat_axis=0, tiled=True)
    slot_count = row_block.shape[1]
    produced = apply_slice(
        row_block.reshape(exp_count * slot_count, D),
        weight_block.reshape(exp_count * slot_count, 1),
        w_in,
        w_back,
    )
    produced = produced.reshape(exp_count, slot_count, D)
    arrived = lax.all_to_all(produced, "exp", split_axis=0, concat_axis=0, tiled=True)
    expert_out = jnp.sum(arrived.astype(jnp.float32), axis=0).astype(jnp.bfloat16)
    return (middle, expert_out)


def solution(mesh):
    in_specs = (
        P("ctx", "exp"),
        P("ctx", None),
        P("ctx", None),
        P("ctx"),
        P("ctx"),
        P("exp", None),
        P(("ctx", "exp"), None),
        P(),
        P(("ctx", "exp"), None),
        P(("ctx", "exp"), None),
        P("exp", None, None),
        P("exp", None, None),
    )
    out_specs = (P(("ctx", "exp"), None), P(("ctx", "exp"), None))
    one_line = mesh.shape["exp"] == HID_SPLIT and mesh.shape["ctx"] == 8
    return jax.shard_map(
        line_device if one_line else wide_device,
        mesh=mesh,
        in_specs=in_specs,
        out_specs=out_specs,
        check_vma=False,
    )
```

```python
import functools

import jax
import jax.numpy as jnp
from jax import lax
from jax.experimental import pallas as pl
from jax.experimental.pallas import tpu as pltpu
from jax.sharding import PartitionSpec as P

D = 4096
HEADS = 64
KV_HEADS = 4
HEAD_DIM = 128
HID_SPLIT = 4
STACK = 4
WIDTHS = (1024, 1024, 1024, 1024)
SPANS = tuple((sum(WIDTHS[:i]), width) for i, width in enumerate(WIDTHS))
PAD_ROWS = 16
BASE = 64
IN_FLIGHT = 2
EARLY = 2
LOG2E = 1.4426950408889634
VMEM = pl.BlockSpec(memory_space=pltpu.VMEM)
ANY = pl.BlockSpec(memory_space=pl.ANY)
LIGHT = pl.CostEstimate(flops=1024, bytes_accessed=1024, transcendentals=0)


def exchange(value, axis, offset, size):
    return lax.ppermute(value, axis, [(i, i ^ offset) for i in range(size)])


def start_weights(w_hbm, w_buf, sems, spans):
    copies = []
    for i, (first, width) in enumerate(spans):
        target = pl.ds(first - spans[0][0], width)
        copy = pltpu.make_async_copy(
            w_hbm.at[:, pl.ds(first, width)], w_buf.at[:, target], sems.at[i]
        )
        copy.start()
        copies.append(copy)
    return copies


def attend_kernel(rank_ref, limit_ref, same_ref, other_ref, q_ref, resid_ref, w_hbm, *refs):
    spans = SPANS[:EARLY]
    outs = refs[: 2 * EARLY]
    attended, w_buf, k_buf, v_buf, bias, acc, sems = refs[2 * EARLY :]
    tok = q_ref.shape[0]
    heads = q_ref.shape[1] // HEAD_DIM
    copies = start_weights(w_hbm, w_buf, sems, spans)
    extra = limit_ref[...].astype(jnp.float32)
    bound = extra[:1, :tok] * BASE + extra[:1, tok:]
    bound = jnp.broadcast_to(bound, (tok, tok)).T
    lane = lax.broadcasted_iota(jnp.int32, (1, tok), 1).astype(jnp.float32)
    ones = jnp.ones((tok, HEAD_DIM), jnp.bfloat16)
    block_rows = tok + PAD_ROWS
    half_count = same_ref.shape[0] // block_rows
    for b in range(2 * half_count):
        rows = slice(b * tok, (b + 1) * tok)
        group, row = (same_ref, b) if b < half_count else (other_ref, b - half_count)
        top = row * block_rows
        k_buf[rows, :] = group[top : top + tok, :HEAD_DIM]
        v_buf[rows, :HEAD_DIM] = group[top : top + tok, HEAD_DIM:]
        v_buf[rows, HEAD_DIM:] = ones
        start = group[top + tok : top + block_rows, :HEAD_DIM].astype(jnp.float32)[:1]
        place = start * tok + lane
        bias[:, rows] = jnp.where(place <= bound, 0.0, -1e30)
    factor = HEAD_DIM ** (-0.5) * LOG2E

    def some_heads(step, carry):
        base = step * STACK * HEAD_DIM
        parts = []
        for j in range(STACK):
            start = pl.multiple_of(base + j * HEAD_DIM, HEAD_DIM)
            parts.append(q_ref[:, pl.ds(start, HEAD_DIM)])
        stacked = jnp.concatenate(parts, axis=0)
        scores = lax.dot_general(
            stacked, k_buf[...], (((1,), (1,)), ((), ())), preferred_element_type=jnp.float32
        )
        scores = scores.reshape(STACK, tok, -1) * factor + bias[...][None]
        row_max = jnp.max(scores, axis=2, keepdims=True)
        weights = jnp.exp2(scores - row_max).astype(jnp.bfloat16)
        summed = jnp.dot(
            weights.reshape(STACK * tok, -1), v_buf[...], preferred_element_type=jnp.float32
        )
        result = (summed[:, :HEAD_DIM] / summed[:, HEAD_DIM:]).astype(jnp.bfloat16)
        for j in range(STACK):
            start = pl.multiple_of(base + j * HEAD_DIM, HEAD_DIM)
            attended[:, pl.ds(start, HEAD_DIM)] = result[j * tok : (j + 1) * tok]
        return carry

    lax.fori_loop(0, heads // STACK, some_heads, 0, unroll=True)
    project_spans(spans, copies, rank_ref[0], attended, w_buf, resid_ref, acc, outs)


def project_spans(spans, copies, rank, attended, w_buf, resid_ref, acc, outs):
    home = resid_ref.shape[0]
    side = rank % 2
    kept = [pl.multiple_of((side + 2 * i) * home, home) for i in range(2)]
    leaving = [pl.multiple_of((1 - side + 2 * i) * home, home) for i in range(2)]
    top = pl.multiple_of(rank * home, home)
    for chunk, (first, width) in enumerate(spans):
        copies[chunk].wait()
        span = slice(first - spans[0][0], first - spans[0][0] + width)
        acc[:, span] = jnp.dot(
            attended[...], w_buf[:, span], preferred_element_type=jnp.float32
        )
        acc[pl.ds(top, home), span] += resid_ref[:, first : first + width].astype(jnp.float32)
        for i in range(2):
            rows = slice(i * home, (i + 1) * home)
            outs[2 * chunk][rows, :] = acc[pl.ds(kept[i], home), span].astype(jnp.bfloat16)
            outs[2 * chunk + 1][rows, :] = acc[pl.ds(leaving[i], home), span].astype(
                jnp.bfloat16
            )


def part_shapes(tok, spans):
    return [
        jax.ShapeDtypeStruct((tok // 2, width), jnp.bfloat16) for _, width in spans for _ in range(2)
    ]


def attend_project(rank, limits, same, other, queries, residual, w_out):
    tok, width = queries.shape
    keys_in_all = 2 * same.shape[0] // (tok + PAD_ROWS) * tok
    spans = SPANS[:EARLY]
    columns = sum(w for _, w in spans)
    return pl.pallas_call(
        attend_kernel,
        out_shape=part_shapes(tok, spans) + [jax.ShapeDtypeStruct((tok, width), jnp.bfloat16)],
        in_specs=[pl.BlockSpec(memory_space=pltpu.SMEM)] + [VMEM] * 5 + [ANY],
        out_specs=[VMEM] * (2 * len(spans) + 1),
        scratch_shapes=[
            pltpu.VMEM((width, columns), jnp.bfloat16),
            pltpu.VMEM((keys_in_all, HEAD_DIM), jnp.bfloat16),
            pltpu.VMEM((keys_in_all, 2 * HEAD_DIM), jnp.bfloat16),
            pltpu.VMEM((tok, keys_in_all), jnp.float32),
            pltpu.VMEM((tok, columns), jnp.float32),
            pltpu.SemaphoreType.DMA((len(spans),)),
        ],
        compiler_params=pltpu.CompilerParams(vmem_limit_bytes=48 * 1024 * 1024),
        cost_estimate=pl.CostEstimate(
            flops=2 * tok * width * (2 * keys_in_all + columns),
            bytes_accessed=2 * width * columns,
            transcendentals=tok * width // HEAD_DIM * keys_in_all,
        ),
        name="attend_project",
    )(rank, limits, same, other, queries, residual, w_out)


def project_kernel(rank_ref, attended, resid_ref, w_hbm, *refs):
    spans = SPANS[EARLY:]
    outs = refs[: 2 * len(spans)]
    w_buf, acc, sems = refs[2 * len(spans) :]
    copies = start_weights(w_hbm, w_buf, sems, spans)
    project_spans(spans, copies, rank_ref[0], attended, w_buf, resid_ref, acc, outs)


def project(rank, attended, residual, w_out):
    tok, width = attended.shape
    spans = SPANS[EARLY:]
    columns = sum(w for _, w in spans)
    return pl.pallas_call(
        project_kernel,
        out_shape=part_shapes(tok, spans),
        in_specs=[pl.BlockSpec(memory_space=pltpu.SMEM)] + [VMEM] * 2 + [ANY],
        out_specs=[VMEM] * (2 * len(spans)),
        scratch_shapes=[
            pltpu.VMEM((width, columns), jnp.bfloat16),
            pltpu.VMEM((tok, columns), jnp.float32),
            pltpu.SemaphoreType.DMA((len(spans),)),
        ],
        compiler_params=pltpu.CompilerParams(vmem_limit_bytes=48 * 1024 * 1024),
        cost_estimate=pl.CostEstimate(
            flops=2 * tok * width * columns,
            bytes_accessed=2 * width * columns,
            transcendentals=0,
        ),
        name="project",
    )(rank, attended, residual, w_out)


def stage_kernel(q_hbm, resid_hbm, q_ref, resid_ref, sems):
    copies = [
        pltpu.make_async_copy(q_hbm, q_ref, sems.at[0]),
        pltpu.make_async_copy(resid_hbm, resid_ref, sems.at[1]),
    ]
    for copy in copies:
        copy.start()
    for copy in copies:
        copy.wait()


def stage(queries, residual):
    arrays = (queries, residual)
    return pl.pallas_call(
        stage_kernel,
        out_shape=[jax.ShapeDtypeStruct(array.shape, array.dtype) for array in arrays],
        in_specs=[ANY, ANY],
        out_specs=[VMEM, VMEM],
        scratch_shapes=[pltpu.SemaphoreType.DMA((2,))],
        compiler_params=pltpu.CompilerParams(vmem_limit_bytes=4 * 1024 * 1024),
        cost_estimate=LIGHT,
        name="stage",
    )(*arrays)


def join_kernel(*refs):
    out_ref = refs[-1]
    first = 0
    for piece in refs[1:-1]:
        rows = piece.shape[0]
        out_ref[first : first + rows, :] = piece[...]
        first += rows


def join_after(pieces, after):
    rows = sum(piece.shape[0] for piece in pieces)
    width = pieces[0].shape[1]
    return pl.pallas_call(
        join_kernel,
        out_shape=jax.ShapeDtypeStruct((rows, width), jnp.bfloat16),
        in_specs=[ANY] + [VMEM] * len(pieces),
        out_specs=VMEM,
        compiler_params=pltpu.CompilerParams(vmem_limit_bytes=8 * 1024 * 1024),
        cost_estimate=LIGHT,
        name="join_after",
    )(after, *pieces)


def absorb_kernel(chunk, rank_ref, mine_ref, theirs_ref, gain_ref, w_ref, *refs):
    last = chunk == len(WIDTHS) - 1
    state_count = 0 if chunk == 0 else 2
    states = refs[:state_count]
    home_ref = refs[state_count + int(last)]
    outs = refs[state_count + int(last) + 1 :]
    first, width = SPANS[chunk]
    span = slice(first, first + width)
    home = home_ref.shape[0]
    place = rank_ref[0] // 2
    home_ref[...] = mine_ref[pl.ds(pl.multiple_of(place * home, home), home), :]
    wide = jnp.concatenate([mine_ref[...], theirs_ref[...]], axis=0).astype(jnp.float32)
    gained = (wide * gain_ref[:, span]).astype(jnp.bfloat16)
    product = lax.dot_general(
        gained, w_ref[:, span], (((1,), (1,)), ((), ())), preferred_element_type=jnp.float32
    )
    square = sum(
        wide[:, i * 128 : (i + 1) * 128] * wide[:, i * 128 : (i + 1) * 128]
        for i in range(width // 128)
    )
    if chunk > 0:
        product += states[0][...]
        square += states[1][...]
    if not last:
        outs[0][...] = product
        outs[1][...] = square
        return
    back_ref = refs[state_count]
    shares, act_buf = outs[:-1], outs[-1]
    hidden = product.shape[1] // 2
    mean_square = jnp.sum(square, axis=1, keepdims=True) / D
    product = product * lax.rsqrt(mean_square + 1e-06)
    gate = product[:, :hidden]
    act_buf[...] = gate / (1.0 + jnp.exp(-gate)) * product[:, hidden:]
    ordered = []
    for offset in range(len(shares)):
        row = (offset % 2) * 2 * home + (place ^ (offset // 2)) * home
        ordered.append(act_buf[pl.ds(pl.multiple_of(row, home), home), :])
    ordered = jnp.concatenate(ordered, axis=0).astype(jnp.bfloat16)
    for part_first, part_width in SPANS:
        part = slice(part_first, part_first + part_width)
        result = jnp.dot(ordered, back_ref[:, part], preferred_element_type=jnp.float32)
        for i, share in enumerate(shares):
            share[:, part] = result[i * home : (i + 1) * home].astype(jnp.bfloat16)


def absorb(chunk, rank, mine, theirs, gain, w_in, states, back):
    half, width = mine.shape
    rows = w_in.shape[0]
    count = lax.axis_size("exp")
    home = 2 * half // count
    out_shape = [jax.ShapeDtypeStruct((home, width), jnp.bfloat16)]
    scratch = []
    operands = [rank, mine, theirs, gain, w_in, *states]
    if chunk == len(WIDTHS) - 1:
        operands.append(back)
        out_shape += [jax.ShapeDtypeStruct((home, D), jnp.bfloat16)] * count
        scratch = [pltpu.VMEM((2 * half, rows // 2), jnp.float32)]
    else:
        out_shape += [
            jax.ShapeDtypeStruct((2 * half, rows), jnp.float32),
            jax.ShapeDtypeStruct((2 * half, 128), jnp.float32),
        ]
    return pl.pallas_call(
        functools.partial(absorb_kernel, chunk),
        out_shape=out_shape,
        in_specs=[pl.BlockSpec(memory_space=pltpu.SMEM)] + [VMEM] * (len(operands) - 1),
        out_specs=[VMEM] * len(out_shape),
        scratch_shapes=scratch,
        compiler_params=pltpu.CompilerParams(vmem_limit_bytes=16 * 1024 * 1024),
        cost_estimate=LIGHT,
        name="absorb",
    )(*operands)


def own_heads(queries, keys, values):
    heads_here = queries.shape[1] // HEAD_DIM
    kv_number = lax.axis_index("exp") * heads_here // (HEADS // KV_HEADS)
    key_head = lax.dynamic_slice_in_dim(keys, kv_number * HEAD_DIM, HEAD_DIM, 1)
    value_head = lax.dynamic_slice_in_dim(values, kv_number * HEAD_DIM, HEAD_DIM, 1)
    return key_head, value_head


def line_device(
    queries,
    keys,
    values,
    positions,
    bounds,
    w_out,
    residual,
    norm_gain,
    routes,
    gates,
    w_in,
    w_back,
):
    tok = queries.shape[0]
    home = residual.shape[0]
    hidden = w_back.shape[1]
    ctx_count = lax.axis_size("ctx")
    exp_count = lax.axis_size("exp")
    rank = lax.axis_index("exp")
    key_head, value_head = own_heads(queries, keys, values)
    staged_queries, staged_residual = stage(queries, residual)
    block = (positions[0] // tok).astype(jnp.bfloat16)
    width = 2 * HEAD_DIM
    payload = jnp.concatenate(
        [
            jnp.concatenate([key_head, value_head], axis=1),
            jnp.full((PAD_ROWS, width), block, jnp.bfloat16),
        ],
        axis=0,
    )
    limits = jnp.concatenate([bounds // BASE, bounds % BASE]).astype(jnp.bfloat16)
    limits = jnp.broadcast_to(limits.reshape(1, width), (PAD_ROWS, width))
    same_keys = join_after(
        [payload] + [exchange(payload, "ctx", r, ctx_count) for r in range(2, ctx_count, 2)],
        payload,
    )
    other_keys = exchange(same_keys, "ctx", 1, ctx_count)

    ranks = rank.astype(jnp.int32).reshape(1)
    *parts, attended = attend_project(
        ranks, limits, same_keys, other_keys, staged_queries, staged_residual, w_out
    )
    parts += project(ranks, attended, staged_residual, w_out)
    shares = gates / jnp.sum(gates, axis=1, keepdims=True)
    coefficient = jnp.sum(jnp.where(routes == 0, shares, 0.0), axis=1, keepdims=True)
    coefficient = coefficient.astype(jnp.bfloat16).astype(jnp.float32)
    gain = norm_gain.reshape(1, D)
    flat_in = w_in.reshape(2 * hidden, D)
    flat_back = w_back.reshape(hidden, D)
    count = len(WIDTHS)

    def swap(values, offset):
        results = []
        for i, value in enumerate(values):
            if i >= IN_FLIGHT:
                value, _ = lax.optimization_barrier((value, results[i - IN_FLIGHT]))
            results.append(exchange(value, "exp", offset, exp_count))
        return results

    arrived = swap(parts[1::2], 1)
    near = [kept + other for kept, other in zip(parts[::2], arrived)]
    across = swap(near, 2)
    mine = [own + other for own, other in zip(near, across)]
    homes, states, theirs, done = [], [], [], [coefficient]
    for chunk in range(count):
        value = mine[chunk]
        if chunk >= IN_FLIGHT:
            own, *states = absorb(
                chunk - IN_FLIGHT,
                ranks,
                mine[chunk - IN_FLIGHT],
                theirs[chunk - IN_FLIGHT],
                gain,
                flat_in,
                states,
                flat_back,
            )
            homes.append(own)
            done = [states[0]]
        if chunk >= IN_FLIGHT or chunk == 1:
            value, *done = lax.optimization_barrier((value, *done))
            if chunk == 1:
                coefficient = done[0]
            else:
                states[0] = done[0]
        theirs.append(exchange(value, "exp", 1, exp_count))
    for chunk in range(count - IN_FLIGHT, count):
        own, *states = absorb(
            chunk, ranks, mine[chunk], theirs[chunk], gain, flat_in, states, flat_back
        )
        homes.append(own)
    middle_out = jnp.concatenate(homes, axis=1)
    expert = states[0].astype(jnp.float32)
    for offset in (2, 3, 1):
        expert = expert + exchange(states[offset], "exp", offset, exp_count).astype(jnp.float32)
    return (middle_out, (expert * coefficient).astype(jnp.bfloat16))


def largest_divisor(row_count):
    candidate = min(row_count, 1024)
    while row_count % candidate != 0:
        candidate = candidate - 1
    return candidate


def apply_slice(row_block, coefficient, w_in, w_back):
    hidden_here = w_back.shape[1]
    flat_in = w_in.reshape(2 * hidden_here, D)
    projected = lax.dot_general(
        row_block, flat_in, (((1,), (1,)), ((), ())), preferred_element_type=jnp.float32
    )
    activated = jax.nn.silu(projected[:, :hidden_here]) * projected[:, hidden_here:]
    blended = (coefficient.astype(jnp.float32) * activated).astype(jnp.bfloat16)
    flat_back = w_back.reshape(hidden_here, D)
    return jnp.dot(blended, flat_back, preferred_element_type=jnp.float32).astype(jnp.bfloat16)


def wide_device(
    queries,
    keys,
    values,
    positions,
    bounds,
    w_out,
    residual,
    norm_gain,
    routes,
    gates,
    w_in,
    w_back,
):
    tok_rows = queries.shape[0]
    head_cols = queries.shape[1]
    heads_here = head_cols // HEAD_DIM
    exp_count = lax.axis_size("exp")
    key_head, value_head = own_heads(queries, keys, values)
    query_heads = queries.reshape(tok_rows, heads_here, HEAD_DIM).transpose(1, 0, 2)
    scale = HEAD_DIM ** (-0.5)
    reach_max = jnp.max(bounds)
    all_keys, all_values, all_places = (
        lax.all_gather(key_head, "ctx", axis=0, tiled=True),
        lax.all_gather(value_head, "ctx", axis=0, tiled=True),
        lax.all_gather(positions, "ctx", axis=0, tiled=True),
    )
    total_rows = all_keys.shape[0]
    tile_len = largest_divisor(total_rows)
    tile_count = total_rows // tile_len

    def process(state_in, key_rows, value_rows, place_rows):
        row_max, row_sum, running = state_in
        scores = (
            jnp.einsum("htd,nd->htn", query_heads, key_rows, preferred_element_type=jnp.float32)
            * scale
        )
        visible = (place_rows[None, :] <= bounds[:, None])[None, :, :]
        masked = jnp.where(visible, scores, -1e30)
        new_max = jnp.maximum(row_max, jnp.max(masked, axis=2))
        weights = jnp.exp(masked - new_max[..., None])
        rescale = jnp.exp(row_max - new_max)
        row_sum = row_sum * rescale + jnp.sum(weights, axis=2)
        running = running * rescale[..., None] + jnp.einsum(
            "htn,nd->htd",
            weights.astype(jnp.bfloat16),
            value_rows,
            preferred_element_type=jnp.float32,
        )
        return (new_max, row_sum, running)

    def one_tile(tile_number, state_now):
        first = tile_number * tile_len
        key_rows = lax.dynamic_slice_in_dim(all_keys, first, tile_len, 0)
        value_rows = lax.dynamic_slice_in_dim(all_values, first, tile_len, 0)
        place_rows = lax.dynamic_slice_in_dim(all_places, first, tile_len, 0)
        return lax.cond(
            jnp.min(place_rows) <= reach_max,
            lambda state_in: process(state_in, key_rows, value_rows, place_rows),
            lambda state_in: state_in,
            state_now,
        )

    start_state = (
        jnp.full((heads_here, tok_rows), -1e30, jnp.float32),
        jnp.zeros((heads_here, tok_rows), jnp.float32),
        jnp.zeros((heads_here, tok_rows, HEAD_DIM), jnp.float32),
    )
    row_max, row_sum, running = lax.fori_loop(0, tile_count, one_tile, start_state)
    attended = (running / row_sum[..., None]).astype(jnp.bfloat16)
    attended = attended.transpose(1, 0, 2).reshape(tok_rows, head_cols)
    attention_rows = lax.psum_scatter(
        jnp.dot(attended, w_out, preferred_element_type=jnp.float32).astype(jnp.bfloat16),
        "exp",
        scatter_dimension=0,
        tiled=True,
    ).astype(jnp.float32)
    middle = (residual.astype(jnp.float32) + attention_rows).astype(jnp.bfloat16)
    wide = middle.astype(jnp.float32)
    mean_square = jnp.mean(wide * wide, axis=1, keepdims=True)
    normed = (wide * lax.rsqrt(mean_square + 1e-06) * norm_gain[None, :]).astype(jnp.bfloat16)
    local_rows = residual.shape[0]
    shares = gates / jnp.sum(gates, axis=1, keepdims=True)
    slice_expert = jnp.arange(exp_count, dtype=jnp.int32) // HID_SPLIT
    hits = routes[:, :, None] == slice_expert[None, None, :]
    coefficient = jnp.sum(jnp.where(hits, shares[:, :, None], 0.0), axis=1).astype(jnp.bfloat16)
    owner_weights = coefficient.transpose(1, 0)[:, :, None]
    copies = jnp.broadcast_to(normed[None, :, :], (exp_count, local_rows, D))
    row_block = lax.all_to_all(copies, "exp", split_axis=0, concat_axis=0, tiled=True)
    weight_block = lax.all_to_all(owner_weights, "exp", split_axis=0, concat_axis=0, tiled=True)
    slot_count = row_block.shape[1]
    produced = apply_slice(
        row_block.reshape(exp_count * slot_count, D),
        weight_block.reshape(exp_count * slot_count, 1),
        w_in,
        w_back,
    )
    produced = produced.reshape(exp_count, slot_count, D)
    arrived = lax.all_to_all(produced, "exp", split_axis=0, concat_axis=0, tiled=True)
    expert_out = jnp.sum(arrived.astype(jnp.float32), axis=0).astype(jnp.bfloat16)
    return (middle, expert_out)


def solution(mesh):
    in_specs = (
        P("ctx", "exp"),
        P("ctx", None),
        P("ctx", None),
        P("ctx"),
        P("ctx"),
        P("exp", None),
        P(("ctx", "exp"), None),
        P(),
        P(("ctx", "exp"), None),
        P(("ctx", "exp"), None),
        P("exp", None, None),
        P("exp", None, None),
    )
    out_specs = (P(("ctx", "exp"), None), P(("ctx", "exp"), None))
    one_line = mesh.shape["exp"] == HID_SPLIT and mesh.shape["ctx"] == 8
    return jax.shard_map(
        line_device if one_line else wide_device,
        mesh=mesh,
        in_specs=in_specs,
        out_specs=out_specs,
        check_vma=False,
    )
```
